32 devices in a mesh: groups: 2 (over y), src: 4 (over z), dst: 4 (over x, core).
Axes of the slice: x: 2, y: 2, z: 4, core: 2. Of those that a mesh axis runs over, the one named last changes fastest.
Arguments:
- node_state: bfloat16 [2, 1024, 128], P(None, ('groups', 'src', 'dst')), parts along dimension 1, may hold values from -6 to 6
- forcing: bfloat16 [2, 1024, 128], P(None, ('groups', 'src', 'dst')), parts along dimension 1, may hold values from -6 to 6
- edge_attr: bfloat16 [2, 8, 4, 512, 128], P(None, ('groups', 'src'), 'dst'), parts along dimension 1, may hold values from -6 to 6
- src_index: int32 [8, 4, 512], P(('groups', 'src'), 'dst'), parts along dimension 0, may hold values from 0 to 127
- dst_index: int32 [8, 4, 512], P(('groups', 'src'), 'dst'), parts along dimension 0, may hold values from 0 to 127
- edge_count: int32 [8, 4], P(('groups', 'src'), 'dst'), parts along dimension 0, may hold values from 128 to 512, as said below
- cotangent: bfloat16 [2, 1024, 256], P(None, ('groups', 'src', 'dst')), parts along dimension 1, may hold values from -6 to 6
- edge_w1: bfloat16 [384, 512], replicated, may hold values from -0.3125 to 0.3125
- edge_w2: bfloat16 [512, 256], replicated, may hold values from -0.25 to 0.25
- node_w1: bfloat16 [512, 256], replicated, may hold values from -0.25 to 0.25
Outputs:
- grad_state: float32 [2, 1024, 128], P(None, ('groups', 'src', 'dst')), parts along dimension 1
- grad_forcing: float32 [2, 1024, 128], P(None, ('groups', 'src', 'dst')), parts along dimension 1
- grad_edges: float32 [2, 8, 4, 512, 128], P(None, ('groups', 'src'), 'dst'), parts along dimension 1
- grad_edge_w1: float32 [768, 512], P('groups'), parts along dimension 0
- grad_edge_w2: float32 [1024, 256], P('groups'), parts along dimension 0
- grad_node_w1: float32 [1024, 256], P('groups'), parts along dimension 0
The draws below stay inside these ranges and needn't reach their ends.
There are 2 independent parts, one for each index of `groups`. The reference program is written for one: setup_inputs(seed, part) draws one part's arguments, and reference() takes and returns one part's arrays. A program takes and returns all parts, laid end to end along the dimension named above; an argument that names none is the same for every part. Nothing has to cross between parts.
Inputs may be any that keep to these rules, and one draw needn't show every extreme that they name: The live slots of a tile are its first edge_count ones; every draw has a tile with all 512 slots live.
All inputs are finite; a program needn't handle non-finite values.
Results may differ from the reference program's by a relative error of at most 0.006.
Values may be sent and summed in bfloat16 or wider, within the bound.
No kernel may reach another device: no remote copies, remote signals or barrier semaphores. Data moves between devices by JAX's collectives and lax.ppermute only.
A program may use at most 64 MiB of HBM per device.

```python
import jax
import jax.numpy as jnp
from jax import lax

DX = 128
DE = 128
DF = 128
HID = 512
DM = 256
DOUT = 256
EIN = 384
NIN = 512
NODE_DEV = 32
ECAP = 512
T_STEPS = 2
GRID_ROWS = 4
GRID_COLS = 4
SRC_BLOCK = 128
DST_BLOCK = 128
NODES = 512


def draw_edge_count(key, part):
    key = jax.random.fold_in(key, 7)
    first_key, second_key = jax.random.split(key)
    divisor = jax.random.randint(first_key, (GRID_ROWS, GRID_COLS), 1, 5)
    counts = (ECAP // divisor).reshape(-1)
    place = jax.random.randint(second_key, (), 0, GRID_ROWS * GRID_COLS)
    counts = counts.at[place].set(ECAP)
    return counts.reshape(GRID_ROWS, GRID_COLS).astype(jnp.int32)


def place_ends(values, rng, smallest, high):
    longest = values.shape.index(max(values.shape))
    spots = []
    for shift in (0, 1):
        where = [jax.random.randint(jax.random.fold_in(rng, axis), (), 0, length) for axis, length in enumerate(values.shape)]
        where[longest] = (where[longest] + shift) % values.shape[longest]
        spots.append(tuple(where))
    return values.at[spots[0]].set(smallest).at[spots[1]].set(high)


def block_levels(rng, shape, cuts, low, high):
    gain, own = 1.0, jax.random.fold_in(rng, 6)
    for axis_at, blocks in cuts:
        draws = jnp.exp(jax.random.uniform(jax.random.fold_in(own, axis_at), (blocks,), jnp.float32, low / len(cuts), high / len(cuts)))
        gain = gain * jnp.repeat(draws, shape[axis_at] // blocks).reshape([-1 if axis == axis_at else 1 for axis in range(len(shape))])
    return gain


def scatter_about(own_key, extent, deviation, most, cuts=(), held_as=jnp.bfloat16):
    entries = deviation * jax.random.normal(own_key, extent, jnp.float32)
    if cuts:
        entries = entries * block_levels(own_key, extent, cuts, -0.22, 0.18)
    return jnp.clip(entries, -most, most).astype(held_as)


def setup_inputs(seed: int = 0, part: int = 0) -> dict:
    arg_keys = jax.random.split(jax.random.key(seed), 11)
    own_keys = jax.random.split(jax.random.fold_in(arg_keys[10], part), 11)
    node_state = scatter_about(own_keys[0], (T_STEPS, NODES, DX), 1.0, 6.0, ((1, 16),))
    forcing = scatter_about(own_keys[1], (T_STEPS, NODES, DF), 1.0, 6.0, ((1, 16),))
    edge_attr = scatter_about(own_keys[2], (T_STEPS, GRID_ROWS, GRID_COLS, ECAP, DE), 1.0, 6.0, ((1, 4), (2, 4)))
    src_index = place_ends(jax.random.randint(own_keys[3], (GRID_ROWS, GRID_COLS, ECAP), 0, SRC_BLOCK), jax.random.fold_in(own_keys[3], 1), 0, SRC_BLOCK - 1).astype(jnp.int32)
    dst_index = place_ends(jax.random.randint(own_keys[4], (GRID_ROWS, GRID_COLS, ECAP), 0, DST_BLOCK), jax.random.fold_in(own_keys[4], 1), 0, DST_BLOCK - 1).astype(jnp.int32)
    edge_count = draw_edge_count(jax.random.fold_in(jax.random.fold_in(arg_keys[10], part), 71), part)
    cotangent = scatter_about(own_keys[6], (T_STEPS, NODES, DOUT), 1.0, 6.0, ((1, 16),))
    edge_w1 = scatter_about(arg_keys[7], (EIN, HID), EIN ** -0.5, 0.3125)
    edge_w2 = scatter_about(arg_keys[8], (HID, DM), HID ** -0.5, 0.25)
    node_w1 = scatter_about(arg_keys[9], (NIN, DOUT), NIN ** -0.5, 0.25)
    return {"node_state": node_state, "forcing": forcing, "edge_attr": edge_attr, "src_index": src_index, "dst_index": dst_index, "edge_count": edge_count, "cotangent": cotangent, "edge_w1": edge_w1, "edge_w2": edge_w2, "node_w1": node_w1}


def silu_slope(value):
    sigma = jax.nn.sigmoid(value)
    return sigma * (1.0 + value * (1.0 - sigma))


def reference(node_state, forcing, edge_attr, src_index, dst_index, edge_count, cotangent, edge_w1, edge_w2, node_w1):
    tiles = GRID_ROWS * GRID_COLS
    row_ids = lax.broadcasted_iota(jnp.int32, (GRID_ROWS, GRID_COLS, ECAP), 0)
    col_ids = lax.broadcasted_iota(jnp.int32, (GRID_ROWS, GRID_COLS, ECAP), 1)
    slot_ids = lax.broadcasted_iota(jnp.int32, (GRID_ROWS, GRID_COLS, ECAP), 2)
    src_glob = (row_ids * SRC_BLOCK + src_index).reshape(tiles, ECAP).astype(jnp.int32)
    dst_glob = (((dst_index // NODE_DEV) * GRID_COLS + col_ids) * NODE_DEV + dst_index % NODE_DEV).reshape(tiles, ECAP).astype(jnp.int32)
    live_mask = (slot_ids < edge_count[:, :, None]).reshape(tiles, ECAP)
    grad_first = jnp.zeros((EIN, HID), jnp.float32)
    grad_second = jnp.zeros((HID, DM), jnp.float32)
    grad_node = jnp.zeros((NIN, DOUT), jnp.float32)
    state_out, forcing_out, edge_out = [], [], []
    for moment in range(T_STEPS):
        state_now = node_state[moment]
        attr_now = edge_attr[moment].reshape(tiles, ECAP, DE)

        def edge_input(src_ids, dst_ids, attrs):
            return jnp.concatenate([state_now[src_ids], state_now[dst_ids], attrs], axis=1)

        def forward_tile(agg_sum, item):
            src_ids, dst_ids, alive, attrs = item
            edge_in = edge_input(src_ids, dst_ids, attrs)
            pre_edge = jnp.dot(edge_in, edge_w1, preferred_element_type=jnp.float32)
            hidden = jax.nn.silu(pre_edge).astype(jnp.bfloat16)
            message = jnp.dot(hidden, edge_w2, preferred_element_type=jnp.float32) * alive.astype(jnp.float32)[:, None]
            return agg_sum + jax.ops.segment_sum(message, dst_ids, num_segments=NODES), None

        agg_sum, _ = lax.scan(forward_tile, jnp.zeros((NODES, DM), jnp.float32), (src_glob, dst_glob, live_mask, attr_now))
        node_in = jnp.concatenate([state_now, agg_sum.astype(jnp.bfloat16), forcing[moment]], axis=1)
        pre_node = jnp.dot(node_in, node_w1, preferred_element_type=jnp.float32)
        grad_pre_node = (cotangent[moment].astype(jnp.float32) * silu_slope(pre_node)).astype(jnp.bfloat16)
        grad_node = grad_node + jnp.dot(node_in.T, grad_pre_node, preferred_element_type=jnp.float32)
        grad_node_in = jnp.dot(grad_pre_node, node_w1.T, preferred_element_type=jnp.float32)
        grad_agg = grad_node_in[:, DX:DX + DM].astype(jnp.bfloat16)

        def backward_tile(carry, item):
            grad_nodes, grad_one, grad_two = carry
            src_ids, dst_ids, alive, attrs = item
            edge_in = edge_input(src_ids, dst_ids, attrs)
            pre_edge = jnp.dot(edge_in, edge_w1, preferred_element_type=jnp.float32)
            hidden = jax.nn.silu(pre_edge).astype(jnp.bfloat16)
            grad_message = grad_agg[dst_ids] * alive.astype(jnp.bfloat16)[:, None]
            grad_two = grad_two + jnp.dot(hidden.T, grad_message, preferred_element_type=jnp.float32)
            grad_hidden = jnp.dot(grad_message, edge_w2.T, preferred_element_type=jnp.float32)
            grad_pre_edge = (grad_hidden * silu_slope(pre_edge)).astype(jnp.bfloat16)
            grad_one = grad_one + jnp.dot(edge_in.T, grad_pre_edge, preferred_element_type=jnp.float32)
            grad_edge_in = jnp.dot(grad_pre_edge, edge_w1.T, preferred_element_type=jnp.float32)
            grad_nodes = grad_nodes + jax.ops.segment_sum(grad_edge_in[:, :DX], src_ids, num_segments=NODES)
            grad_nodes = grad_nodes + jax.ops.segment_sum(grad_edge_in[:, DX:2 * DX], dst_ids, num_segments=NODES)
            return (grad_nodes, grad_one, grad_two), grad_edge_in[:, 2 * DX:]

        carry, grad_attr = lax.scan(backward_tile, (grad_node_in[:, :DX], grad_first, grad_second), (src_glob, dst_glob, live_mask, attr_now))
        grad_nodes, grad_first, grad_second = carry
        state_out.append(grad_nodes)
        forcing_out.append(grad_node_in[:, DX + DM:])
        edge_out.append(grad_attr.reshape(GRID_ROWS, GRID_COLS, ECAP, DE))
    return (jnp.stack(state_out), jnp.stack(forcing_out), jnp.stack(edge_out), grad_first, grad_second, grad_node)
```

```python
import functools

import jax
import jax.numpy as jnp
from jax import lax
from jax.experimental import pallas as pl
from jax.experimental.pallas import tpu as pltpu
from jax.sharding import PartitionSpec as P

T_STEPS = 2
WAYS = 4
LANES = 128
BF = jnp.bfloat16
F32 = jnp.float32


def sigmoid(value):
    return 0.5 * jnp.tanh(0.5 * value) + 0.5


def slope_of(value):
    sigma = sigmoid(value)
    return sigma * (1.0 + value * (1.0 - sigma))


def mm(a, b):
    return jnp.dot(a, b, preferred_element_type=F32)


def mm_nt(a, b):
    return lax.dot_general(a, b, (((1,), (1,)), ((), ())), preferred_element_type=F32)


def mm_tn(a, b):
    return lax.dot_general(a, b, (((0,), (0,)), ((), ())), preferred_element_type=F32)


def one_hot_t(index, nodes, live=None):
    hit = lax.broadcasted_iota(jnp.int32, (nodes, index.shape[1]), 0) == index
    if live is not None:
        hit = jnp.logical_and(hit, live)
    return jnp.where(hit, 1.0, 0.0).astype(BF)


def stacked(refs, moment):
    return jnp.concatenate([ref[moment] for ref in refs], axis=0)


def summed(refs, moment):
    rows = refs[0].shape[1] // WAYS
    return jnp.concatenate(
        [
            sum(ref[moment, (j ^ k) * rows : ((j ^ k) + 1) * rows].astype(F32) for k, ref in enumerate(refs))
            for j in range(WAYS)
        ],
        axis=0,
    )


def selectors(place, src_index, dst_index, rows):
    nodes = rows * WAYS
    slots = src_index.shape[1]
    live = lax.broadcasted_iota(jnp.int32, (1, slots), 1) < place[2]
    src_t = one_hot_t(src_index[...] ^ (place[1] * rows), nodes)
    dst_t = one_hot_t(dst_index[...] ^ (place[0] * rows), nodes, live)
    dst_all = one_hot_t(dst_index[...] ^ (place[0] * rows), nodes)
    return src_t, dst_t, dst_all


def forward_kernel(place, *refs):
    sources, targets = refs[:WAYS], refs[WAYS : 2 * WAYS]
    attr, src_index, dst_index, w1, w2 = refs[2 * WAYS : 2 * WAYS + 5]
    message, slope, *pieces, held = refs[2 * WAYS + 5 :]
    rows, width = sources[0].shape[1], sources[0].shape[2]
    src_t, dst_t, dst_all = selectors(place, src_index, dst_index, rows)
    for moment in range(T_STEPS):
        edge_in = jnp.concatenate(
            [
                mm_tn(src_t, stacked(sources, moment)).astype(BF),
                mm_tn(dst_all, stacked(targets, moment)[:, :width]).astype(BF),
                attr[moment],
            ],
            axis=1,
        )
        pre = mm(edge_in, w1[...])
        sigma = sigmoid(pre)
        hidden = (pre * sigma).astype(BF)
        slope[moment] = sigma * (1.0 + pre * (1.0 - sigma))
        sums = mm(dst_t, hidden).astype(BF)
        held[moment] = sums
        message[moment] = mm(sums, w2[...]).astype(BF)
    block = w1.shape[1] // WAYS
    for k in range(WAYS):
        start = pl.multiple_of((place[0] ^ k) * block, block)
        pieces[k][...] = held[:, :, pl.ds(start, block)]


def backward_kernel(place, *refs):
    n = WAYS
    sources, targets, messages, pieces = refs[:n], refs[n : 2 * n], refs[2 * n : 3 * n], refs[3 * n : 4 * n]
    attr, src_index, dst_index, slope, w1, w2, wn = refs[4 * n : 4 * n + 7]
    outs = refs[4 * n + 7 :]
    state_own, forcing_own, edges = outs[:3]
    over_dst, over_src = outs[3 : 3 + n], outs[3 + n : 3 + 2 * n]
    node_held, pre_held, agg_held, gpe_held, p_held, q_held, first = outs[3 + 2 * n :]
    rows, width = sources[0].shape[1], sources[0].shape[2]
    nodes = rows * n
    slots = attr.shape[1]
    width_m = w2.shape[1]
    src_t, dst_t, _ = selectors(place, src_index, dst_index, rows)
    for moment in range(T_STEPS):
        at = slice(moment * nodes, (moment + 1) * nodes)
        block = stacked(targets, moment)
        state, forcing, cotangent = block[:, :width], block[:, width : 2 * width], block[:, 2 * width :]
        agg = summed(messages, moment)
        node_in = jnp.concatenate([state, agg.astype(BF), forcing], axis=1)
        pre_node = mm(node_in, wn[...])
        grad_pre = (cotangent.astype(F32) * slope_of(pre_node)).astype(BF)
        node_held[at] = node_in
        pre_held[at] = grad_pre
        grad_in = mm_nt(grad_pre, wn[...])
        state_own[moment] = grad_in[:rows, :width]
        forcing_own[moment] = grad_in[:rows, width + width_m :]
        grad_agg = grad_in[:, width : width + width_m].astype(BF)
        agg_held[at] = grad_agg
        grad_message = mm_tn(dst_t, grad_agg).astype(BF)
        grad_pre_edge = (mm_nt(grad_message, w2[...]) * slope[moment]).astype(BF)
        gpe_held[moment * slots : (moment + 1) * slots] = grad_pre_edge
        edges[moment] = mm_nt(grad_pre_edge, w1[2 * width :])
        from_src = mm(src_t, grad_pre_edge).astype(BF)
        from_dst = mm(dst_t, grad_pre_edge).astype(BF)
        p_held[at] = from_src
        q_held[at] = from_dst
        to_src = mm_nt(from_src, w1[:width]).astype(BF)
        to_dst = mm_nt(from_dst, w1[width : 2 * width]).astype(BF)
        half = rows // 2
        for k in range(n):
            for j in range(2):
                lanes = slice((moment * 2 + j) * width, (moment * 2 + j + 1) * width)
                spot = slice(k * rows + j * half, k * rows + (j + 1) * half)
                over_dst[k][-half:, lanes] = to_src[spot]
                over_src[k][:, lanes] = to_dst[spot]
    states = jnp.concatenate([stacked(sources, moment) for moment in range(T_STEPS)], axis=0)
    first[:width] = mm_tn(states, p_held[...])
    first[width : 2 * width] = mm_tn(node_held[:, :width], q_held[...])
    first[2 * width :] = mm_tn(attr[...].reshape(T_STEPS * slots, width), gpe_held[...])
    block = wn.shape[0] // n
    spot = pl.multiple_of(place[0] * block, block)
    node_grad = mm_tn(node_held[:, pl.ds(spot, block)], pre_held[...])
    sums = jnp.concatenate([summed(pieces, moment) for moment in range(T_STEPS)], axis=0).astype(BF)
    second = mm_tn(sums, agg_held[...])
    both = jnp.concatenate([second, node_grad], axis=1)
    part = first.shape[0] // n
    small = block // n

    for k in range(n):
        other = place[1] ^ k
        over_dst[k][:part] = first[pl.ds(pl.multiple_of(other * part, part), part)].astype(BF)
    for j in range(n):
        for k in range(n):
            @pl.when((place[1] ^ k) == j)
            def _(j=j, k=k):
                over_dst[k][part : part + small] = both[j * small : (j + 1) * small].astype(BF)


def middle_kernel(state_own, *refs):
    n = WAYS
    parts, pieces = refs[:n], refs[n : 2 * n]
    state_sum, own, *sent = refs[2 * n :]
    total = sum(ref[...].astype(F32) for ref in parts)
    half = pieces[0].shape[0]
    width = state_own.shape[2]
    core = total[:-half]
    own[...] = core
    rounded = core.astype(BF)
    nodes = total[-half:] + pieces[0][...].astype(F32)
    for moment in range(T_STEPS):
        for j in range(2):
            lanes = slice((moment * 2 + j) * width, (moment * 2 + j + 1) * width)
            spot = slice(j * half, (j + 1) * half)
            state_sum[moment, spot] = state_own[moment, spot] + nodes[:, lanes]
    for k in range(1, n):
        sent[k - 1][:-half] = rounded
        sent[k - 1][-half:] = pieces[k][...]


def gather_kernel(place, state_sum, own, *refs):
    n = WAYS
    arrived = refs[: n - 1]
    state, sent = refs[n - 1 :]
    width = state_sum.shape[2]
    half = state_sum.shape[1] // 2
    wide = own.shape[0]
    small = (sent.shape[0] - wide) // (n - 1)
    part = wide - small
    nodes = sum(ref[wide:].astype(F32) for ref in arrived)
    for moment in range(T_STEPS):
        for j in range(2):
            lanes = slice((moment * 2 + j) * width, (moment * 2 + j + 1) * width)
            spot = slice(j * half, (j + 1) * half)
            state[moment, spot] = state_sum[moment, spot] + nodes[:, lanes]
    first = own[:part] + sum(ref[:part].astype(F32) for ref in arrived)
    sent[:part] = first.astype(BF)
    for k in range(n):
        start = pl.multiple_of(part + (place[0] ^ k) * small, small)
        sent[pl.ds(start, small)] = own[part:].astype(BF) if k == 0 else arrived[k - 1][part:wide]


def final_kernel(place, *refs):
    n = WAYS
    arrived = refs[:n]
    first, second, node = refs[n:]
    part = first.shape[0] // n
    small = second.shape[0] // n // n
    half = second.shape[1]
    for k in range(n):
        other = place[1] ^ k
        first[pl.ds(pl.multiple_of(other * part, part), part)] = arrived[k][:part].astype(F32)
        for j in range(n):
            rows = arrived[k][part + j * small : part + (j + 1) * small].astype(F32)
            start = pl.multiple_of((j * n + other) * small, small)
            second[pl.ds(start, small)] = rows[:, :half]
            node[pl.ds(start, small)] = rows[:, half:]


def call(kernel, outs, scratch, args, scalars=True):
    in_specs = [pl.BlockSpec(memory_space=pltpu.SMEM)] if scalars else []
    in_specs += [pl.BlockSpec(memory_space=pltpu.VMEM)] * (len(args) - len(in_specs))
    return pl.pallas_call(
        kernel,
        out_shape=[jax.ShapeDtypeStruct(shape, dtype) for shape, dtype in outs],
        in_specs=in_specs,
        out_specs=[pl.BlockSpec(memory_space=pltpu.VMEM)] * len(outs),
        scratch_shapes=[pltpu.VMEM(shape, dtype) for shape, dtype in scratch],
        compiler_params=pltpu.CompilerParams(vmem_limit_bytes=48 << 20),
    )(*args)


def swap(value, axis, k):
    return lax.ppermute(value, axis, [(i, i ^ k) for i in range(WAYS)])


def fan(value, axis):
    return [value] + [swap(value, axis, k) for k in range(1, WAYS)]


def exchange(values, axis):
    return [values[0]] + [swap(values[k], axis, k) for k in range(1, WAYS)]


def local(
    node_state,
    forcing,
    edge_attr,
    src_index,
    dst_index,
    edge_count,
    cotangent,
    edge_w1,
    edge_w2,
    node_w1,
):
    rows, width = node_state.shape[1:]
    hid, width_m = edge_w2.shape
    width_in, width_out = node_w1.shape
    slots = edge_attr.shape[3]
    nodes = rows * WAYS
    steps = T_STEPS
    place = jnp.stack(
        [lax.axis_index("src"), lax.axis_index("dst"), edge_count[0, 0]]
    ).astype(jnp.int32)
    attr = edge_attr[:, 0, 0]
    src_row, dst_row = src_index[0], dst_index[0]
    sources = fan(node_state, "dst")
    targets = fan(jnp.concatenate([node_state, forcing, cotangent], axis=2), "src")
    block = hid // WAYS
    message, slope, *pieces = call(
        forward_kernel,
        [((steps, nodes, width_m), BF), ((steps, slots, hid), F32)]
        + [((steps, nodes, block), BF)] * WAYS,
        [((steps, nodes, hid), BF)],
        [place, *sources, *targets, attr, src_row, dst_row, edge_w1, edge_w2],
    )
    messages = fan(message, "src")
    pieces = exchange(pieces, "src")
    part = edge_w1.shape[0] // WAYS
    small = block // WAYS
    half = rows // 2
    wide = part + small
    state_own, grad_forcing, edges, *sent = call(
        backward_kernel,
        [((steps, rows, width), F32), ((steps, rows, width), F32), ((steps, slots, width), F32)]
        + [((wide + half, hid), BF)] * WAYS
        + [((half, hid), BF)] * WAYS,
        [
            ((steps * nodes, width_in), BF),
            ((steps * nodes, width_out), BF),
            ((steps * nodes, width_m), BF),
            ((steps * slots, hid), BF),
            ((steps * nodes, hid), BF),
            ((steps * nodes, hid), BF),
            (edge_w1.shape, F32),
        ],
        [place, *sources, *targets, *messages, *pieces, attr, src_row, dst_row, slope, edge_w1, edge_w2, node_w1],
    )
    over_dst, over_src = sent[:WAYS], sent[WAYS:]
    state_sum, own, *sent = call(
        middle_kernel,
        [((steps, rows, width), F32), ((wide, hid), F32)] + [((wide + half, hid), BF)] * (WAYS - 1),
        [],
        [state_own, *exchange(over_dst, "dst"), *over_src],
        scalars=False,
    )
    arrived = [swap(sent[k - 1], "src", k) for k in range(1, WAYS)]
    grad_state, share = call(
        gather_kernel,
        [((steps, rows, width), F32), ((wide + (WAYS - 1) * small, hid), BF)],
        [],
        [place, state_sum, own, *arrived],
    )
    across = swap(share, "dst", 2)
    grad_first, grad_second, grad_node = call(
        final_kernel,
        [(edge_w1.shape, F32), (edge_w2.shape, F32), (node_w1.shape, F32)],
        [],
        [place, share, swap(share, "dst", 1), across, swap(across, "dst", 1)],
    )
    return grad_state, grad_forcing, edges[:, None, None], grad_first, grad_second, grad_node


def silu_slope(value):
    sigma = jax.nn.sigmoid(value)
    return sigma * (1.0 + value * (1.0 - sigma))


def local_any(
    node_state,
    forcing,
    edge_attr,
    src_index,
    dst_index,
    edge_count,
    cotangent,
    edge_w1,
    edge_w2,
    node_w1,
):
    node_rows = node_state.shape[1]
    width_x = node_state.shape[2]
    width_m = edge_w2.shape[1]
    src_rows = node_rows * lax.axis_size("dst")
    dst_rows = node_rows * lax.axis_size("src")
    sources = lax.all_gather(node_state, "dst", axis=1, tiled=True)
    targets, forcing_block, cotangent_block = (
        lax.all_gather(node_state, "src", axis=1, tiled=True),
        lax.all_gather(forcing, "src", axis=1, tiled=True),
        lax.all_gather(cotangent, "src", axis=1, tiled=True),
    )
    src_local = src_index[0, 0]
    dst_local = dst_index[0, 0]
    alive = lax.iota(jnp.int32, src_local.shape[0]) < edge_count[0, 0]
    alive_float = alive.astype(jnp.float32)[:, None]
    alive_half = alive.astype(jnp.bfloat16)[:, None]
    own_start = lax.axis_index("src") * node_rows
    grad_first = jnp.zeros(edge_w1.shape, jnp.float32)
    grad_second = jnp.zeros(edge_w2.shape, jnp.float32)
    grad_node = jnp.zeros(node_w1.shape, jnp.float32)
    state_out, forcing_out, edge_out = ([], [], [])
    for moment in range(T_STEPS):
        edge_in = jnp.concatenate(
            [sources[moment][src_local], targets[moment][dst_local], edge_attr[moment, 0, 0]],
            axis=1,
        )
        pre_edge = jnp.dot(edge_in, edge_w1, preferred_element_type=jnp.float32)
        hidden = jax.nn.silu(pre_edge).astype(jnp.bfloat16)
        message = jnp.dot(hidden, edge_w2, preferred_element_type=jnp.float32) * alive_float
        partial_value = jax.ops.segment_sum(message, dst_local, num_segments=dst_rows)
        agg_block = lax.psum(partial_value, "src")
        node_in = jnp.concatenate(
            [targets[moment], agg_block.astype(jnp.bfloat16), forcing_block[moment]], axis=1
        )
        pre_node = jnp.dot(node_in, node_w1, preferred_element_type=jnp.float32)
        grad_pre_node = (cotangent_block[moment].astype(jnp.float32) * silu_slope(pre_node)).astype(
            jnp.bfloat16
        )
        grad_node_in = jnp.dot(grad_pre_node, node_w1.T, preferred_element_type=jnp.float32)
        own_in = lax.dynamic_slice_in_dim(node_in, own_start, node_rows, 0)
        own_pre = lax.dynamic_slice_in_dim(grad_pre_node, own_start, node_rows, 0)
        grad_node = grad_node + jnp.dot(own_in.T, own_pre, preferred_element_type=jnp.float32)
        own_grad = lax.dynamic_slice_in_dim(grad_node_in, own_start, node_rows, 0)
        grad_agg = grad_node_in[:, width_x : width_x + width_m].astype(jnp.bfloat16)
        grad_message = grad_agg[dst_local] * alive_half
        grad_second = grad_second + jnp.dot(
            hidden.T, grad_message, preferred_element_type=jnp.float32
        )
        grad_hidden = jnp.dot(grad_message, edge_w2.T, preferred_element_type=jnp.float32)
        grad_pre_edge = (grad_hidden * silu_slope(pre_edge)).astype(jnp.bfloat16)
        grad_first = grad_first + jnp.dot(
            edge_in.T, grad_pre_edge, preferred_element_type=jnp.float32
        )
        grad_edge_in = jnp.dot(grad_pre_edge, edge_w1.T, preferred_element_type=jnp.float32)
        source_part = jax.ops.segment_sum(
            grad_edge_in[:, :width_x], src_local, num_segments=src_rows
        )
        target_part = jax.ops.segment_sum(
            grad_edge_in[:, width_x : 2 * width_x], dst_local, num_segments=dst_rows
        )
        from_sources = lax.psum_scatter(source_part, "dst", scatter_dimension=0, tiled=True)
        from_targets = lax.psum_scatter(target_part, "src", scatter_dimension=0, tiled=True)
        state_out.append(own_grad[:, :width_x] + from_sources + from_targets)
        forcing_out.append(own_grad[:, width_x + width_m :])
        edge_out.append(grad_edge_in[:, 2 * width_x :])
    grad_first, grad_second, grad_node = lax.psum(
        (grad_first, grad_second, grad_node), ("src", "dst")
    )
    return (
        jnp.stack(state_out),
        jnp.stack(forcing_out),
        jnp.stack(edge_out)[:, None, None],
        grad_first,
        grad_second,
        grad_node,
    )


def solution(mesh):
    in_specs = (
        P(None, ("groups", "src", "dst"), None),
        P(None, ("groups", "src", "dst"), None),
        P(None, ("groups", "src"), "dst", None, None),
        P(("groups", "src"), "dst", None),
        P(("groups", "src"), "dst", None),
        P(("groups", "src"), "dst"),
        P(None, ("groups", "src", "dst"), None),
        P(),
        P(),
        P(),
    )
    out_specs = (
        P(None, ("groups", "src", "dst"), None),
        P(None, ("groups", "src", "dst"), None),
        P(None, ("groups", "src"), "dst", None, None),
        P("groups", None),
        P("groups", None),
        P("groups", None),
    )
    square = mesh.shape["src"] == WAYS and mesh.shape["dst"] == WAYS
    body = local if square else local_any
    return jax.shard_map(body, mesh=mesh, in_specs=in_specs, out_specs=out_specs, check_vma=False)
```

```python
import functools

import jax
import jax.numpy as jnp
from jax import lax
from jax.experimental import pallas as pl
from jax.experimental.pallas import tpu as pltpu
from jax.sharding import PartitionSpec as P

T_STEPS = 2
WAYS = 4
LANES = 128
BF = jnp.bfloat16
F32 = jnp.float32


def sigmoid(value):
    return 0.5 * jnp.tanh(0.5 * value) + 0.5


def slope_of(value):
    sigma = sigmoid(value)
    return sigma * (1.0 + value * (1.0 - sigma))


def mm(a, b):
    return jnp.dot(a, b, preferred_element_type=F32)


def mm_nt(a, b):
    return lax.dot_general(a, b, (((1,), (1,)), ((), ())), preferred_element_type=F32)


def mm_tn(a, b):
    return lax.dot_general(a, b, (((0,), (0,)), ((), ())), preferred_element_type=F32)


def one_hot_t(index, nodes, live=None):
    hit = lax.broadcasted_iota(jnp.int32, (nodes, index.shape[1]), 0) == index
    if live is not None:
        hit = jnp.logical_and(hit, live)
    return jnp.where(hit, 1.0, 0.0).astype(BF)


def stacked(refs, moment):
    return jnp.concatenate([ref[moment] for ref in refs], axis=0)


def summed(refs, moment):
    rows = refs[0].shape[1] // WAYS
    return jnp.concatenate(
        [
            sum(ref[moment, (j ^ k) * rows : ((j ^ k) + 1) * rows].astype(F32) for k, ref in enumerate(refs))
            for j in range(WAYS)
        ],
        axis=0,
    )


def join_kernel(state, forcing, cotangent, joined, sems):
    width = state.shape[2]
    copies = [
        pltpu.make_async_copy(state, joined.at[:, :, :width], sems.at[0]),
        pltpu.make_async_copy(forcing, joined.at[:, :, width : 2 * width], sems.at[1]),
        pltpu.make_async_copy(cotangent, joined.at[:, :, 2 * width :], sems.at[2]),
    ]
    for copy in copies:
        copy.start()
    for copy in copies:
        copy.wait()


def stage_kernel(count, src_hbm, dst_hbm, state, attr_hbm, w1_hbm, w2_hbm, wn_hbm, *refs):
    own, attr, w1, w2, wn, src_t, dst_t, base, src_held, dst_held, sems = refs
    width = state.shape[2]
    copies = [
        pltpu.make_async_copy(source, target, sems.at[i])
        for i, (source, target) in enumerate(
            [
                (src_hbm, src_held),
                (dst_hbm, dst_held),
                (attr_hbm, attr),
                (w1_hbm, w1),
                (state, own),
                (w2_hbm, w2),
                (wn_hbm, wn),
            ]
        )
    ]
    for copy in copies:
        copy.start()
    copies[0].wait()
    copies[1].wait()
    rows = own.shape[1]
    nodes, slots = src_t.shape
    live = lax.broadcasted_iota(jnp.int32, (1, slots), 1) < count[0, 0]
    src_t[...] = one_hot_t(src_held[...] ^ (lax.axis_index("dst") * rows), nodes)
    dst_t[...] = one_hot_t(dst_held[...] ^ (lax.axis_index("src") * rows), nodes, live)
    copies[2].wait()
    copies[3].wait()
    for moment in range(T_STEPS):
        base[moment] = mm(attr[moment], w1[2 * width :])
    for copy in copies[4:]:
        copy.wait()


def forward_kernel(*refs):
    sources, targets = refs[:WAYS], refs[WAYS : 2 * WAYS]
    base, src_t, dst_t, w1, w2 = refs[2 * WAYS : 2 * WAYS + 5]
    message, message_own, slope, *pieces, held = refs[2 * WAYS + 5 :]
    width = sources[0].shape[2]
    for moment in range(T_STEPS):
        ends = jnp.concatenate(
            [
                mm_tn(src_t[...], stacked(sources, moment)).astype(BF),
                mm_tn(dst_t[...], stacked(targets, moment)[:, :width]).astype(BF),
            ],
            axis=1,
        )
        pre = base[moment] + mm(ends, w1[: 2 * width])
        sigma = sigmoid(pre)
        hidden = (pre * sigma).astype(BF)
        slope[moment] = sigma * (1.0 + pre * (1.0 - sigma))
        sums = mm(dst_t[...], hidden)
        high = sums.astype(BF)
        low = (sums - high.astype(F32)).astype(BF)
        held[moment] = high
        total = mm(high, w2[...]) + mm(low, w2[...])
        message_own[moment] = total
        message[moment] = total.astype(BF)
    block = w1.shape[1] // WAYS
    for k in range(WAYS):
        start = pl.multiple_of((lax.axis_index("src") ^ k) * block, block)
        pieces[k][...] = held[:, :, pl.ds(start, block)]


def backward_kernel(*refs):
    n = WAYS
    sources, targets, messages = refs[:n], refs[n : 2 * n], refs[2 * n : 3 * n]
    attr, src_t, dst_t, slope, w1, w2, wn = refs[3 * n : 3 * n + 7]
    state_own, forcing_own, edges, agg_held, node_grad, to_src, to_dst, first = refs[3 * n + 7 : 3 * n + 15]
    node_held, pre_held, gpe_held, p_held, q_held = refs[3 * n + 15 :]
    rows, width = sources[0].shape[1], sources[0].shape[2]
    nodes = rows * n
    slots = attr.shape[1]
    width_m = w2.shape[1]
    for moment in range(T_STEPS):
        at = slice(moment * nodes, (moment + 1) * nodes)
        block = stacked(targets, moment)
        state, forcing, cotangent = block[:, :width], block[:, width : 2 * width], block[:, 2 * width :]
        agg = summed(messages, moment)
        node_in = jnp.concatenate([state, agg.astype(BF), forcing], axis=1)
        pre_node = mm(node_in, wn[...])
        grad_pre = (cotangent.astype(F32) * slope_of(pre_node)).astype(BF)
        node_held[at] = node_in
        pre_held[at] = grad_pre
        grad_in = mm_nt(grad_pre, wn[...])
        state_own[moment] = grad_in[:rows, :width]
        forcing_own[moment] = grad_in[:rows, width + width_m :]
        grad_agg = grad_in[:, width : width + width_m].astype(BF)
        agg_held[at] = grad_agg
        grad_message = mm_tn(dst_t[...], grad_agg).astype(BF)
        grad_pre_edge = (mm_nt(grad_message, w2[...]) * slope[moment]).astype(BF)
        gpe_held[moment * slots : (moment + 1) * slots] = grad_pre_edge
        edges[moment] = mm_nt(grad_pre_edge, w1[2 * width :])
        from_src = mm(src_t[...], grad_pre_edge).astype(BF)
        from_dst = mm(dst_t[...], grad_pre_edge).astype(BF)
        p_held[at] = from_src
        q_held[at] = from_dst
        to_src[moment] = mm_nt(from_src, w1[:width]).astype(BF)
        to_dst[moment] = mm_nt(from_dst, w1[width : 2 * width]).astype(BF)
    states = jnp.concatenate([stacked(sources, moment) for moment in range(T_STEPS)], axis=0)
    first[:width] = mm_tn(states, p_held[...])
    first[width : 2 * width] = mm_tn(node_held[:, :width], q_held[...])
    first[2 * width :] = mm_tn(attr[...].reshape(T_STEPS * slots, width), gpe_held[...])
    block = wn.shape[0] // n
    spot = pl.multiple_of(lax.axis_index("src") * block, block)
    node_grad[...] = mm_tn(node_held[:, pl.ds(spot, block)], pre_held[...])


def pack_kernel(*refs):
    n = WAYS
    pieces, (agg_held, node_grad, to_src, to_dst, first) = refs[:n], refs[n : n + 5]
    over_dst, over_src = refs[n + 5 : 2 * n + 5], refs[2 * n + 5 : 3 * n + 5]
    held = refs[3 * n + 5]
    width = to_src.shape[2]
    rows = to_src.shape[1] // n
    half = rows // 2
    sums = jnp.concatenate([summed(pieces, moment) for moment in range(T_STEPS)], axis=0).astype(BF)
    second = mm_tn(sums, agg_held[...])
    held[:, : second.shape[1]] = second
    held[:, second.shape[1] :] = node_grad[...]
    part = first.shape[0] // n
    small = held.shape[0] // n
    for k in range(n):
        other = lax.axis_index("dst") ^ k
        over_dst[k][:part] = first[pl.ds(pl.multiple_of(other * part, part), part)].astype(BF)
        over_dst[k][part : part + small] = held[pl.ds(pl.multiple_of(other * small, small), small)].astype(BF)
        for moment in range(T_STEPS):
            for j in range(2):
                lanes = slice((moment * 2 + j) * width, (moment * 2 + j + 1) * width)
                spot = slice(k * rows + j * half, k * rows + (j + 1) * half)
                over_dst[k][-half:, lanes] = to_src[moment, spot]
                over_src[k][:, lanes] = to_dst[moment, spot]


def middle_kernel(state_own, *refs):
    n = WAYS
    parts, pieces = refs[:n], refs[n : 2 * n]
    state_sum, own, *sent = refs[2 * n :]
    total = sum(ref[...].astype(F32) for ref in parts)
    half = pieces[0].shape[0]
    width = state_own.shape[2]
    core = total[:-half]
    own[...] = core
    rounded = core.astype(BF)
    nodes = total[-half:] + pieces[0][...].astype(F32)
    for moment in range(T_STEPS):
        for j in range(2):
            lanes = slice((moment * 2 + j) * width, (moment * 2 + j + 1) * width)
            spot = slice(j * half, (j + 1) * half)
            state_sum[moment, spot] = state_own[moment, spot] + nodes[:, lanes]
    for k in range(1, n):
        sent[k - 1][:-half] = rounded
        sent[k - 1][-half:] = pieces[k][...]


def gather_kernel(state_sum, own, *refs):
    n = WAYS
    arrived = refs[: n - 1]
    state, sent = refs[n - 1 :]
    width = state_sum.shape[2]
    half = state_sum.shape[1] // 2
    wide = own.shape[0]
    small = (sent.shape[0] - wide) // (n - 1)
    part = wide - small
    nodes = sum(ref[wide:].astype(F32) for ref in arrived)
    for moment in range(T_STEPS):
        for j in range(2):
            lanes = slice((moment * 2 + j) * width, (moment * 2 + j + 1) * width)
            spot = slice(j * half, (j + 1) * half)
            state[moment, spot] = state_sum[moment, spot] + nodes[:, lanes]
    first = own[:part] + sum(ref[:part].astype(F32) for ref in arrived)
    sent[:part] = first.astype(BF)
    for k in range(n):
        start = pl.multiple_of(part + (lax.axis_index("src") ^ k) * small, small)
        sent[pl.ds(start, small)] = own[part:].astype(BF) if k == 0 else arrived[k - 1][part:wide]


def final_kernel(*refs):
    n = WAYS
    arrived = refs[:n]
    first, second, node = refs[n:]
    part = first.shape[0] // n
    small = second.shape[0] // n // n
    half = second.shape[1]
    for k in range(n):
        other = lax.axis_index("dst") ^ k
        first[pl.ds(pl.multiple_of(other * part, part), part)] = arrived[k][:part].astype(F32)
        for j in range(n):
            rows = arrived[k][part + j * small : part + (j + 1) * small].astype(F32)
            start = pl.multiple_of((j * n + other) * small, small)
            second[pl.ds(start, small)] = rows[:, :half]
            node[pl.ds(start, small)] = rows[:, half:]


def call(kernel, outs, scratch, args, spaces=None):
    return pl.pallas_call(
        kernel,
        out_shape=[jax.ShapeDtypeStruct(shape, dtype) for shape, dtype in outs],
        in_specs=[pl.BlockSpec(memory_space=space) for space in spaces or [pltpu.VMEM] * len(args)],
        out_specs=[pl.BlockSpec(memory_space=pltpu.VMEM)] * len(outs),
        scratch_shapes=[
            pltpu.VMEM(*entry) if isinstance(entry, tuple) else entry for entry in scratch
        ],
        compiler_params=pltpu.CompilerParams(vmem_limit_bytes=32 << 20),
    )(*args)


def in_hbm(value):
    return pltpu.with_memory_space_constraint(value, pltpu.HBM)


def swap(value, axis, k):
    return lax.ppermute(value, axis, [(i, i ^ k) for i in range(WAYS)])


def fan(value, axis):
    return [value] + [swap(value, axis, k) for k in range(1, WAYS)]


def exchange(values, axis):
    return [values[0]] + [swap(values[k], axis, k) for k in range(1, WAYS)]


def local(
    node_state,
    forcing,
    edge_attr,
    src_index,
    dst_index,
    edge_count,
    cotangent,
    edge_w1,
    edge_w2,
    node_w1,
):
    rows, width = node_state.shape[1:]
    hid, width_m = edge_w2.shape
    width_in, width_out = node_w1.shape
    slots = edge_attr.shape[3]
    nodes = rows * WAYS
    steps = T_STEPS
    attr = edge_attr[:, 0, 0]
    sources = fan(node_state, "dst")
    joined = call(
        join_kernel,
        [((steps, rows, 2 * width + width_out), BF)],
        [pltpu.SemaphoreType.DMA((3,))],
        [in_hbm(value) for value in (node_state, forcing, cotangent)],
        [pltpu.HBM] * 3,
    )[0]
    targets = fan(joined, "src")
    state_in, attr, w1, w2, wn, src_t, dst_t, base = call(
        stage_kernel,
        [
            (node_state.shape, BF),
            (attr.shape, BF),
            (edge_w1.shape, BF),
            (edge_w2.shape, BF),
            (node_w1.shape, BF),
            ((nodes, slots), BF),
            ((nodes, slots), BF),
            ((steps, slots, hid), F32),
        ],
        [((1, slots), jnp.int32), ((1, slots), jnp.int32), pltpu.SemaphoreType.DMA((7,))],
        [edge_count]
        + [in_hbm(value) for value in (src_index[0], dst_index[0], node_state, attr, edge_w1, edge_w2, node_w1)],
        [pltpu.SMEM] + [pltpu.HBM] * 7,
    )
    sources = [state_in] + sources[1:]
    block = hid // WAYS
    message, message_own, slope, *pieces = call(
        forward_kernel,
        [((steps, nodes, width_m), BF), ((steps, nodes, width_m), F32), ((steps, slots, hid), F32)]
        + [((steps, nodes, block), BF)] * WAYS,
        [((steps, nodes, hid), BF)],
        [*sources, *targets, base, src_t, dst_t, w1, w2],
    )
    messages = [message_own] + fan(message, "src")[1:]
    pieces = exchange(pieces, "src")
    part = edge_w1.shape[0] // WAYS
    small = block // WAYS
    half = rows // 2
    wide = part + small
    state_own, grad_forcing, edges, *partials = call(
        backward_kernel,
        [
            ((steps, rows, width), F32),
            ((steps, rows, width), F32),
            ((steps, slots, width), F32),
            ((steps * nodes, width_m), BF),
            ((block, width_out), F32),
            ((steps, nodes, width), BF),
            ((steps, nodes, width), BF),
            (edge_w1.shape, F32),
        ],
        [
            ((steps * nodes, width_in), BF),
            ((steps * nodes, width_out), BF),
            ((steps * slots, hid), BF),
            ((steps * nodes, hid), BF),
            ((steps * nodes, hid), BF),
        ],
        [*sources, *targets, *messages, attr, src_t, dst_t, slope, w1, w2, wn],
    )
    sent = call(
        pack_kernel,
        [((wide + half, hid), BF)] * WAYS + [((half, hid), BF)] * WAYS,
        [((block, hid), F32)],
        [*pieces, *partials],
    )
    over_dst, over_src = sent[:WAYS], sent[WAYS:]
    state_sum, own, *sent = call(
        middle_kernel,
        [((steps, rows, width), F32), ((wide, hid), F32)] + [((wide + half, hid), BF)] * (WAYS - 1),
        [],
        [state_own, *exchange(over_dst, "dst"), *over_src],
    )
    arrived = [swap(sent[k - 1], "src", k) for k in range(1, WAYS)]
    grad_state, share = call(
        gather_kernel,
        [((steps, rows, width), F32), ((wide + (WAYS - 1) * small, hid), BF)],
        [],
        [state_sum, own, *arrived],
    )
    across = swap(share, "dst", 2)
    grad_first, grad_second, grad_node = call(
        final_kernel,
        [(edge_w1.shape, F32), (edge_w2.shape, F32), (node_w1.shape, F32)],
        [],
        [share, swap(share, "dst", 1), across, swap(across, "dst", 1)],
    )
    return grad_state, grad_forcing, edges[:, None, None], grad_first, grad_second, grad_node


def silu_slope(value):
    sigma = jax.nn.sigmoid(value)
    return sigma * (1.0 + value * (1.0 - sigma))


def local_any(
    node_state,
    forcing,
    edge_attr,
    src_index,
    dst_index,
    edge_count,
    cotangent,
    edge_w1,
    edge_w2,
    node_w1,
):
    node_rows = node_state.shape[1]
    width_x = node_state.shape[2]
    width_m = edge_w2.shape[1]
    src_rows = node_rows * lax.axis_size("dst")
    dst_rows = node_rows * lax.axis_size("src")
    sources = lax.all_gather(node_state, "dst", axis=1, tiled=True)
    targets, forcing_block, cotangent_block = (
        lax.all_gather(node_state, "src", axis=1, tiled=True),
        lax.all_gather(forcing, "src", axis=1, tiled=True),
        lax.all_gather(cotangent, "src", axis=1, tiled=True),
    )
    src_local = src_index[0, 0]
    dst_local = dst_index[0, 0]
    alive = lax.iota(jnp.int32, src_local.shape[0]) < edge_count[0, 0]
    alive_float = alive.astype(jnp.float32)[:, None]
    alive_half = alive.astype(jnp.bfloat16)[:, None]
    own_start = lax.axis_index("src") * node_rows
    grad_first = jnp.zeros(edge_w1.shape, jnp.float32)
    grad_second = jnp.zeros(edge_w2.shape, jnp.float32)
    grad_node = jnp.zeros(node_w1.shape, jnp.float32)
    state_out, forcing_out, edge_out = ([], [], [])
    for moment in range(T_STEPS):
        edge_in = jnp.concatenate(
            [sources[moment][src_local], targets[moment][dst_local], edge_attr[moment, 0, 0]],
            axis=1,
        )
        pre_edge = jnp.dot(edge_in, edge_w1, preferred_element_type=jnp.float32)
        hidden = jax.nn.silu(pre_edge).astype(jnp.bfloat16)
        message = jnp.dot(hidden, edge_w2, preferred_element_type=jnp.float32) * alive_float
        partial_value = jax.ops.segment_sum(message, dst_local, num_segments=dst_rows)
        agg_block = lax.psum(partial_value, "src")
        node_in = jnp.concatenate(
            [targets[moment], agg_block.astype(jnp.bfloat16), forcing_block[moment]], axis=1
        )
        pre_node = jnp.dot(node_in, node_w1, preferred_element_type=jnp.float32)
        grad_pre_node = (cotangent_block[moment].astype(jnp.float32) * silu_slope(pre_node)).astype(
            jnp.bfloat16
        )
        grad_node_in = jnp.dot(grad_pre_node, node_w1.T, preferred_element_type=jnp.float32)
        own_in = lax.dynamic_slice_in_dim(node_in, own_start, node_rows, 0)
        own_pre = lax.dynamic_slice_in_dim(grad_pre_node, own_start, node_rows, 0)
        grad_node = grad_node + jnp.dot(own_in.T, own_pre, preferred_element_type=jnp.float32)
        own_grad = lax.dynamic_slice_in_dim(grad_node_in, own_start, node_rows, 0)
        grad_agg = grad_node_in[:, width_x : width_x + width_m].astype(jnp.bfloat16)
        grad_message = grad_agg[dst_local] * alive_half
        grad_second = grad_second + jnp.dot(
            hidden.T, grad_message, preferred_element_type=jnp.float32
        )
        grad_hidden = jnp.dot(grad_message, edge_w2.T, preferred_element_type=jnp.float32)
        grad_pre_edge = (grad_hidden * silu_slope(pre_edge)).astype(jnp.bfloat16)
        grad_first = grad_first + jnp.dot(
            edge_in.T, grad_pre_edge, preferred_element_type=jnp.float32
        )
        grad_edge_in = jnp.dot(grad_pre_edge, edge_w1.T, preferred_element_type=jnp.float32)
        source_part = jax.ops.segment_sum(
            grad_edge_in[:, :width_x], src_local, num_segments=src_rows
        )
        target_part = jax.ops.segment_sum(
            grad_edge_in[:, width_x : 2 * width_x], dst_local, num_segments=dst_rows
        )
        from_sources = lax.psum_scatter(source_part, "dst", scatter_dimension=0, tiled=True)
        from_targets = lax.psum_scatter(target_part, "src", scatter_dimension=0, tiled=True)
        state_out.append(own_grad[:, :width_x] + from_sources + from_targets)
        forcing_out.append(own_grad[:, width_x + width_m :])
        edge_out.append(grad_edge_in[:, 2 * width_x :])
    grad_first, grad_second, grad_node = lax.psum(
        (grad_first, grad_second, grad_node), ("src", "dst")
    )
    return (
        jnp.stack(state_out),
        jnp.stack(forcing_out),
        jnp.stack(edge_out)[:, None, None],
        grad_first,
        grad_second,
        grad_node,
    )


def solution(mesh):
    in_specs = (
        P(None, ("groups", "src", "dst"), None),
        P(None, ("groups", "src", "dst"), None),
        P(None, ("groups", "src"), "dst", None, None),
        P(("groups", "src"), "dst", None),
        P(("groups", "src"), "dst", None),
        P(("groups", "src"), "dst"),
        P(None, ("groups", "src", "dst"), None),
        P(),
        P(),
        P(),
    )
    out_specs = (
        P(None, ("groups", "src", "dst"), None),
        P(None, ("groups", "src", "dst"), None),
        P(None, ("groups", "src"), "dst", None, None),
        P("groups", None),
        P("groups", None),
        P("groups", None),
    )
    square = mesh.shape["src"] == WAYS and mesh.shape["dst"] == WAYS
    body = local if square else local_any
    return jax.shard_map(body, mesh=mesh, in_specs=in_specs, out_specs=out_specs, check_vma=False)
```

```python
import functools

import jax
import jax.numpy as jnp
from jax import lax
from jax.experimental import pallas as pl
from jax.experimental.pallas import tpu as pltpu
from jax.sharding import PartitionSpec as P

T_STEPS = 2
WAYS = 4
ORDER = (3, 1, 2)
BF = jnp.bfloat16
F32 = jnp.float32


def sigmoid(value):
    return 0.5 * jnp.tanh(0.5 * value) + 0.5


def slope_of(value):
    sigma = sigmoid(value)
    return sigma * (1.0 + value * (1.0 - sigma))


def mm(a, b):
    return jnp.dot(a, b, preferred_element_type=F32)


def mm_nt(a, b):
    return lax.dot_general(a, b, (((1,), (1,)), ((), ())), preferred_element_type=F32)


def mm_tn(a, b):
    return lax.dot_general(a, b, (((0,), (0,)), ((), ())), preferred_element_type=F32)


def one_hot_t(index, nodes, live=None):
    hit = lax.broadcasted_iota(jnp.int32, (nodes, index.shape[1]), 0) == index
    if live is not None:
        hit = jnp.logical_and(hit, live)
    return jnp.where(hit, 1.0, 0.0).astype(BF)


def stacked(refs, moment):
    return jnp.concatenate([ref[moment] for ref in refs], axis=0)


def turned(value, k):
    rows = value.shape[0] // WAYS
    return jnp.concatenate([value[(j ^ k) * rows : ((j ^ k) + 1) * rows] for j in range(WAYS)], axis=0)


def join_kernel(near, state, forcing, cotangent, joined, sems):
    width = state.shape[2]
    copies = [
        pltpu.make_async_copy(state, joined.at[:, :, :width], sems.at[0]),
        pltpu.make_async_copy(forcing, joined.at[:, :, width : 2 * width], sems.at[1]),
        pltpu.make_async_copy(cotangent, joined.at[:, :, 2 * width :], sems.at[2]),
    ]
    for copy in copies:
        copy.start()
    for copy in copies:
        copy.wait()


def stage_kernel(count, src_hbm, dst_hbm, attr_hbm, w1_hbm, w2_hbm, wn_hbm, state_hbm, *refs):
    attr, w1, w2, wn, src_t, dst_t, base, state, src_held, dst_held, sems = refs
    width = attr.shape[2]
    copies = [
        pltpu.make_async_copy(source, target, sems.at[i])
        for i, (source, target) in enumerate(
            [
                (src_hbm, src_held),
                (dst_hbm, dst_held),
                (attr_hbm, attr),
                (w1_hbm, w1),
                (w2_hbm, w2),
                (wn_hbm, wn),
                (state_hbm, state),
            ]
        )
    ]
    for copy in copies:
        copy.start()
    copies[0].wait()
    copies[1].wait()
    nodes, slots = src_t.shape
    rows = nodes // WAYS
    live = lax.broadcasted_iota(jnp.int32, (1, slots), 1) < count[0, 0]
    src_t[...] = one_hot_t(src_held[...] ^ (lax.axis_index("dst") * rows), nodes)
    dst_t[...] = one_hot_t(dst_held[...] ^ (lax.axis_index("src") * rows), nodes, live)
    copies[2].wait()
    copies[3].wait()
    for moment in range(T_STEPS):
        base[moment] = mm(attr[moment], w1[2 * width :])
    for copy in copies[4:]:
        copy.wait()


def forward_kernel(moment, *refs):
    n = WAYS
    sources, targets, refs = refs[:n], refs[n : 2 * n], refs[2 * n :]
    base, src_t, dst_t, w1, w2, message, own, slope, sums = refs
    width = sources[0].shape[2]
    ends = jnp.concatenate(
        [
            mm_tn(src_t[...], stacked(sources, moment)).astype(BF),
            mm_tn(dst_t[...], stacked(targets, moment)[:, :width]).astype(BF),
        ],
        axis=1,
    )
    pre = base[moment] + mm(ends, w1[: 2 * width])
    sigma = sigmoid(pre)
    hidden = (pre * sigma).astype(BF)
    slope[...] = sigma * (1.0 + pre * (1.0 - sigma))
    total = mm(dst_t[...], hidden)
    high = total.astype(BF)
    low = (total - high.astype(F32)).astype(BF)
    sums[...] = high
    product = mm(high, w2[...]) + mm(low, w2[...])
    own[...] = product
    message[...] = product.astype(BF)


def first_sum_kernel(own, arrived, total, sent):
    value = own[...] + turned(arrived[...].astype(F32), 1)
    total[...] = value
    sent[...] = value.astype(BF)


def backward(moment, sources, targets, total, arrived, attr, src_t, dst_t, slope, sums, w1, w2, wn, node_held):
    n = WAYS
    rows, width = targets[0].shape[1], sources[0].shape[2]
    width_m = w2.shape[1]
    joined = stacked(targets, moment)
    state, forcing, cotangent = joined[:, :width], joined[:, width : 2 * width], joined[:, 2 * width :]
    agg = total[...] + turned(arrived[...].astype(F32), 2)
    node_in = jnp.concatenate([state, agg.astype(BF), forcing], axis=1)
    node_held[...] = node_in
    grad_pre = (cotangent.astype(F32) * slope_of(mm(node_in, wn[...]))).astype(BF)
    grad_in = mm_nt(grad_pre, wn[...])
    grad_agg = grad_in[:, width : width + width_m].astype(BF)
    grad_message = mm_tn(dst_t[...], grad_agg).astype(BF)
    grad_pre_edge = (mm_nt(grad_message, w2[...]) * slope[...]).astype(BF)
    edges = mm_nt(grad_pre_edge, w1[2 * width :])
    from_src = mm(src_t[...], grad_pre_edge).astype(BF)
    from_dst = mm(dst_t[...], grad_pre_edge).astype(BF)
    to_src = mm_nt(from_src, w1[:width])
    to_dst = mm_nt(from_dst, w1[width : 2 * width])
    first = [
        mm_tn(stacked(sources, moment), from_src),
        mm_tn(state, from_dst),
        mm_tn(attr[moment], grad_pre_edge),
    ]
    second = mm_tn(sums[...], grad_agg)
    block = wn.shape[0] // n
    spot = pl.multiple_of(lax.axis_index("src") * block, block)
    node_grad = mm_tn(node_held[:, pl.ds(spot, block)], grad_pre)
    state_own = grad_in[:rows, :width] + to_dst[:rows]
    return state_own, grad_in[:rows, width + width_m :], edges, to_src, to_dst, first, second, node_grad


def split_refs(refs):
    n = WAYS
    return refs[:n], refs[n : 2 * n], refs[2 * n : 2 * n + 10], refs[2 * n + 10 :]


def backward_first_kernel(*refs):
    sources, targets, args, refs = split_refs(refs)
    *outs, first_out, second_out, node_out, node_held = refs
    *values, first, second, node_grad = backward(0, sources, targets, *args, node_held)
    for ref, value in zip(outs, values, strict=True):
        ref[...] = value
    width = first[0].shape[0]
    for i, value in enumerate(first):
        first_out[i * width : (i + 1) * width] = value
    second_out[...] = second
    node_out[...] = node_grad


def backward_last_kernel(*refs):
    n = WAYS
    sources, targets, args, refs = split_refs(refs)
    state_0, forcing_0, edges_0, to_src_0, to_dst_0, first_0, second_0, node_0 = refs[:8]
    state_own, forcing_own, edges, kept_a, core_a, kept_b, core_b, target_kept, target_sent = refs[8:17]
    first_held, second_held, node_grad_held, node_held = refs[17:]
    state_1, forcing_1, edges_1, to_src_1, to_dst_1, first, second, node_grad = backward(
        1, sources, targets, *args, node_held
    )
    state_own[0], state_own[1] = state_0[...], state_1
    forcing_own[0], forcing_own[1] = forcing_0[...], forcing_1
    edges[0], edges[1] = edges_0[...], edges_1
    width = first[0].shape[0]
    for i, value in enumerate(first):
        first_held[i * width : (i + 1) * width] = first_0[i * width : (i + 1) * width] + value
    second_held[...] = second_0[...] + second
    node_grad_held[...] = node_0[...] + node_grad
    part, block, small = first_held.shape[0] // n, second_held.shape[0] // n, node_grad_held.shape[0] // n
    wide = node_grad_held.shape[1]
    for k in range(n):
        other = lax.axis_index("dst") ^ k
        into = core_a if k % 2 else kept_a
        start = (k // 2) * part
        into[start : start + part] = first_held[pl.ds(pl.multiple_of(other * part, part), part)].astype(into.dtype)
        into = core_b if k % 2 else kept_b
        start = (k // 2) * (into.shape[0] // 2)
        for j in range(2):
            lanes = slice(j * wide, (j + 1) * wide)
            size = block // 2
            spot = pl.ds(pl.multiple_of(other * block + j * size, size), size)
            into[start : start + size, lanes] = second_held[spot].astype(into.dtype)
            tiny = small // 2
            spot = pl.ds(pl.multiple_of(other * small + j * tiny, tiny), tiny)
            into[start + size : start + size + tiny, lanes] = node_grad_held[spot].astype(into.dtype)
        start += block // 2 + small // 2
        put_nodes(into, start, k, (to_src_0[...], to_src_1))
    put_nodes(target_kept, 0, 2, (to_dst_0[...], to_dst_1))
    for i, k in enumerate((1, 3)):
        put_nodes(target_sent, i * target_kept.shape[0], k, (to_dst_0[...], to_dst_1))


def put_nodes(into, start, k, values):
    width = values[0].shape[1]
    rows = values[0].shape[0] // WAYS
    half = rows // 2
    for moment, value in enumerate(values):
        for j in range(2):
            lanes = slice((moment * 2 + j) * width, (moment * 2 + j + 1) * width)
            spot = slice(k * rows + j * half, k * rows + (j + 1) * half)
            into[start : start + half, lanes] = value[spot].astype(into.dtype)


def add_nodes(state, base, value):
    width, half = state.shape[2], value.shape[0]
    for moment in range(T_STEPS):
        for j in range(2):
            lanes = slice((moment * 2 + j) * width, (moment * 2 + j + 1) * width)
            spot = slice(j * half, (j + 1) * half)
            state[moment, spot] = base[moment, spot] + value[:, lanes]


def near_kernel(kept, arrived, own, across):
    wide = own.shape[0]
    own[...] = kept[:wide] + arrived[:wide].astype(F32)
    across[...] = (kept[wide:] + arrived[wide:].astype(F32)).astype(BF)


def add_kernel(mine, arrived, own, sent):
    total = mine[...] + arrived[...].astype(F32)
    own[...] = total
    sent[...] = total.astype(BF)


def last_add_kernel(mine, arrived, sent):
    sent[...] = (mine[...] + arrived[...].astype(F32)).astype(BF)


def middle_kernel(mine, arrived, state_own, target_sent, state, own, sent):
    total = mine[...] + arrived[...].astype(F32)
    core = own.shape[0]
    own[...] = total[:core]
    sent[:core] = total[:core].astype(BF)
    sent[core:] = target_sent[...]
    add_nodes(state, state_own, total[core:])


def second_sum_kernel(mine, arrived, target_kept, state_in, state, own, sent):
    size, half = own.shape[0], target_kept.shape[0]
    core = mine.shape[0]
    tiny = core - size
    total = mine[:size] + arrived[:size].astype(F32)
    own[...] = total
    sent[:size] = total.astype(BF)
    sent[size:core] = mine[size:].astype(BF)
    sent[core : core + tiny] = arrived[size:core]
    add_nodes(state, state_in, arrived[core : core + half].astype(F32))
    sent[core + tiny :] = (target_kept[...] + arrived[core + half :].astype(F32)).astype(BF)


def gather_kernel(mine, sent, arrived, state_in, state, share):
    size, half = mine.shape[0], state.shape[1] // 2
    tiny = (share.shape[0] - size) // WAYS
    share[:size] = (mine[...] + arrived[:size].astype(F32)).astype(BF)
    add_nodes(state, state_in, arrived[size + 2 * tiny :].astype(F32))
    for k in range(WAYS):
        start = pl.multiple_of(size + (lax.axis_index("src") ^ k) * tiny, tiny)
        spot = slice(size + (k % 2) * tiny, size + (k % 2 + 1) * tiny)
        share[pl.ds(start, tiny)] = (arrived if k // 2 else sent)[spot]


def final_first_kernel(*refs):
    shares, out = refs[:WAYS], refs[WAYS]
    part = out.shape[0] // WAYS
    for k in range(WAYS):
        start = pl.multiple_of((lax.axis_index("dst") ^ k) * part, part)
        out[pl.ds(start, part)] = shares[k][...].astype(F32)


def final_second_kernel(*refs):
    n = WAYS
    shares, (second, node) = refs[:n], refs[n:]
    block = second.shape[0] // n
    small = block // n
    size, tiny = block // 2, small // 2
    wide = second.shape[1]
    for k in range(n):
        other = lax.axis_index("dst") ^ k
        for i in range(2):
            lanes = slice(i * wide, (i + 1) * wide)
            start = pl.multiple_of(other * block + i * size, size)
            second[pl.ds(start, size)] = shares[k][:size, lanes].astype(F32)
            for j in range(n):
                start = pl.multiple_of(j * block + other * small + i * tiny, tiny)
                spot = slice(size + j * tiny, size + (j + 1) * tiny)
                node[pl.ds(start, tiny)] = shares[k][spot, lanes].astype(F32)


def call(kernel, outs, scratch, args, spaces=None):
    return pl.pallas_call(
        kernel,
        out_shape=[jax.ShapeDtypeStruct(shape, dtype) for shape, dtype in outs],
        in_specs=[pl.BlockSpec(memory_space=space) for space in spaces or [pltpu.VMEM] * len(args)],
        out_specs=[pl.BlockSpec(memory_space=pltpu.VMEM)] * len(outs),
        scratch_shapes=[
            pltpu.VMEM(*entry) if isinstance(entry, tuple) else entry for entry in scratch
        ],
        compiler_params=pltpu.CompilerParams(vmem_limit_bytes=32 << 20),
    )(*args)


def in_hbm(value):
    return pltpu.with_memory_space_constraint(value, pltpu.HBM)


def swap(value, axis, k):
    return lax.ppermute(value, axis, [(i, i ^ k) for i in range(WAYS)])


def all_dst(share):
    across = swap(share, "dst", 2)
    return [share, swap(share, "dst", 1), across, swap(across, "dst", 1)]


def local(
    node_state,
    forcing,
    edge_attr,
    src_index,
    dst_index,
    edge_count,
    cotangent,
    edge_w1,
    edge_w2,
    node_w1,
):
    rows, width = node_state.shape[1:]
    hid, width_m = edge_w2.shape
    width_in, width_out = node_w1.shape
    slots = edge_attr.shape[3]
    nodes = rows * WAYS
    steps = T_STEPS
    attr = edge_attr[:, 0, 0]
    near = swap(node_state, "dst", 1)
    across = swap(node_state, "dst", 2)
    joined = call(
        join_kernel,
        [((steps, rows, 2 * width + width_out), BF)],
        [pltpu.SemaphoreType.DMA((3,))],
        [near, *(in_hbm(value) for value in (node_state, forcing, cotangent))],
        [pltpu.VMEM] + [pltpu.HBM] * 3,
    )[0]
    targets = {k: swap(joined, "src", k) for k in ORDER}
    targets = [joined] + [targets[k] for k in range(1, WAYS)]
    sources = [node_state, near, across, swap(near, "dst", 2)]
    attr, w1, w2, wn, src_t, dst_t, base, sources[0] = call(
        stage_kernel,
        [
            (attr.shape, BF),
            (edge_w1.shape, BF),
            (edge_w2.shape, BF),
            (node_w1.shape, BF),
            ((nodes, slots), BF),
            ((nodes, slots), BF),
            ((steps, slots, hid), F32),
            (node_state.shape, BF),
        ],
        [((1, slots), jnp.int32), ((1, slots), jnp.int32), pltpu.SemaphoreType.DMA((7,))],
        [edge_count]
        + [in_hbm(value) for value in (src_index[0], dst_index[0], attr, edge_w1, edge_w2, node_w1, node_state)],
        [pltpu.SMEM] + [pltpu.HBM] * 7,
    )
    forward, sums = [], []
    for moment in range(steps):
        forward.append(
            call(
                functools.partial(forward_kernel, moment),
                [((nodes, width_m), BF), ((nodes, width_m), F32), ((slots, hid), F32), ((nodes, hid), BF)],
                [],
                [*sources, *targets, base, src_t, dst_t, w1, w2],
            )
        )
    for message, own, _, _ in forward:
        total, sent = call(
            first_sum_kernel,
            [((nodes, width_m), F32), ((nodes, width_m), BF)],
            [],
            [own, swap(message, "src", 1)],
        )
        sums.append([total, swap(sent, "src", 2)])
    args = [
        [*sources, *targets, *sums[moment], attr, src_t, dst_t, *forward[moment][2:], w1, w2, wn]
        for moment in range(steps)
    ]
    block = width_in // WAYS
    earlier = call(
        backward_first_kernel,
        [
            ((rows, width), F32),
            ((rows, width), F32),
            ((slots, width), F32),
            ((nodes, width), F32),
            ((nodes, width), F32),
            (edge_w1.shape, F32),
            (edge_w2.shape, F32),
            ((block, width_out), F32),
        ],
        [((nodes, width_in), BF)],
        args[0],
    )
    part, size, tiny, half = edge_w1.shape[0] // WAYS, hid // WAYS // 2, block // WAYS // 2, rows // 2
    core = size + tiny
    wide = core + half
    state_own, grad_forcing, edges, kept_a, core_a, kept_b, core_b, target_kept, target_sent = call(
        backward_last_kernel,
        [
            ((steps, rows, width), F32),
            ((steps, rows, width), F32),
            ((steps, slots, width), F32),
            ((2 * part, hid), F32),
            ((2 * part, hid), BF),
            ((2 * wide, hid), F32),
            ((2 * wide, hid), BF),
            ((half, hid), F32),
            ((2 * half, hid), BF),
        ],
        [(edge_w1.shape, F32), (edge_w2.shape, F32), ((block, width_out), F32), ((nodes, width_in), BF)],
        [*args[1], *earlier],
    )

    def pair(size):
        return [((size, hid), F32), ((size, hid), BF)]

    state = ((steps, rows, width), F32)
    mine_a, across_a = call(near_kernel, pair(part), [], [kept_a, swap(core_a, "dst", 1)])
    mine_b, across_b = call(near_kernel, pair(wide), [], [kept_b, swap(core_b, "dst", 1)])
    own_a, sent_a = call(add_kernel, pair(part), [], [mine_a, swap(across_a, "dst", 2)])
    state_sum, own_b, sent_b = call(
        middle_kernel,
        [state, ((core, hid), F32), ((core + 2 * half, hid), BF)],
        [],
        [mine_b, swap(across_b, "dst", 2), state_own, target_sent],
    )
    own_a, sent_a = call(add_kernel, pair(part), [], [own_a, swap(sent_a, "src", 1)])
    state_sum, own_b, sent_b = call(
        second_sum_kernel,
        [state, ((size, hid), F32), ((core + tiny + half, hid), BF)],
        [],
        [own_b, swap(sent_b, "src", 1), target_kept, state_sum],
    )
    share_a = call(last_add_kernel, [((part, hid), BF)], [], [own_a, swap(sent_a, "src", 2)])[0]
    grad_state, share_b = call(
        gather_kernel,
        [state, ((size + WAYS * tiny, hid), BF)],
        [],
        [own_b, sent_b, swap(sent_b, "src", 2), state_sum],
    )
    grad_first = call(final_first_kernel, [(edge_w1.shape, F32)], [], all_dst(share_a))[0]
    grad_second, grad_node = call(
        final_second_kernel, [(edge_w2.shape, F32), (node_w1.shape, F32)], [], all_dst(share_b)
    )
    return grad_state, grad_forcing, edges[:, None, None], grad_first, grad_second, grad_node


def silu_slope(value):
    sigma = jax.nn.sigmoid(value)
    return sigma * (1.0 + value * (1.0 - sigma))


def local_any(
    node_state,
    forcing,
    edge_attr,
    src_index,
    dst_index,
    edge_count,
    cotangent,
    edge_w1,
    edge_w2,
    node_w1,
):
    node_rows = node_state.shape[1]
    width_x = node_state.shape[2]
    width_m = edge_w2.shape[1]
    src_rows = node_rows * lax.axis_size("dst")
    dst_rows = node_rows * lax.axis_size("src")
    sources = lax.all_gather(node_state, "dst", axis=1, tiled=True)
    targets, forcing_block, cotangent_block = (
        lax.all_gather(node_state, "src", axis=1, tiled=True),
        lax.all_gather(forcing, "src", axis=1, tiled=True),
        lax.all_gather(cotangent, "src", axis=1, tiled=True),
    )
    src_local = src_index[0, 0]
    dst_local = dst_index[0, 0]
    alive = lax.iota(jnp.int32, src_local.shape[0]) < edge_count[0, 0]
    alive_float = alive.astype(jnp.float32)[:, None]
    alive_half = alive.astype(jnp.bfloat16)[:, None]
    own_start = lax.axis_index("src") * node_rows
    grad_first = jnp.zeros(edge_w1.shape, jnp.float32)
    grad_second = jnp.zeros(edge_w2.shape, jnp.float32)
    grad_node = jnp.zeros(node_w1.shape, jnp.float32)
    state_out, forcing_out, edge_out = ([], [], [])
    for moment in range(T_STEPS):
        edge_in = jnp.concatenate(
            [sources[moment][src_local], targets[moment][dst_local], edge_attr[moment, 0, 0]],
            axis=1,
        )
        pre_edge = jnp.dot(edge_in, edge_w1, preferred_element_type=jnp.float32)
        hidden = jax.nn.silu(pre_edge).astype(jnp.bfloat16)
        message = jnp.dot(hidden, edge_w2, preferred_element_type=jnp.float32) * alive_float
        partial_value = jax.ops.segment_sum(message, dst_local, num_segments=dst_rows)
        agg_block = lax.psum(partial_value, "src")
        node_in = jnp.concatenate(
            [targets[moment], agg_block.astype(jnp.bfloat16), forcing_block[moment]], axis=1
        )
        pre_node = jnp.dot(node_in, node_w1, preferred_element_type=jnp.float32)
        grad_pre_node = (cotangent_block[moment].astype(jnp.float32) * silu_slope(pre_node)).astype(
            jnp.bfloat16
        )
        grad_node_in = jnp.dot(grad_pre_node, node_w1.T, preferred_element_type=jnp.float32)
        own_in = lax.dynamic_slice_in_dim(node_in, own_start, node_rows, 0)
        own_pre = lax.dynamic_slice_in_dim(grad_pre_node, own_start, node_rows, 0)
        grad_node = grad_node + jnp.dot(own_in.T, own_pre, preferred_element_type=jnp.float32)
        own_grad = lax.dynamic_slice_in_dim(grad_node_in, own_start, node_rows, 0)
        grad_agg = grad_node_in[:, width_x : width_x + width_m].astype(jnp.bfloat16)
        grad_message = grad_agg[dst_local] * alive_half
        grad_second = grad_second + jnp.dot(
            hidden.T, grad_message, preferred_element_type=jnp.float32
        )
        grad_hidden = jnp.dot(grad_message, edge_w2.T, preferred_element_type=jnp.float32)
        grad_pre_edge = (grad_hidden * silu_slope(pre_edge)).astype(jnp.bfloat16)
        grad_first = grad_first + jnp.dot(
            edge_in.T, grad_pre_edge, preferred_element_type=jnp.float32
        )
        grad_edge_in = jnp.dot(grad_pre_edge, edge_w1.T, preferred_element_type=jnp.float32)
        source_part = jax.ops.segment_sum(
            grad_edge_in[:, :width_x], src_local, num_segments=src_rows
        )
        target_part = jax.ops.segment_sum(
            grad_edge_in[:, width_x : 2 * width_x], dst_local, num_segments=dst_rows
        )
        from_sources = lax.psum_scatter(source_part, "dst", scatter_dimension=0, tiled=True)
        from_targets = lax.psum_scatter(target_part, "src", scatter_dimension=0, tiled=True)
        state_out.append(own_grad[:, :width_x] + from_sources + from_targets)
        forcing_out.append(own_grad[:, width_x + width_m :])
        edge_out.append(grad_edge_in[:, 2 * width_x :])
    grad_first, grad_second, grad_node = lax.psum(
        (grad_first, grad_second, grad_node), ("src", "dst")
    )
    return (
        jnp.stack(state_out),
        jnp.stack(forcing_out),
        jnp.stack(edge_out)[:, None, None],
        grad_first,
        grad_second,
        grad_node,
    )


def solution(mesh):
    in_specs = (
        P(None, ("groups", "src", "dst"), None),
        P(None, ("groups", "src", "dst"), None),
        P(None, ("groups", "src"), "dst", None, None),
        P(("groups", "src"), "dst", None),
        P(("groups", "src"), "dst", None),
        P(("groups", "src"), "dst"),
        P(None, ("groups", "src", "dst"), None),
        P(),
        P(),
        P(),
    )
    out_specs = (
        P(None, ("groups", "src", "dst"), None),
        P(None, ("groups", "src", "dst"), None),
        P(None, ("groups", "src"), "dst", None, None),
        P("groups", None),
        P("groups", None),
        P("groups", None),
    )
    square = mesh.shape["src"] == WAYS and mesh.shape["dst"] == WAYS
    body = local if square else local_any
    return jax.shard_map(body, mesh=mesh, in_specs=in_specs, out_specs=out_specs, check_vma=False)
```

```python
import functools

import jax
import jax.numpy as jnp
from jax import lax
from jax.experimental import pallas as pl
from jax.experimental.pallas import tpu as pltpu
from jax.sharding import PartitionSpec as P

T_STEPS = 2
WAYS = 4
ORDER = (3, 1, 2)
BF = jnp.bfloat16
F32 = jnp.float32


def sigmoid(value):
    return 0.5 * jnp.tanh(0.5 * value) + 0.5


def slope_of(value):
    sigma = sigmoid(value)
    return sigma * (1.0 + value * (1.0 - sigma))


def mm(a, b):
    return jnp.dot(a, b, preferred_element_type=F32)


def mm_nt(a, b):
    return lax.dot_general(a, b, (((1,), (1,)), ((), ())), preferred_element_type=F32)


def mm_tn(a, b):
    return lax.dot_general(a, b, (((0,), (0,)), ((), ())), preferred_element_type=F32)


def one_hot_t(index, nodes, live=None):
    hit = lax.broadcasted_iota(jnp.int32, (nodes, index.shape[1]), 0) == index
    if live is not None:
        hit = jnp.logical_and(hit, live)
    return jnp.where(hit, 1.0, 0.0).astype(BF)


def stacked(refs, moment, width):
    return jnp.concatenate([ref[moment, :, :width] for ref in refs], axis=0)


def turned(value, k):
    rows = value.shape[0] // WAYS
    return jnp.concatenate([value[(j ^ k) * rows : ((j ^ k) + 1) * rows] for j in range(WAYS)], axis=0)


def join_kernel(state, forcing, cotangent, joined, sems):
    width = state.shape[2]
    copies = [
        pltpu.make_async_copy(state, joined.at[:, :, :width], sems.at[0]),
        pltpu.make_async_copy(forcing, joined.at[:, :, width : 2 * width], sems.at[1]),
        pltpu.make_async_copy(cotangent, joined.at[:, :, 2 * width :], sems.at[2]),
    ]
    for copy in copies:
        copy.start()
    for copy in copies:
        copy.wait()


def stage_kernel(count, src_hbm, dst_hbm, attr_hbm, w1_hbm, w2_hbm, wn_hbm, *refs):
    attr, w1, w2, wn, src_t, dst_t, base, src_held, dst_held, sems = refs
    width = attr.shape[2]
    nodes, slots = src_t.shape
    rows = nodes // WAYS
    copies = [
        pltpu.make_async_copy(source, target, sems.at[i])
        for i, (source, target) in enumerate(
            [
                (src_hbm, src_held),
                (dst_hbm, dst_held),
                (attr_hbm, attr),
                (w1_hbm, w1),
                (w2_hbm, w2),
                (wn_hbm, wn),
            ]
        )
    ]
    for copy in copies:
        copy.start()
    copies[0].wait()
    copies[1].wait()
    live = lax.broadcasted_iota(jnp.int32, (1, slots), 1) < count[0, 0]
    src_t[...] = one_hot_t(src_held[...] ^ (lax.axis_index("dst") * rows), nodes)
    dst_t[...] = one_hot_t(dst_held[...] ^ (lax.axis_index("src") * rows), nodes, live)
    copies[2].wait()
    copies[3].wait()
    for moment in range(T_STEPS):
        base[moment] = mm(attr[moment], w1[2 * width :])
    for copy in copies[4:]:
        copy.wait()


def forward_kernel(moment, *refs):
    n = WAYS
    sources, targets, refs = refs[:n], refs[n : 2 * n], refs[2 * n :]
    base, src_t, dst_t, w1, w2, message, own, slope, sums = refs
    width = sources[1].shape[2]
    ends = jnp.concatenate(
        [
            mm_tn(src_t[...], stacked(sources, moment, width)).astype(BF),
            mm_tn(dst_t[...], stacked(targets, moment, width)).astype(BF),
        ],
        axis=1,
    )
    pre = base[moment] + mm(ends, w1[: 2 * width])
    sigma = sigmoid(pre)
    hidden = (pre * sigma).astype(BF)
    slope[...] = sigma * (1.0 + pre * (1.0 - sigma))
    total = mm(dst_t[...], hidden)
    high = total.astype(BF)
    low = (total - high.astype(F32)).astype(BF)
    sums[...] = high
    product = mm(high, w2[...]) + mm(low, w2[...])
    own[...] = product
    message[...] = product.astype(BF)


def first_sum_kernel(own, arrived, total, sent):
    value = own[...] + turned(arrived[...].astype(F32), 1)
    total[...] = value
    sent[...] = value.astype(BF)


def backward(moment, sources, targets, total, arrived, attr, src_t, dst_t, slope, sums, w1, w2, wn, node_held):
    n = WAYS
    rows, width = sources[1].shape[1:]
    width_m = w2.shape[1]
    joined = stacked(targets, moment, targets[0].shape[2])
    state, forcing, cotangent = joined[:, :width], joined[:, width : 2 * width], joined[:, 2 * width :]
    agg = total[...] + turned(arrived[...].astype(F32), 2)
    node_in = jnp.concatenate([state, agg.astype(BF), forcing], axis=1)
    node_held[...] = node_in
    grad_pre = (cotangent.astype(F32) * slope_of(mm(node_in, wn[...]))).astype(BF)
    grad_in = mm_nt(grad_pre, wn[...])
    grad_agg = grad_in[:, width : width + width_m].astype(BF)
    grad_message = mm_tn(dst_t[...], grad_agg).astype(BF)
    grad_pre_edge = (mm_nt(grad_message, w2[...]) * slope[...]).astype(BF)
    edges = mm_nt(grad_pre_edge, w1[2 * width :])
    from_src = mm(src_t[...], grad_pre_edge).astype(BF)
    from_dst = mm(dst_t[...], grad_pre_edge).astype(BF)
    to_src = mm_nt(from_src, w1[:width])
    to_dst = mm_nt(from_dst, w1[width : 2 * width])
    first = [
        mm_tn(stacked(sources, moment, width), from_src),
        mm_tn(state, from_dst),
        mm_tn(attr[moment], grad_pre_edge),
    ]
    second = mm_tn(sums[...], grad_agg)
    block = wn.shape[0] // n
    spot = pl.multiple_of(lax.axis_index("src") * block, block)
    node_grad = mm_tn(node_held[:, pl.ds(spot, block)], grad_pre)
    state_own = grad_in[:rows, :width] + to_dst[:rows]
    return state_own, grad_in[:rows, width + width_m :], edges, to_src, to_dst, first, second, node_grad


def split_refs(refs):
    n = WAYS
    return refs[:n], refs[n : 2 * n], refs[2 * n : 2 * n + 10], refs[2 * n + 10 :]


def backward_first_kernel(*refs):
    sources, targets, args, refs = split_refs(refs)
    *outs, first_out, second_out, node_out, node_held = refs
    *values, first, second, node_grad = backward(0, sources, targets, *args, node_held)
    for ref, value in zip(outs, values, strict=True):
        ref[...] = value
    width = first[0].shape[0]
    for i, value in enumerate(first):
        first_out[i * width : (i + 1) * width] = value
    second_out[...] = second
    node_out[...] = node_grad


def backward_last_kernel(*refs):
    n = WAYS
    sources, targets, args, refs = split_refs(refs)
    state_0, forcing_0, edges_0, to_src_0, to_dst_0, first_0, second_0, node_0 = refs[:8]
    state_own, forcing_own, edges, kept_a, core_a, kept_b, core_b, target_kept, target_sent = refs[8:17]
    first_held, second_held, node_grad_held, node_held = refs[17:]
    state_1, forcing_1, edges_1, to_src_1, to_dst_1, first, second, node_grad = backward(
        1, sources, targets, *args, node_held
    )
    state_own[0], state_own[1] = state_0[...], state_1
    forcing_own[0], forcing_own[1] = forcing_0[...], forcing_1
    edges[0], edges[1] = edges_0[...], edges_1
    width = first[0].shape[0]
    for i, value in enumerate(first):
        first_held[i * width : (i + 1) * width] = first_0[i * width : (i + 1) * width] + value
    second_held[...] = second_0[...] + second
    node_grad_held[...] = node_0[...] + node_grad
    part, block, small = first_held.shape[0] // n, second_held.shape[0] // n, node_grad_held.shape[0] // n
    wide = node_grad_held.shape[1]
    for k in range(n):
        other = lax.axis_index("dst") ^ k
        into = core_a if k % 2 else kept_a
        start = (k // 2) * part
        into[start : start + part] = first_held[pl.ds(pl.multiple_of(other * part, part), part)].astype(into.dtype)
        into = core_b if k % 2 else kept_b
        start = (k // 2) * (into.shape[0] // 2)
        for j in range(2):
            lanes = slice(j * wide, (j + 1) * wide)
            size = block // 2
            spot = pl.ds(pl.multiple_of(other * block + j * size, size), size)
            into[start : start + size, lanes] = second_held[spot].astype(into.dtype)
            tiny = small // 2
            spot = pl.ds(pl.multiple_of(other * small + j * tiny, tiny), tiny)
            into[start + size : start + size + tiny, lanes] = node_grad_held[spot].astype(into.dtype)
        start += block // 2 + small // 2
        put_nodes(into, start, k, (to_src_0[...], to_src_1))
    put_nodes(target_kept, 0, 2, (to_dst_0[...], to_dst_1))
    for i, k in enumerate((1, 3)):
        put_nodes(target_sent, i * target_kept.shape[0], k, (to_dst_0[...], to_dst_1))


def put_nodes(into, start, k, values):
    width = values[0].shape[1]
    rows = values[0].shape[0] // WAYS
    half = rows // 2
    for moment, value in enumerate(values):
        for j in range(2):
            lanes = slice((moment * 2 + j) * width, (moment * 2 + j + 1) * width)
            spot = slice(k * rows + j * half, k * rows + (j + 1) * half)
            into[start : start + half, lanes] = value[spot].astype(into.dtype)


def add_nodes(state, base, value):
    width, half = state.shape[2], value.shape[0]
    for moment in range(T_STEPS):
        for j in range(2):
            lanes = slice((moment * 2 + j) * width, (moment * 2 + j + 1) * width)
            spot = slice(j * half, (j + 1) * half)
            state[moment, spot] = base[moment, spot] + value[:, lanes]


def near_kernel(kept, arrived, own, across):
    wide = own.shape[0]
    own[...] = kept[:wide] + arrived[:wide].astype(F32)
    across[...] = (kept[wide:] + arrived[wide:].astype(F32)).astype(BF)


def add_kernel(mine, arrived, own, sent):
    total = mine[...] + arrived[...].astype(F32)
    own[...] = total
    sent[...] = total.astype(BF)


def last_add_kernel(mine, arrived, sent):
    sent[...] = (mine[...] + arrived[...].astype(F32)).astype(BF)


def middle_kernel(mine, arrived, state_own, target_sent, state, own, sent):
    total = mine[...] + arrived[...].astype(F32)
    core = own.shape[0]
    own[...] = total[:core]
    sent[:core] = total[:core].astype(BF)
    sent[core:] = target_sent[...]
    add_nodes(state, state_own, total[core:])


def second_sum_kernel(mine, arrived, target_kept, state_in, state, own, sent):
    size, half = own.shape[0], target_kept.shape[0]
    core = mine.shape[0]
    tiny = core - size
    total = mine[:size] + arrived[:size].astype(F32)
    own[...] = total
    sent[:size] = total.astype(BF)
    sent[size:core] = mine[size:].astype(BF)
    sent[core : core + tiny] = arrived[size:core]
    add_nodes(state, state_in, arrived[core : core + half].astype(F32))
    sent[core + tiny :] = (target_kept[...] + arrived[core + half :].astype(F32)).astype(BF)


def gather_kernel(mine, sent, arrived, state_in, state, share):
    size, half = mine.shape[0], state.shape[1] // 2
    tiny = (share.shape[0] - size) // WAYS
    share[:size] = (mine[...] + arrived[:size].astype(F32)).astype(BF)
    add_nodes(state, state_in, arrived[size + 2 * tiny :].astype(F32))
    for k in range(WAYS):
        start = pl.multiple_of(size + (lax.axis_index("src") ^ k) * tiny, tiny)
        spot = slice(size + (k % 2) * tiny, size + (k % 2 + 1) * tiny)
        share[pl.ds(start, tiny)] = (arrived if k // 2 else sent)[spot]


def put_shares(places, shares_a, shares_b, outs, scratch):
    first, second, node = outs
    first_held, second_held, node_held, sems = scratch
    n = WAYS
    part, block = first.shape[0] // n, second.shape[0] // n
    small = node.shape[0] // n // n
    size, tiny, wide = block // 2, small // 2, second.shape[1]
    copies = []

    def put(source, target):
        copies.append(pltpu.make_async_copy(source, target, sems.at[len(copies)]))
        copies[-1].start()

    for i, k in enumerate(places):
        other = lax.axis_index("dst") ^ k
        first_held[i] = shares_a[i][...].astype(F32)
        put(first_held.at[i], first.at[pl.ds(pl.multiple_of(other * part, part), part)])
        for h in range(2):
            lanes = slice(h * wide, (h + 1) * wide)
            second_held[i, h * size : (h + 1) * size] = shares_b[i][:size, lanes].astype(F32)
            for j in range(n):
                spot = slice(size + j * tiny, size + (j + 1) * tiny)
                node_held[i, j, h * tiny : (h + 1) * tiny] = shares_b[i][spot, lanes].astype(F32)
        put(second_held.at[i], second.at[pl.ds(pl.multiple_of(other * block, block), block)])
        for j in range(n):
            start = pl.multiple_of(j * block + other * small, small)
            put(node_held.at[i, j], node.at[pl.ds(start, small)])
    for copy in copies:
        copy.wait()


def first_shares_kernel(own_a, near_a, own_b, near_b, *refs):
    put_shares((0, 1), (own_a, near_a), (own_b, near_b), refs[:3], refs[3:])


def last_shares_kernel(across_a, far_a, across_b, far_b, *refs):
    put_shares((2, 3), (across_a, far_a), (across_b, far_b), refs[3:6], refs[6:])


def call(kernel, outs, scratch, args, spaces=None, out_spaces=None, aliases=None):
    return pl.pallas_call(
        kernel,
        out_shape=[jax.ShapeDtypeStruct(shape, dtype) for shape, dtype in outs],
        in_specs=[pl.BlockSpec(memory_space=space) for space in spaces or [pltpu.VMEM] * len(args)],
        out_specs=[pl.BlockSpec(memory_space=space) for space in out_spaces or [pltpu.VMEM] * len(outs)],
        scratch_shapes=[
            pltpu.VMEM(*entry) if isinstance(entry, tuple) else entry for entry in scratch
        ],
        input_output_aliases=aliases or {},
        compiler_params=pltpu.CompilerParams(vmem_limit_bytes=32 << 20),
    )(*args)


def in_hbm(value):
    return pltpu.with_memory_space_constraint(value, pltpu.HBM)


def swap(value, axis, k):
    return lax.ppermute(value, axis, [(i, i ^ k) for i in range(WAYS)])


def local(
    node_state,
    forcing,
    edge_attr,
    src_index,
    dst_index,
    edge_count,
    cotangent,
    edge_w1,
    edge_w2,
    node_w1,
):
    rows, width = node_state.shape[1:]
    hid, width_m = edge_w2.shape
    width_in, width_out = node_w1.shape
    slots = edge_attr.shape[3]
    nodes = rows * WAYS
    steps = T_STEPS
    attr = edge_attr[:, 0, 0]
    joined = call(
        join_kernel,
        [((steps, rows, 2 * width + width_out), BF)],
        [pltpu.SemaphoreType.DMA((3,))],
        [in_hbm(value) for value in (node_state, forcing, cotangent)],
        [pltpu.HBM] * 3,
    )[0]
    targets = {k: swap(joined, "src", k) for k in ORDER}
    targets = [joined] + [targets[k] for k in range(1, WAYS)]
    sources = [joined] + [swap(node_state, "dst", k) for k in range(1, WAYS)]
    given = (src_index[0], dst_index[0], attr, edge_w1, edge_w2, node_w1)
    attr, w1, w2, wn, src_t, dst_t, base = call(
        stage_kernel,
        [(value.shape, value.dtype) for value in given[2:]]
        + [((nodes, slots), BF), ((nodes, slots), BF), ((steps, slots, hid), F32)],
        [((1, slots), jnp.int32), ((1, slots), jnp.int32), pltpu.SemaphoreType.DMA((len(given),))],
        [edge_count, *(in_hbm(value) for value in given)],
        [pltpu.SMEM] + [pltpu.HBM] * len(given),
    )
    forward, sums = [], []
    for moment in range(steps):
        forward.append(
            call(
                functools.partial(forward_kernel, moment),
                [((nodes, width_m), BF), ((nodes, width_m), F32), ((slots, hid), F32), ((nodes, hid), BF)],
                [],
                [*sources, *targets, base, src_t, dst_t, w1, w2],
            )
        )
    for message, own, _, _ in forward:
        total, sent = call(
            first_sum_kernel,
            [((nodes, width_m), F32), ((nodes, width_m), BF)],
            [],
            [own, swap(message, "src", 1)],
        )
        sums.append([total, swap(sent, "src", 2)])
    args = [
        [*sources, *targets, *sums[moment], attr, src_t, dst_t, *forward[moment][2:], w1, w2, wn]
        for moment in range(steps)
    ]
    block = width_in // WAYS
    earlier = call(
        backward_first_kernel,
        [
            ((rows, width), F32),
            ((rows, width), F32),
            ((slots, width), F32),
            ((nodes, width), F32),
            ((nodes, width), F32),
            (edge_w1.shape, F32),
            (edge_w2.shape, F32),
            ((block, width_out), F32),
        ],
        [((nodes, width_in), BF)],
        args[0],
    )
    part, size, tiny, half = edge_w1.shape[0] // WAYS, hid // WAYS // 2, block // WAYS // 2, rows // 2
    core = size + tiny
    wide = core + half
    state_own, grad_forcing, edges, kept_a, core_a, kept_b, core_b, target_kept, target_sent = call(
        backward_last_kernel,
        [
            ((steps, rows, width), F32),
            ((steps, rows, width), F32),
            ((steps, slots, width), F32),
            ((2 * part, hid), F32),
            ((2 * part, hid), BF),
            ((2 * wide, hid), F32),
            ((2 * wide, hid), BF),
            ((half, hid), F32),
            ((2 * half, hid), BF),
        ],
        [(edge_w1.shape, F32), (edge_w2.shape, F32), ((block, width_out), F32), ((nodes, width_in), BF)],
        [*args[1], *earlier],
    )

    def pair(size):
        return [((size, hid), F32), ((size, hid), BF)]

    state = ((steps, rows, width), F32)
    mine_a, across_a = call(near_kernel, pair(part), [], [kept_a, swap(core_a, "dst", 1)])
    mine_b, across_b = call(near_kernel, pair(wide), [], [kept_b, swap(core_b, "dst", 1)])
    own_a, sent_a = call(add_kernel, pair(part), [], [mine_a, swap(across_a, "dst", 2)])
    state_sum, own_b, sent_b = call(
        middle_kernel,
        [state, ((core, hid), F32), ((core + 2 * half, hid), BF)],
        [],
        [mine_b, swap(across_b, "dst", 2), state_own, target_sent],
    )
    own_a, sent_a = call(add_kernel, pair(part), [], [own_a, swap(sent_a, "src", 1)])
    state_sum, own_b, sent_b = call(
        second_sum_kernel,
        [state, ((size, hid), F32), ((core + tiny + half, hid), BF)],
        [],
        [own_b, swap(sent_b, "src", 1), target_kept, state_sum],
    )
    share_a = call(last_add_kernel, [((part, hid), BF)], [], [own_a, swap(sent_a, "src", 2)])[0]
    grad_state, share_b = call(
        gather_kernel,
        [state, ((size + WAYS * tiny, hid), BF)],
        [],
        [own_b, sent_b, swap(sent_b, "src", 2), state_sum],
    )
    outs = [(edge_w1.shape, F32), (edge_w2.shape, F32), (node_w1.shape, F32)]
    held = [
        ((2, part, hid), F32),
        ((2, block, width_out), F32),
        ((2, WAYS, 2 * tiny, width_out), F32),
        pltpu.SemaphoreType.DMA((2 * (2 + WAYS),)),
    ]
    shares = [share_a, share_b]
    across = [swap(share, "dst", 2) for share in shares]
    near = [swap(share, "dst", 1) for share in shares]
    grads = call(
        first_shares_kernel,
        outs,
        held,
        [share_a, near[0], share_b, near[1]],
        out_spaces=[pltpu.HBM] * 3,
    )
    far = [swap(share, "dst", 1) for share in across]
    grad_first, grad_second, grad_node = call(
        last_shares_kernel,
        outs,
        held,
        [across[0], far[0], across[1], far[1], *grads],
        [pltpu.VMEM] * 4 + [pltpu.HBM] * 3,
        [pltpu.HBM] * 3,
        {4: 0, 5: 1, 6: 2},
    )
    return grad_state, grad_forcing, edges[:, None, None], grad_first, grad_second, grad_node


def silu_slope(value):
    sigma = jax.nn.sigmoid(value)
    return sigma * (1.0 + value * (1.0 - sigma))


def local_any(
    node_state,
    forcing,
    edge_attr,
    src_index,
    dst_index,
    edge_count,
    cotangent,
    edge_w1,
    edge_w2,
    node_w1,
):
    node_rows = node_state.shape[1]
    width_x = node_state.shape[2]
    width_m = edge_w2.shape[1]
    src_rows = node_rows * lax.axis_size("dst")
    dst_rows = node_rows * lax.axis_size("src")
    sources = lax.all_gather(node_state, "dst", axis=1, tiled=True)
    targets, forcing_block, cotangent_block = (
        lax.all_gather(node_state, "src", axis=1, tiled=True),
        lax.all_gather(forcing, "src", axis=1, tiled=True),
        lax.all_gather(cotangent, "src", axis=1, tiled=True),
    )
    src_local = src_index[0, 0]
    dst_local = dst_index[0, 0]
    alive = lax.iota(jnp.int32, src_local.shape[0]) < edge_count[0, 0]
    alive_float = alive.astype(jnp.float32)[:, None]
    alive_half = alive.astype(jnp.bfloat16)[:, None]
    own_start = lax.axis_index("src") * node_rows
    grad_first = jnp.zeros(edge_w1.shape, jnp.float32)
    grad_second = jnp.zeros(edge_w2.shape, jnp.float32)
    grad_node = jnp.zeros(node_w1.shape, jnp.float32)
    state_out, forcing_out, edge_out = ([], [], [])
    for moment in range(T_STEPS):
        edge_in = jnp.concatenate(
            [sources[moment][src_local], targets[moment][dst_local], edge_attr[moment, 0, 0]],
            axis=1,
        )
        pre_edge = jnp.dot(edge_in, edge_w1, preferred_element_type=jnp.float32)
        hidden = jax.nn.silu(pre_edge).astype(jnp.bfloat16)
        message = jnp.dot(hidden, edge_w2, preferred_element_type=jnp.float32) * alive_float
        partial_value = jax.ops.segment_sum(message, dst_local, num_segments=dst_rows)
        agg_block = lax.psum(partial_value, "src")
        node_in = jnp.concatenate(
            [targets[moment], agg_block.astype(jnp.bfloat16), forcing_block[moment]], axis=1
        )
        pre_node = jnp.dot(node_in, node_w1, preferred_element_type=jnp.float32)
        grad_pre_node = (cotangent_block[moment].astype(jnp.float32) * silu_slope(pre_node)).astype(
            jnp.bfloat16
        )
        grad_node_in = jnp.dot(grad_pre_node, node_w1.T, preferred_element_type=jnp.float32)
        own_in = lax.dynamic_slice_in_dim(node_in, own_start, node_rows, 0)
        own_pre = lax.dynamic_slice_in_dim(grad_pre_node, own_start, node_rows, 0)
        grad_node = grad_node + jnp.dot(own_in.T, own_pre, preferred_element_type=jnp.float32)
        own_grad = lax.dynamic_slice_in_dim(grad_node_in, own_start, node_rows, 0)
        grad_agg = grad_node_in[:, width_x : width_x + width_m].astype(jnp.bfloat16)
        grad_message = grad_agg[dst_local] * alive_half
        grad_second = grad_second + jnp.dot(
            hidden.T, grad_message, preferred_element_type=jnp.float32
        )
        grad_hidden = jnp.dot(grad_message, edge_w2.T, preferred_element_type=jnp.float32)
        grad_pre_edge = (grad_hidden * silu_slope(pre_edge)).astype(jnp.bfloat16)
        grad_first = grad_first + jnp.dot(
            edge_in.T, grad_pre_edge, preferred_element_type=jnp.float32
        )
        grad_edge_in = jnp.dot(grad_pre_edge, edge_w1.T, preferred_element_type=jnp.float32)
        source_part = jax.ops.segment_sum(
            grad_edge_in[:, :width_x], src_local, num_segments=src_rows
        )
        target_part = jax.ops.segment_sum(
            grad_edge_in[:, width_x : 2 * width_x], dst_local, num_segments=dst_rows
        )
        from_sources = lax.psum_scatter(source_part, "dst", scatter_dimension=0, tiled=True)
        from_targets = lax.psum_scatter(target_part, "src", scatter_dimension=0, tiled=True)
        state_out.append(own_grad[:, :width_x] + from_sources + from_targets)
        forcing_out.append(own_grad[:, width_x + width_m :])
        edge_out.append(grad_edge_in[:, 2 * width_x :])
    grad_first, grad_second, grad_node = lax.psum(
        (grad_first, grad_second, grad_node), ("src", "dst")
    )
    return (
        jnp.stack(state_out),
        jnp.stack(forcing_out),
        jnp.stack(edge_out)[:, None, None],
        grad_first,
        grad_second,
        grad_node,
    )


def solution(mesh):
    in_specs = (
        P(None, ("groups", "src", "dst"), None),
        P(None, ("groups", "src", "dst"), None),
        P(None, ("groups", "src"), "dst", None, None),
        P(("groups", "src"), "dst", None),
        P(("groups", "src"), "dst", None),
        P(("groups", "src"), "dst"),
        P(None, ("groups", "src", "dst"), None),
        P(),
        P(),
        P(),
    )
    out_specs = (
        P(None, ("groups", "src", "dst"), None),
        P(None, ("groups", "src", "dst"), None),
        P(None, ("groups", "src"), "dst", None, None),
        P("groups", None),
        P("groups", None),
        P("groups", None),
    )
    square = mesh.shape["src"] == WAYS and mesh.shape["dst"] == WAYS
    body = local if square else local_any
    return jax.shard_map(body, mesh=mesh, in_specs=in_specs, out_specs=out_specs, check_vma=False)
```

```python
import functools

import jax
import jax.numpy as jnp
from jax import lax
from jax.experimental import pallas as pl
from jax.experimental.pallas import tpu as pltpu
from jax.sharding import PartitionSpec as P

T_STEPS = 2
WAYS = 4
ORDER = (3, 1, 2)
BF = jnp.bfloat16
F32 = jnp.float32


def sigmoid(value):
    return 0.5 * jnp.tanh(0.5 * value) + 0.5


def slope_of(value):
    sigma = sigmoid(value)
    return sigma * (1.0 + value * (1.0 - sigma))


def mm(a, b):
    return jnp.dot(a, b, preferred_element_type=F32)


def mm_nt(a, b):
    return lax.dot_general(a, b, (((1,), (1,)), ((), ())), preferred_element_type=F32)


def mm_tn(a, b):
    return lax.dot_general(a, b, (((0,), (0,)), ((), ())), preferred_element_type=F32)


def one_hot_t(index, nodes, live=None):
    hit = lax.broadcasted_iota(jnp.int32, (nodes, index.shape[1]), 0) == index
    if live is not None:
        hit = jnp.logical_and(hit, live)
    return jnp.where(hit, 1.0, 0.0).astype(BF)


def stacked(refs, moment, width):
    return jnp.concatenate([ref[moment, :, :width] for ref in refs], axis=0)


def turned(value, k):
    rows = value.shape[0] // WAYS
    return jnp.concatenate([value[(j ^ k) * rows : ((j ^ k) + 1) * rows] for j in range(WAYS)], axis=0)


def join_kernel(state, forcing, cotangent, joined, sems):
    width = state.shape[2]
    copies = [
        pltpu.make_async_copy(state, joined.at[:, :, :width], sems.at[0]),
        pltpu.make_async_copy(forcing, joined.at[:, :, width : 2 * width], sems.at[1]),
        pltpu.make_async_copy(cotangent, joined.at[:, :, 2 * width :], sems.at[2]),
    ]
    for copy in copies:
        copy.start()
    for copy in copies:
        copy.wait()


def stage_kernel(count, src_hbm, dst_hbm, attr_hbm, w1_hbm, w2_hbm, wn_hbm, *refs):
    attr, w1, w2, wn, src_t, dst_t, base, src_held, dst_held, sems = refs
    width = attr.shape[2]
    nodes, slots = src_t.shape
    rows = nodes // WAYS
    copies = [
        pltpu.make_async_copy(source, target, sems.at[i])
        for i, (source, target) in enumerate(
            [
                (src_hbm, src_held),
                (dst_hbm, dst_held),
                (attr_hbm, attr),
                (w1_hbm, w1),
                (w2_hbm, w2),
                (wn_hbm, wn),
            ]
        )
    ]
    for copy in copies:
        copy.start()
    copies[0].wait()
    copies[1].wait()
    live = lax.broadcasted_iota(jnp.int32, (1, slots), 1) < count[0, 0]
    src_t[...] = one_hot_t(src_held[...] ^ (lax.axis_index("dst") * rows), nodes)
    dst_t[...] = one_hot_t(dst_held[...] ^ (lax.axis_index("src") * rows), nodes, live)
    copies[2].wait()
    copies[3].wait()
    for moment in range(T_STEPS):
        base[moment] = mm(attr[moment], w1[2 * width :])
    for copy in copies[4:]:
        copy.wait()


def forward_kernel(moment, *refs):
    n = WAYS
    sources, targets, refs = refs[:n], refs[n : 2 * n], refs[2 * n :]
    base, src_t, dst_t, w1, w2, message, own, slope, sums = refs
    width = sources[1].shape[2]
    ends = jnp.concatenate(
        [
            mm_tn(src_t[...], stacked(sources, moment, width)).astype(BF),
            mm_tn(dst_t[...], stacked(targets, moment, width)).astype(BF),
        ],
        axis=1,
    )
    pre = base[moment] + mm(ends, w1[: 2 * width])
    sigma = sigmoid(pre)
    hidden = (pre * sigma).astype(BF)
    slope[...] = sigma * (1.0 + pre * (1.0 - sigma))
    total = mm(dst_t[...], hidden)
    high = total.astype(BF)
    low = (total - high.astype(F32)).astype(BF)
    sums[...] = high
    product = mm(high, w2[...]) + mm(low, w2[...])
    own[...] = product
    message[...] = product.astype(BF)


def first_sum_kernel(own, arrived, total, sent):
    value = own[...] + turned(arrived[...].astype(F32), 1)
    total[...] = value
    sent[...] = value.astype(BF)


def backward(moment, put_edges, sources, targets, total, arrived, attr, src_t, dst_t, slope, sums, w1, w2, wn):
    rows, width = sources[1].shape[1:]
    width_m = w2.shape[1]
    joined = stacked(targets, moment, targets[0].shape[2])
    state, forcing, cotangent = joined[:, :width], joined[:, width : 2 * width], joined[:, 2 * width :]
    agg = total[...] + turned(arrived[...].astype(F32), 2)
    node_in = jnp.concatenate([state, agg.astype(BF), forcing], axis=1)
    grad_pre = (cotangent.astype(F32) * slope_of(mm(node_in, wn[...]))).astype(BF)
    grad_in = mm_nt(grad_pre, wn[...])
    grad_agg = grad_in[:, width : width + width_m].astype(BF)
    grad_message = mm_tn(dst_t[...], grad_agg).astype(BF)
    grad_pre_edge = (mm_nt(grad_message, w2[...]) * slope[...]).astype(BF)
    put_edges(mm_nt(grad_pre_edge, w1[2 * width :]), grad_in[:rows, width + width_m :])
    from_src = mm(src_t[...], grad_pre_edge).astype(BF)
    from_dst = mm(dst_t[...], grad_pre_edge).astype(BF)
    to_src = mm_nt(from_src, w1[:width])
    to_dst = mm_nt(from_dst, w1[width : 2 * width])
    first = [
        mm_tn(stacked(sources, moment, width), from_src),
        mm_tn(state, from_dst),
        mm_tn(attr[moment], grad_pre_edge),
    ]
    second = mm_tn(sums[...], grad_agg)
    node_grad = mm_tn(node_in, grad_pre)
    state_own = grad_in[:rows, :width] + to_dst[:rows]
    return state_own, to_src, to_dst, first, second, node_grad


def split_refs(refs):
    n = WAYS
    return refs[:n], refs[n : 2 * n], refs[2 * n : 2 * n + 10], refs[2 * n + 10 :]


def backward_first_kernel(*refs):
    sources, targets, args, refs = split_refs(refs)
    state, forcing, edges, to_src, to_dst, first_out, second_out, node_out = refs

    def put_edges(edge_values, forcing_values):
        edges[...] = edge_values
        forcing[...] = forcing_values

    state[...], to_src[...], to_dst[...], first, second, node_grad = backward(0, put_edges, sources, targets, *args)
    width = first[0].shape[0]
    for i, value in enumerate(first):
        first_out[i * width : (i + 1) * width] = value
    second_out[...] = second
    node_out[...] = node_grad


def backward_last_kernel(*refs):
    n = WAYS
    sources, targets, args, refs = split_refs(refs)
    state_0, forcing_0, edges_0, to_src_0, to_dst_0, first_0, second_0, node_0 = refs[:8]
    state_own, forcing_own, edges, kept_a, core_a, kept_b, core_b, target_kept, target_sent = refs[8:17]
    first_held, second_held, node_grad_held, edges_1, forcing_1, sems = refs[17:]
    copies = [
        pltpu.make_async_copy(source, target, sems.at[i])
        for i, (source, target) in enumerate(
            [(edges_0, edges.at[0]), (forcing_0, forcing_own.at[0]), (edges_1, edges.at[1]), (forcing_1, forcing_own.at[1])]
        )
    ]
    copies[0].start()
    copies[1].start()

    def put_edges(edge_values, forcing_values):
        edges_1[...] = edge_values
        forcing_1[...] = forcing_values
        copies[2].start()
        copies[3].start()

    state_1, to_src_1, to_dst_1, first, second, node_grad = backward(1, put_edges, sources, targets, *args)
    state_own[0], state_own[1] = state_0[...], state_1
    width = first[0].shape[0]
    for i, value in enumerate(first):
        first_held[i * width : (i + 1) * width] = first_0[i * width : (i + 1) * width] + value
    second_held[...] = second_0[...] + second
    node_grad_held[...] = node_0[...] + node_grad
    part, block = first_held.shape[0] // n, second_held.shape[0] // n
    size, wide = block // 2, second_held.shape[1]
    for k in range(n):
        other = lax.axis_index("dst") ^ k
        into = core_a if k % 2 else kept_a
        start = (k // 2) * part
        into[start : start + part] = first_held[pl.ds(pl.multiple_of(other * part, part), part)].astype(into.dtype)
        into = core_b if k % 2 else kept_b
        start = (k // 2) * (into.shape[0] // 2)
        for held in (second_held, node_grad_held):
            for j in range(2):
                spot = pl.ds(pl.multiple_of(other * block + j * size, size), size)
                into[start : start + size, j * wide : (j + 1) * wide] = held[spot].astype(into.dtype)
            start += size
        put_nodes(into, start, k, (to_src_0[...], to_src_1))
    put_nodes(target_kept, 0, 2, (to_dst_0[...], to_dst_1))
    for i, k in enumerate((1, 3)):
        put_nodes(target_sent, i * target_kept.shape[0], k, (to_dst_0[...], to_dst_1))
    for copy in copies:
        copy.wait()


def put_nodes(into, start, k, values):
    width = values[0].shape[1]
    rows = values[0].shape[0] // WAYS
    half = rows // 2
    for moment, value in enumerate(values):
        for j in range(2):
            lanes = slice((moment * 2 + j) * width, (moment * 2 + j + 1) * width)
            spot = slice(k * rows + j * half, k * rows + (j + 1) * half)
            into[start : start + half, lanes] = value[spot].astype(into.dtype)


def add_nodes(state, base, value):
    width, half = state.shape[2], value.shape[0]
    for moment in range(T_STEPS):
        for j in range(2):
            lanes = slice((moment * 2 + j) * width, (moment * 2 + j + 1) * width)
            spot = slice(j * half, (j + 1) * half)
            state[moment, spot] = base[moment, spot] + value[:, lanes]


def near_kernel(kept, arrived, own, across):
    wide = own.shape[0]
    own[...] = kept[:wide] + arrived[:wide].astype(F32)
    across[...] = (kept[wide:] + arrived[wide:].astype(F32)).astype(BF)


def add_kernel(mine, arrived, own, sent):
    total = mine[...] + arrived[...].astype(F32)
    own[...] = total
    sent[...] = total.astype(BF)


def last_add_kernel(mine, arrived, sent):
    sent[...] = (mine[...] + arrived[...].astype(F32)).astype(BF)


def middle_kernel(mine, arrived, state_own, target_sent, state, own, sent, node_share):
    total = mine[...] + arrived[...].astype(F32)
    size = own.shape[0]
    own[...] = total[:size]
    sent[:size] = total[:size].astype(BF)
    sent[size:] = target_sent[...]
    node_share[...] = total[size : 2 * size].astype(BF)
    add_nodes(state, state_own, total[2 * size :])


def second_sum_kernel(mine, arrived, target_kept, state_in, state, own, sent):
    size, half = own.shape[0], target_kept.shape[0]
    total = mine[...] + arrived[:size].astype(F32)
    own[...] = total
    sent[:size] = total.astype(BF)
    add_nodes(state, state_in, arrived[size : size + half].astype(F32))
    sent[size:] = (target_kept[...] + arrived[size + half :].astype(F32)).astype(BF)


def gather_kernel(mine, arrived, node_across, share, node_sent):
    share[...] = (mine[...] + arrived[: mine.shape[0]].astype(F32)).astype(BF)
    node_sent[...] = node_across[...]


def put_shares(places, shares, outs, scratch):
    *held, sems = scratch
    copies = []

    def put(source, target):
        copies.append(pltpu.make_async_copy(source, target, sems.at[len(copies)]))
        copies[-1].start()

    for i, k in enumerate(places):
        other = lax.axis_index("dst") ^ k
        for out, into, share in zip(outs, held, shares[i], strict=True):
            rows, wide = into.shape[1:]
            size = share.shape[0]
            for h in range(rows // size):
                into[i, h * size : (h + 1) * size] = share[:, h * wide : (h + 1) * wide].astype(F32)
            put(into.at[i], out.at[pl.ds(pl.multiple_of(other * rows, rows), rows)])
    return copies


def first_shares_kernel(*refs):
    copies = put_shares((0, 1), (refs[:3], refs[3:6]), refs[6:9], refs[9:])
    for copy in copies:
        copy.wait()


def last_shares_kernel(state_in, arrived, *refs):
    state_held, state_sem = refs[17:]
    copies = put_shares((2, 3), (refs[:3], refs[3:6]), refs[10:13], refs[13:17])
    add_nodes(state_held, state_in, arrived[arrived.shape[0] - state_in.shape[1] // 2 :].astype(F32))
    copies.append(pltpu.make_async_copy(state_held, refs[9], state_sem))
    copies[-1].start()
    for copy in copies:
        copy.wait()


def call(kernel, outs, scratch, args, spaces=None, out_spaces=None, aliases=None):
    return pl.pallas_call(
        kernel,
        out_shape=[jax.ShapeDtypeStruct(shape, dtype) for shape, dtype in outs],
        in_specs=[pl.BlockSpec(memory_space=space) for space in spaces or [pltpu.VMEM] * len(args)],
        out_specs=[pl.BlockSpec(memory_space=space) for space in out_spaces or [pltpu.VMEM] * len(outs)],
        scratch_shapes=[
            pltpu.VMEM(*entry) if isinstance(entry, tuple) else entry for entry in scratch
        ],
        input_output_aliases=aliases or {},
        compiler_params=pltpu.CompilerParams(vmem_limit_bytes=32 << 20),
    )(*args)


def in_hbm(value):
    return pltpu.with_memory_space_constraint(value, pltpu.HBM)


def swap(value, axis, k):
    return lax.ppermute(value, axis, [(i, i ^ k) for i in range(WAYS)])


def local(
    node_state,
    forcing,
    edge_attr,
    src_index,
    dst_index,
    edge_count,
    cotangent,
    edge_w1,
    edge_w2,
    node_w1,
):
    rows, width = node_state.shape[1:]
    hid, width_m = edge_w2.shape
    width_out = node_w1.shape[1]
    slots = edge_attr.shape[3]
    nodes = rows * WAYS
    steps = T_STEPS
    attr = edge_attr[:, 0, 0]
    joined = call(
        join_kernel,
        [((steps, rows, 2 * width + width_out), BF)],
        [pltpu.SemaphoreType.DMA((3,))],
        [in_hbm(value) for value in (node_state, forcing, cotangent)],
        [pltpu.HBM] * 3,
    )[0]
    targets = {k: swap(joined, "src", k) for k in ORDER}
    targets = [joined] + [targets[k] for k in range(1, WAYS)]
    sources = [joined] + [swap(node_state, "dst", k) for k in range(1, WAYS)]
    given = (src_index[0], dst_index[0], attr, edge_w1, edge_w2, node_w1)
    attr, w1, w2, wn, src_t, dst_t, base = call(
        stage_kernel,
        [(value.shape, value.dtype) for value in given[2:]]
        + [((nodes, slots), BF), ((nodes, slots), BF), ((steps, slots, hid), F32)],
        [((1, slots), jnp.int32), ((1, slots), jnp.int32), pltpu.SemaphoreType.DMA((len(given),))],
        [edge_count, *(in_hbm(value) for value in given)],
        [pltpu.SMEM] + [pltpu.HBM] * len(given),
    )
    forward, sums = [], []
    for moment in range(steps):
        forward.append(
            call(
                functools.partial(forward_kernel, moment),
                [((nodes, width_m), BF), ((nodes, width_m), F32), ((slots, hid), F32), ((nodes, hid), BF)],
                [],
                [*sources, *targets, base, src_t, dst_t, w1, w2],
            )
        )
    for message, own, _, _ in forward:
        total, sent = call(
            first_sum_kernel,
            [((nodes, width_m), F32), ((nodes, width_m), BF)],
            [],
            [own, swap(message, "src", 1)],
        )
        sums.append([total, swap(sent, "src", 2)])
    args = [
        [*sources, *targets, *sums[moment], attr, src_t, dst_t, *forward[moment][2:], w1, w2, wn]
        for moment in range(steps)
    ]
    earlier = call(
        backward_first_kernel,
        [
            ((rows, width), F32),
            ((rows, width), F32),
            ((slots, width), F32),
            ((nodes, width), F32),
            ((nodes, width), F32),
            (edge_w1.shape, F32),
            (edge_w2.shape, F32),
            (node_w1.shape, F32),
        ],
        [],
        args[0],
    )
    part, block, half = edge_w1.shape[0] // WAYS, hid // WAYS, rows // 2
    size = block // 2
    wide = 2 * size + half
    state_own, grad_forcing, edges, kept_a, core_a, kept_b, core_b, target_kept, target_sent = call(
        backward_last_kernel,
        [
            ((steps, rows, width), F32),
            ((steps, rows, width), F32),
            ((steps, slots, width), F32),
            ((2 * part, hid), F32),
            ((2 * part, hid), BF),
            ((2 * wide, hid), F32),
            ((2 * wide, hid), BF),
            ((half, hid), F32),
            ((2 * half, hid), BF),
        ],
        [
            (edge_w1.shape, F32),
            (edge_w2.shape, F32),
            (node_w1.shape, F32),
            ((slots, width), F32),
            ((rows, width), F32),
            pltpu.SemaphoreType.DMA((4,)),
        ],
        [*args[1], *earlier],
        out_spaces=[pltpu.VMEM] + [pltpu.HBM] * 2 + [pltpu.VMEM] * 6,
    )

    def pair(size):
        return [((size, hid), F32), ((size, hid), BF)]

    state = ((steps, rows, width), F32)
    mine_a, across_a = call(near_kernel, pair(part), [], [kept_a, swap(core_a, "dst", 1)])
    mine_b, across_b = call(near_kernel, pair(wide), [], [kept_b, swap(core_b, "dst", 1)])
    own_a, sent_a = call(add_kernel, pair(part), [], [mine_a, swap(across_a, "dst", 2)])
    state_sum, own_b, sent_b, node_share = call(
        middle_kernel,
        [state, ((size, hid), F32), ((size + 2 * half, hid), BF), ((size, hid), BF)],
        [],
        [mine_b, swap(across_b, "dst", 2), state_own, target_sent],
    )
    node_across = swap(node_share, "dst", 2)
    own_a, sent_a = call(add_kernel, pair(part), [], [own_a, swap(sent_a, "src", 1)])
    state_sum, own_b, sent_b = call(
        second_sum_kernel,
        [state, ((size, hid), F32), ((size + half, hid), BF)],
        [],
        [own_b, swap(sent_b, "src", 1), target_kept, state_sum],
    )
    share_a = call(last_add_kernel, [((part, hid), BF)], [], [own_a, swap(sent_a, "src", 2)])[0]
    arrived = swap(sent_b, "src", 2)
    share_b, node_across = call(gather_kernel, [((size, hid), BF)] * 2, [], [own_b, arrived, node_across])
    own = [share_a, share_b, node_share]
    across = [swap(share_a, "dst", 2), swap(share_b, "dst", 2), node_across]
    outs = [(edge_w1.shape, F32), (edge_w2.shape, F32), (node_w1.shape, F32)]
    held = [((2, value.shape[0] // WAYS, value.shape[1]), F32) for value in (edge_w1, edge_w2, node_w1)]
    held.append(pltpu.SemaphoreType.DMA((6,)))
    grads = call(
        first_shares_kernel,
        outs,
        held,
        own + [swap(share, "dst", 1) for share in own],
        out_spaces=[pltpu.HBM] * 3,
    )
    grad_state, grad_first, grad_second, grad_node = call(
        last_shares_kernel,
        [state] + outs,
        held + [state, pltpu.SemaphoreType.DMA],
        [state_sum, arrived] + across + [swap(share, "dst", 1) for share in across] + list(grads),
        [pltpu.VMEM] * 8 + [pltpu.HBM] * 3,
        [pltpu.HBM] * 4,
        {8: 1, 9: 2, 10: 3},
    )
    return grad_state, grad_forcing, edges[:, None, None], grad_first, grad_second, grad_node


def silu_slope(value):
    sigma = jax.nn.sigmoid(value)
    return sigma * (1.0 + value * (1.0 - sigma))


def local_any(
    node_state,
    forcing,
    edge_attr,
    src_index,
    dst_index,
    edge_count,
    cotangent,
    edge_w1,
    edge_w2,
    node_w1,
):
    node_rows = node_state.shape[1]
    width_x = node_state.shape[2]
    width_m = edge_w2.shape[1]
    src_rows = node_rows * lax.axis_size("dst")
    dst_rows = node_rows * lax.axis_size("src")
    sources = lax.all_gather(node_state, "dst", axis=1, tiled=True)
    targets, forcing_block, cotangent_block = (
        lax.all_gather(node_state, "src", axis=1, tiled=True),
        lax.all_gather(forcing, "src", axis=1, tiled=True),
        lax.all_gather(cotangent, "src", axis=1, tiled=True),
    )
    src_local = src_index[0, 0]
    dst_local = dst_index[0, 0]
    alive = lax.iota(jnp.int32, src_local.shape[0]) < edge_count[0, 0]
    alive_float = alive.astype(jnp.float32)[:, None]
    alive_half = alive.astype(jnp.bfloat16)[:, None]
    own_start = lax.axis_index("src") * node_rows
    grad_first = jnp.zeros(edge_w1.shape, jnp.float32)
    grad_second = jnp.zeros(edge_w2.shape, jnp.float32)
    grad_node = jnp.zeros(node_w1.shape, jnp.float32)
    state_out, forcing_out, edge_out = ([], [], [])
    for moment in range(T_STEPS):
        edge_in = jnp.concatenate(
            [sources[moment][src_local], targets[moment][dst_local], edge_attr[moment, 0, 0]],
            axis=1,
        )
        pre_edge = jnp.dot(edge_in, edge_w1, preferred_element_type=jnp.float32)
        hidden = jax.nn.silu(pre_edge).astype(jnp.bfloat16)
        message = jnp.dot(hidden, edge_w2, preferred_element_type=jnp.float32) * alive_float
        partial_value = jax.ops.segment_sum(message, dst_local, num_segments=dst_rows)
        agg_block = lax.psum(partial_value, "src")
        node_in = jnp.concatenate(
            [targets[moment], agg_block.astype(jnp.bfloat16), forcing_block[moment]], axis=1
        )
        pre_node = jnp.dot(node_in, node_w1, preferred_element_type=jnp.float32)
        grad_pre_node = (cotangent_block[moment].astype(jnp.float32) * silu_slope(pre_node)).astype(
            jnp.bfloat16
        )
        grad_node_in = jnp.dot(grad_pre_node, node_w1.T, preferred_element_type=jnp.float32)
        own_in = lax.dynamic_slice_in_dim(node_in, own_start, node_rows, 0)
        own_pre = lax.dynamic_slice_in_dim(grad_pre_node, own_start, node_rows, 0)
        grad_node = grad_node + jnp.dot(own_in.T, own_pre, preferred_element_type=jnp.float32)
        own_grad = lax.dynamic_slice_in_dim(grad_node_in, own_start, node_rows, 0)
        grad_agg = grad_node_in[:, width_x : width_x + width_m].astype(jnp.bfloat16)
        grad_message = grad_agg[dst_local] * alive_half
        grad_second = grad_second + jnp.dot(
            hidden.T, grad_message, preferred_element_type=jnp.float32
        )
        grad_hidden = jnp.dot(grad_message, edge_w2.T, preferred_element_type=jnp.float32)
        grad_pre_edge = (grad_hidden * silu_slope(pre_edge)).astype(jnp.bfloat16)
        grad_first = grad_first + jnp.dot(
            edge_in.T, grad_pre_edge, preferred_element_type=jnp.float32
        )
        grad_edge_in = jnp.dot(grad_pre_edge, edge_w1.T, preferred_element_type=jnp.float32)
        source_part = jax.ops.segment_sum(
            grad_edge_in[:, :width_x], src_local, num_segments=src_rows
        )
        target_part = jax.ops.segment_sum(
            grad_edge_in[:, width_x : 2 * width_x], dst_local, num_segments=dst_rows
        )
        from_sources = lax.psum_scatter(source_part, "dst", scatter_dimension=0, tiled=True)
        from_targets = lax.psum_scatter(target_part, "src", scatter_dimension=0, tiled=True)
        state_out.append(own_grad[:, :width_x] + from_sources + from_targets)
        forcing_out.append(own_grad[:, width_x + width_m :])
        edge_out.append(grad_edge_in[:, 2 * width_x :])
    grad_first, grad_second, grad_node = lax.psum(
        (grad_first, grad_second, grad_node), ("src", "dst")
    )
    return (
        jnp.stack(state_out),
        jnp.stack(forcing_out),
        jnp.stack(edge_out)[:, None, None],
        grad_first,
        grad_second,
        grad_node,
    )


def solution(mesh):
    in_specs = (
        P(None, ("groups", "src", "dst"), None),
        P(None, ("groups", "src", "dst"), None),
        P(None, ("groups", "src"), "dst", None, None),
        P(("groups", "src"), "dst", None),
        P(("groups", "src"), "dst", None),
        P(("groups", "src"), "dst"),
        P(None, ("groups", "src", "dst"), None),
        P(),
        P(),
        P(),
    )
    out_specs = (
        P(None, ("groups", "src", "dst"), None),
        P(None, ("groups", "src", "dst"), None),
        P(None, ("groups", "src"), "dst", None, None),
        P("groups", None),
        P("groups", None),
        P("groups", None),
    )
    square = mesh.shape["src"] == WAYS and mesh.shape["dst"] == WAYS
    body = local if square else local_any
    return jax.shard_map(body, mesh=mesh, in_specs=in_specs, out_specs=out_specs, check_vma=False)
```

```python
import functools

import jax
import jax.numpy as jnp
from jax import lax
from jax.experimental import pallas as pl
from jax.experimental.pallas import tpu as pltpu
from jax.sharding import PartitionSpec as P

T_STEPS = 2
WAYS = 4
ORDER = (3, 1, 2)
BF = jnp.bfloat16
F32 = jnp.float32


def sigmoid(value):
    return 0.5 * jnp.tanh(0.5 * value) + 0.5


def slope_of(value):
    sigma = sigmoid(value)
    return sigma * (1.0 + value * (1.0 - sigma))


def mm(a, b):
    return jnp.dot(a, b, preferred_element_type=F32)


def mm_nt(a, b):
    return lax.dot_general(a, b, (((1,), (1,)), ((), ())), preferred_element_type=F32)


def mm_tn(a, b):
    return lax.dot_general(a, b, (((0,), (0,)), ((), ())), preferred_element_type=F32)


def one_hot_t(index, nodes, live=None):
    hit = lax.broadcasted_iota(jnp.int32, (nodes, index.shape[1]), 0) == index
    if live is not None:
        hit = jnp.logical_and(hit, live)
    return jnp.where(hit, 1.0, 0.0).astype(BF)


def stacked(refs, moment, width):
    return jnp.concatenate([ref[moment, :, :width] for ref in refs], axis=0)


def turned(value, k):
    rows = value.shape[0] // WAYS
    return jnp.concatenate([value[(j ^ k) * rows : ((j ^ k) + 1) * rows] for j in range(WAYS)], axis=0)


def join_kernel(state, forcing, cotangent, joined, sems):
    width = state.shape[2]
    copies = [
        pltpu.make_async_copy(state, joined.at[:, :, :width], sems.at[0]),
        pltpu.make_async_copy(forcing, joined.at[:, :, width : 2 * width], sems.at[1]),
        pltpu.make_async_copy(cotangent, joined.at[:, :, 2 * width :], sems.at[2]),
    ]
    for copy in copies:
        copy.start()
    for copy in copies:
        copy.wait()


def stage_kernel(count, src_hbm, dst_hbm, attr_hbm, w1_hbm, w2_hbm, wn_hbm, *refs):
    attr, w1, w2, wn, src_t, dst_t, base, src_held, dst_held, sems = refs
    width = attr.shape[2]
    nodes, slots = src_t.shape
    rows = nodes // WAYS
    copies = [
        pltpu.make_async_copy(source, target, sems.at[i])
        for i, (source, target) in enumerate(
            [
                (src_hbm, src_held),
                (dst_hbm, dst_held),
                (attr_hbm, attr),
                (w1_hbm, w1),
                (w2_hbm, w2),
                (wn_hbm, wn),
            ]
        )
    ]
    for copy in copies:
        copy.start()
    copies[0].wait()
    copies[1].wait()
    live = lax.broadcasted_iota(jnp.int32, (1, slots), 1) < count[0, 0]
    src_t[...] = one_hot_t(src_held[...] ^ (lax.axis_index("dst") * rows), nodes)
    dst_t[...] = one_hot_t(dst_held[...] ^ (lax.axis_index("src") * rows), nodes, live)
    copies[2].wait()
    copies[3].wait()
    for moment in range(T_STEPS):
        base[moment] = mm(attr[moment], w1[2 * width :])
    for copy in copies[4:]:
        copy.wait()


def forward_kernel(moment, *refs):
    n = WAYS
    sources, targets, refs = refs[:n], refs[n : 2 * n], refs[2 * n :]
    base, src_t, dst_t, w1, w2, message, own, slope, sums = refs
    width = sources[1].shape[2]
    ends = jnp.concatenate(
        [
            mm_tn(src_t[...], stacked(sources, moment, width)).astype(BF),
            mm_tn(dst_t[...], stacked(targets, moment, width)).astype(BF),
        ],
        axis=1,
    )
    pre = base[moment] + mm(ends, w1[: 2 * width])
    sigma = sigmoid(pre)
    hidden = (pre * sigma).astype(BF)
    slope[...] = sigma * (1.0 + pre * (1.0 - sigma))
    total = mm(dst_t[...], hidden)
    high = total.astype(BF)
    low = (total - high.astype(F32)).astype(BF)
    sums[...] = high
    product = mm(high, w2[...]) + mm(low, w2[...])
    own[...] = product
    message[...] = product.astype(BF)


def first_sum_kernel(own, arrived, total, sent):
    value = own[...] + turned(arrived[...].astype(F32), 1)
    total[...] = value
    sent[...] = value.astype(BF)


def backward(moment, put_edges, sources, targets, total, arrived, attr, src_t, dst_t, slope, sums, w1, w2, wn):
    rows, width = sources[1].shape[1:]
    width_m = w2.shape[1]
    joined = stacked(targets, moment, targets[0].shape[2])
    state, forcing, cotangent = joined[:, :width], joined[:, width : 2 * width], joined[:, 2 * width :]
    agg = total[...] + turned(arrived[...].astype(F32), 2)
    node_in = jnp.concatenate([state, agg.astype(BF), forcing], axis=1)
    grad_pre = (cotangent.astype(F32) * slope_of(mm(node_in, wn[...]))).astype(BF)
    grad_in = mm_nt(grad_pre, wn[...])
    grad_agg = grad_in[:, width : width + width_m].astype(BF)
    grad_message = mm_tn(dst_t[...], grad_agg).astype(BF)
    grad_pre_edge = (mm_nt(grad_message, w2[...]) * slope[...]).astype(BF)
    put_edges(mm_nt(grad_pre_edge, w1[2 * width :]), grad_in[:rows, width + width_m :])
    from_src = mm(src_t[...], grad_pre_edge).astype(BF)
    from_dst = mm(dst_t[...], grad_pre_edge).astype(BF)
    to_src = mm_nt(from_src, w1[:width])
    to_dst = mm_nt(from_dst, w1[width : 2 * width])
    first = [
        mm_tn(stacked(sources, moment, width), from_src),
        mm_tn(state, from_dst),
        mm_tn(attr[moment], grad_pre_edge),
    ]
    second = mm_tn(sums[...], grad_agg)
    node_grad = mm_tn(node_in, grad_pre)
    state_own = grad_in[:rows, :width] + to_dst[:rows]
    return state_own, to_src, to_dst, first, second, node_grad


def split_refs(refs):
    n = WAYS
    return refs[:n], refs[n : 2 * n], refs[2 * n : 2 * n + 10], refs[2 * n + 10 :]


def backward_first_kernel(*refs):
    sources, targets, args, refs = split_refs(refs)
    state, forcing, edges, to_src, to_dst, first_out, second_out, node_out = refs

    def put_edges(edge_values, forcing_values):
        edges[...] = edge_values
        forcing[...] = forcing_values

    state[...], to_src[...], to_dst[...], first, second, node_grad = backward(0, put_edges, sources, targets, *args)
    width = first[0].shape[0]
    for i, value in enumerate(first):
        first_out[i * width : (i + 1) * width] = value
    second_out[...] = second
    node_out[...] = node_grad


def backward_last_kernel(*refs):
    n = WAYS
    sources, targets, args, refs = split_refs(refs)
    state_0, to_src_0, to_dst_0, first_0, second_0, node_0 = refs[:6]
    state_own, forcing, edges, first_held, second_held, node_grad_held, src_kept = refs[6:13]
    core_a, core_b, target_kept, target_sent = refs[13:]

    def put_edges(edge_values, forcing_values):
        edges[...] = edge_values
        forcing[...] = forcing_values

    state_1, to_src_1, to_dst_1, first, second, node_grad = backward(1, put_edges, sources, targets, *args)
    state_own[0], state_own[1] = state_0[...], state_1
    width = first[0].shape[0]
    for i, value in enumerate(first):
        first_held[i * width : (i + 1) * width] = first_0[i * width : (i + 1) * width] + value
    second_held[...] = second_0[...] + second
    node_grad_held[...] = node_0[...] + node_grad
    part, block = first_held.shape[0] // n, second_held.shape[0] // n
    size, wide = block // 2, second_held.shape[1]
    for i, k in enumerate((1, 3)):
        other = lax.axis_index("dst") ^ k
        core_a[i * part : (i + 1) * part] = first_held[pl.ds(pl.multiple_of(other * part, part), part)].astype(BF)
        start = i * (core_b.shape[0] // 2)
        for held in (second_held, node_grad_held):
            for j in range(2):
                spot = pl.ds(pl.multiple_of(other * block + j * size, size), size)
                core_b[start : start + size, j * wide : (j + 1) * wide] = held[spot].astype(BF)
            start += size
        put_nodes(core_b, start, k, (to_src_0[...], to_src_1))
    for i, k in enumerate((0, 2)):
        put_nodes(src_kept, i * target_kept.shape[0], k, (to_src_0[...], to_src_1))
    put_nodes(target_kept, 0, 2, (to_dst_0[...], to_dst_1))
    for i, k in enumerate((1, 3)):
        put_nodes(target_sent, i * target_kept.shape[0], k, (to_dst_0[...], to_dst_1))


def out_kernel(forcing_0, edges_0, forcing_1, edges_1, forcing, edges, token, sems):
    pairs = [(edges_0, edges.at[0]), (edges_1, edges.at[1]), (forcing_0, forcing.at[0]), (forcing_1, forcing.at[1])]
    copies = [pltpu.make_async_copy(*ends, sems.at[i]) for i, ends in enumerate(pairs)]
    for copy in copies:
        copy.start()
    token[...] = jnp.zeros_like(token)
    for copy in copies:
        copy.wait()


def put_nodes(into, start, k, values):
    width = values[0].shape[1]
    rows = values[0].shape[0] // WAYS
    half = rows // 2
    for moment, value in enumerate(values):
        for j in range(2):
            lanes = slice((moment * 2 + j) * width, (moment * 2 + j + 1) * width)
            spot = slice(k * rows + j * half, k * rows + (j + 1) * half)
            into[start : start + half, lanes] = value[spot].astype(into.dtype)


def add_nodes(state, base, value):
    width, half = state.shape[2], value.shape[0]
    for moment in range(T_STEPS):
        for j in range(2):
            lanes = slice((moment * 2 + j) * width, (moment * 2 + j + 1) * width)
            spot = slice(j * half, (j + 1) * half)
            state[moment, spot] = base[moment, spot] + value[:, lanes]


def first_near_kernel(whole, arrived, own, across):
    part = own.shape[0]
    for i, (k, into) in enumerate(((0, own), (2, across))):
        spot = pl.ds(pl.multiple_of((lax.axis_index("dst") ^ k) * part, part), part)
        into[...] = (whole[spot] + arrived[i * part : (i + 1) * part].astype(F32)).astype(into.dtype)


def second_near_kernel(second, node_grad, src_kept, arrived, own, across):
    wide = second.shape[1]
    block = second.shape[0] // WAYS
    size, half = block // 2, src_kept.shape[0] // 2
    for i, (k, into) in enumerate(((0, own), (2, across))):
        other = lax.axis_index("dst") ^ k
        start = 0
        for whole in (second, node_grad):
            for j in range(2):
                lanes = slice(j * wide, (j + 1) * wide)
                spot = pl.ds(pl.multiple_of(other * block + j * size, size), size)
                value = arrived[i * into.shape[0] + start : i * into.shape[0] + start + size, lanes]
                into[start : start + size, lanes] = (whole[spot] + value.astype(F32)).astype(into.dtype)
            start += size
        value = arrived[i * into.shape[0] + start : (i + 1) * into.shape[0]]
        into[start:] = (src_kept[i * half : (i + 1) * half] + value.astype(F32)).astype(into.dtype)


def add_kernel(mine, arrived, own, sent):
    total = mine[...] + arrived[...].astype(F32)
    own[...] = total
    sent[...] = total.astype(BF)


def second_middle_kernel(mine, arrived, target_sent, _, own, sent, node_share, nodes):
    total = mine[...] + arrived[...].astype(F32)
    size = own.shape[0]
    own[...] = total[:size]
    sent[:size] = total[:size].astype(BF)
    sent[size:] = target_sent[...]
    node_share[...] = total[size : 2 * size].astype(BF)
    nodes[...] = total[2 * size :]


def second_sum_over_src_kernel(mine, arrived, target_kept, own, sent):
    size, half = own.shape[0], target_kept.shape[0]
    total = mine[...] + arrived[:size].astype(F32)
    own[...] = total
    sent[:size] = total.astype(BF)
    sent[size:] = (target_kept[...] + arrived[size + half :].astype(F32)).astype(BF)


def first_gather_kernel(mine, arrived, share):
    share[...] = (mine[...] + arrived[...].astype(F32)).astype(BF)


def second_gather_kernel(mine, arrived, node_across, share, node_sent):
    share[...] = (mine[...] + arrived[: mine.shape[0]].astype(F32)).astype(BF)
    node_sent[...] = node_across[...]


def put_shares(places, shares, outs, scratch):
    *held, sems = scratch
    copies = []

    def put(source, target):
        copies.append(pltpu.make_async_copy(source, target, sems.at[len(copies)]))
        copies[-1].start()

    for i, k in enumerate(places):
        other = lax.axis_index("dst") ^ k
        for out, into, share in zip(outs, held, shares[i], strict=True):
            rows, wide = into.shape[1:]
            size = share.shape[0]
            for h in range(rows // size):
                into[i, h * size : (h + 1) * size] = share[:, h * wide : (h + 1) * wide].astype(F32)
            put(into.at[i], out.at[pl.ds(pl.multiple_of(other * rows, rows), rows)])
    return copies


def first_shares_kernel(*refs):
    copies = put_shares((0, 1), (refs[:3], refs[3:6]), refs[6:9], refs[9:])
    for copy in copies:
        copy.wait()


def last_shares_kernel(state_own, nodes, arrived_1, arrived_2, *refs):
    shares, outs, scratch = refs[:6], refs[9:13], refs[13:]
    *held, state_held, state_sem = scratch
    copies = put_shares((2, 3), (shares[:3], shares[3:]), outs[1:], held)
    half = nodes.shape[0]
    part = arrived_2.shape[0] - half
    add_nodes(
        state_held,
        state_own,
        nodes[...] + arrived_1[part : part + half].astype(F32) + arrived_2[part:].astype(F32),
    )
    copies.append(pltpu.make_async_copy(state_held, outs[0], state_sem))
    copies[-1].start()
    for copy in copies:
        copy.wait()


def call(kernel, outs, scratch, args, spaces=None, out_spaces=None, aliases=None):
    return pl.pallas_call(
        kernel,
        out_shape=[jax.ShapeDtypeStruct(shape, dtype) for shape, dtype in outs],
        in_specs=[pl.BlockSpec(memory_space=space) for space in spaces or [pltpu.VMEM] * len(args)],
        out_specs=[pl.BlockSpec(memory_space=space) for space in out_spaces or [pltpu.VMEM] * len(outs)],
        scratch_shapes=[
            pltpu.VMEM(*entry) if isinstance(entry, tuple) else entry for entry in scratch
        ],
        input_output_aliases=aliases or {},
        compiler_params=pltpu.CompilerParams(vmem_limit_bytes=32 << 20),
    )(*args)


def in_hbm(value):
    return pltpu.with_memory_space_constraint(value, pltpu.HBM)


def swap(value, axis, k):
    return lax.ppermute(value, axis, [(i, i ^ k) for i in range(WAYS)])


def local(
    node_state,
    forcing,
    edge_attr,
    src_index,
    dst_index,
    edge_count,
    cotangent,
    edge_w1,
    edge_w2,
    node_w1,
):
    rows, width = node_state.shape[1:]
    hid, width_m = edge_w2.shape
    width_out = node_w1.shape[1]
    slots = edge_attr.shape[3]
    nodes = rows * WAYS
    steps = T_STEPS
    attr = edge_attr[:, 0, 0]
    joined = call(
        join_kernel,
        [((steps, rows, 2 * width + width_out), BF)],
        [pltpu.SemaphoreType.DMA((3,))],
        [in_hbm(value) for value in (node_state, forcing, cotangent)],
        [pltpu.HBM] * 3,
    )[0]
    targets = {k: swap(joined, "src", k) for k in ORDER}
    targets = [joined] + [targets[k] for k in range(1, WAYS)]
    sources = [joined] + [swap(node_state, "dst", k) for k in range(1, WAYS)]
    given = (src_index[0], dst_index[0], attr, edge_w1, edge_w2, node_w1)
    attr, w1, w2, wn, src_t, dst_t, base = call(
        stage_kernel,
        [(value.shape, value.dtype) for value in given[2:]]
        + [((nodes, slots), BF), ((nodes, slots), BF), ((steps, slots, hid), F32)],
        [((1, slots), jnp.int32), ((1, slots), jnp.int32), pltpu.SemaphoreType.DMA((len(given),))],
        [edge_count, *(in_hbm(value) for value in given)],
        [pltpu.SMEM] + [pltpu.HBM] * len(given),
    )
    forward, sums = [], []
    for moment in range(steps):
        forward.append(
            call(
                functools.partial(forward_kernel, moment),
                [((nodes, width_m), BF), ((nodes, width_m), F32), ((slots, hid), F32), ((nodes, hid), BF)],
                [],
                [*sources, *targets, base, src_t, dst_t, w1, w2],
            )
        )
    for message, own, _, _ in forward:
        total, sent = call(
            first_sum_kernel,
            [((nodes, width_m), F32), ((nodes, width_m), BF)],
            [],
            [own, swap(message, "src", 1)],
        )
        sums.append([total, swap(sent, "src", 2)])
    args = [
        [*sources, *targets, *sums[moment], attr, src_t, dst_t, *forward[moment][2:], w1, w2, wn]
        for moment in range(steps)
    ]
    state_0, forcing_0, edges_0, *earlier = call(
        backward_first_kernel,
        [
            ((rows, width), F32),
            ((rows, width), F32),
            ((slots, width), F32),
            ((nodes, width), F32),
            ((nodes, width), F32),
            (edge_w1.shape, F32),
            (edge_w2.shape, F32),
            (node_w1.shape, F32),
        ],
        [],
        args[0],
    )
    part, block, half = edge_w1.shape[0] // WAYS, hid // WAYS, rows // 2
    size = block // 2
    wide = 2 * size + half
    state_own, forcing_1, edges_1, first, second, node_grad, src_kept, core_a, core_b, target_kept, target_sent = call(
        backward_last_kernel,
        [
            ((steps, rows, width), F32),
            ((rows, width), F32),
            ((slots, width), F32),
            (edge_w1.shape, F32),
            (edge_w2.shape, F32),
            (node_w1.shape, F32),
            ((2 * half, hid), F32),
            ((2 * part, hid), BF),
            ((2 * wide, hid), BF),
            ((half, hid), F32),
            ((2 * half, hid), BF),
        ],
        [],
        [*args[1], state_0, *earlier],
    )
    grad_forcing, edges, token = call(
        out_kernel,
        [((steps, rows, width), F32), ((steps, slots, width), F32), ((8, 128), F32)],
        [pltpu.SemaphoreType.DMA((4,))],
        [forcing_0, edges_0, forcing_1, edges_1],
        out_spaces=[pltpu.HBM] * 2 + [pltpu.VMEM],
    )

    def both(count, sent):
        return [((count, hid), F32), ((sent, hid), BF)]

    mine_a, across_a = call(first_near_kernel, both(part, part), [], [first, swap(core_a, "dst", 1)])
    mine_b, across_b = call(
        second_near_kernel, both(wide, wide), [], [second, node_grad, src_kept, swap(core_b, "dst", 1)]
    )
    own_a, sent_a = call(add_kernel, both(part, part), [], [mine_a, swap(across_a, "dst", 2)])
    own_b, sent_b, node_share, nodes_sum = call(
        second_middle_kernel,
        both(size, size + 2 * half) + [((size, hid), BF), ((half, hid), F32)],
        [],
        [mine_b, swap(across_b, "dst", 2), target_sent, token],
    )
    node_across = swap(node_share, "dst", 2)
    own_a, sent_a = call(add_kernel, both(part, part), [], [own_a, swap(sent_a, "src", 1)])
    arrived_1 = swap(sent_b, "src", 1)
    own_b, sent_b = call(
        second_sum_over_src_kernel, both(size, size + half), [], [own_b, arrived_1, target_kept]
    )
    share_a = call(first_gather_kernel, [((part, hid), BF)], [], [own_a, swap(sent_a, "src", 2)])[0]
    arrived_2 = swap(sent_b, "src", 2)
    share_b, node_across = call(
        second_gather_kernel, [((size, hid), BF)] * 2, [], [own_b, arrived_2, node_across]
    )
    state = ((steps, rows, width), F32)
    own = [share_a, share_b, node_share]
    across = [swap(share_a, "dst", 2), swap(share_b, "dst", 2), node_across]
    outs = [(edge_w1.shape, F32), (edge_w2.shape, F32), (node_w1.shape, F32)]
    held = [((2, value.shape[0] // WAYS, value.shape[1]), F32) for value in (edge_w1, edge_w2, node_w1)]
    held.append(pltpu.SemaphoreType.DMA((6,)))
    grads = call(
        first_shares_kernel,
        outs,
        held,
        own + [swap(share, "dst", 1) for share in own],
        out_spaces=[pltpu.HBM] * 3,
    )
    grad_state, grad_first, grad_second, grad_node = call(
        last_shares_kernel,
        [state] + outs,
        held + [state, pltpu.SemaphoreType.DMA],
        [state_own, nodes_sum, arrived_1, arrived_2] + across + [swap(share, "dst", 1) for share in across] + list(grads),
        [pltpu.VMEM] * 10 + [pltpu.HBM] * 3,
        [pltpu.HBM] * 4,
        {10: 1, 11: 2, 12: 3},
    )
    return grad_state, grad_forcing, edges[:, None, None], grad_first, grad_second, grad_node


def silu_slope(value):
    sigma = jax.nn.sigmoid(value)
    return sigma * (1.0 + value * (1.0 - sigma))


def local_any(
    node_state,
    forcing,
    edge_attr,
    src_index,
    dst_index,
    edge_count,
    cotangent,
    edge_w1,
    edge_w2,
    node_w1,
):
    node_rows = node_state.shape[1]
    width_x = node_state.shape[2]
    width_m = edge_w2.shape[1]
    src_rows = node_rows * lax.axis_size("dst")
    dst_rows = node_rows * lax.axis_size("src")
    sources = lax.all_gather(node_state, "dst", axis=1, tiled=True)
    targets, forcing_block, cotangent_block = (
        lax.all_gather(node_state, "src", axis=1, tiled=True),
        lax.all_gather(forcing, "src", axis=1, tiled=True),
        lax.all_gather(cotangent, "src", axis=1, tiled=True),
    )
    src_local = src_index[0, 0]
    dst_local = dst_index[0, 0]
    alive = lax.iota(jnp.int32, src_local.shape[0]) < edge_count[0, 0]
    alive_float = alive.astype(jnp.float32)[:, None]
    alive_half = alive.astype(jnp.bfloat16)[:, None]
    own_start = lax.axis_index("src") * node_rows
    grad_first = jnp.zeros(edge_w1.shape, jnp.float32)
    grad_second = jnp.zeros(edge_w2.shape, jnp.float32)
    grad_node = jnp.zeros(node_w1.shape, jnp.float32)
    state_out, forcing_out, edge_out = ([], [], [])
    for moment in range(T_STEPS):
        edge_in = jnp.concatenate(
            [sources[moment][src_local], targets[moment][dst_local], edge_attr[moment, 0, 0]],
            axis=1,
        )
        pre_edge = jnp.dot(edge_in, edge_w1, preferred_element_type=jnp.float32)
        hidden = jax.nn.silu(pre_edge).astype(jnp.bfloat16)
        message = jnp.dot(hidden, edge_w2, preferred_element_type=jnp.float32) * alive_float
        partial_value = jax.ops.segment_sum(message, dst_local, num_segments=dst_rows)
        agg_block = lax.psum(partial_value, "src")
        node_in = jnp.concatenate(
            [targets[moment], agg_block.astype(jnp.bfloat16), forcing_block[moment]], axis=1
        )
        pre_node = jnp.dot(node_in, node_w1, preferred_element_type=jnp.float32)
        grad_pre_node = (cotangent_block[moment].astype(jnp.float32) * silu_slope(pre_node)).astype(
            jnp.bfloat16
        )
        grad_node_in = jnp.dot(grad_pre_node, node_w1.T, preferred_element_type=jnp.float32)
        own_in = lax.dynamic_slice_in_dim(node_in, own_start, node_rows, 0)
        own_pre = lax.dynamic_slice_in_dim(grad_pre_node, own_start, node_rows, 0)
        grad_node = grad_node + jnp.dot(own_in.T, own_pre, preferred_element_type=jnp.float32)
        own_grad = lax.dynamic_slice_in_dim(grad_node_in, own_start, node_rows, 0)
        grad_agg = grad_node_in[:, width_x : width_x + width_m].astype(jnp.bfloat16)
        grad_message = grad_agg[dst_local] * alive_half
        grad_second = grad_second + jnp.dot(
            hidden.T, grad_message, preferred_element_type=jnp.float32
        )
        grad_hidden = jnp.dot(grad_message, edge_w2.T, preferred_element_type=jnp.float32)
        grad_pre_edge = (grad_hidden * silu_slope(pre_edge)).astype(jnp.bfloat16)
        grad_first = grad_first + jnp.dot(
            edge_in.T, grad_pre_edge, preferred_element_type=jnp.float32
        )
        grad_edge_in = jnp.dot(grad_pre_edge, edge_w1.T, preferred_element_type=jnp.float32)
        source_part = jax.ops.segment_sum(
            grad_edge_in[:, :width_x], src_local, num_segments=src_rows
        )
        target_part = jax.ops.segment_sum(
            grad_edge_in[:, width_x : 2 * width_x], dst_local, num_segments=dst_rows
        )
        from_sources = lax.psum_scatter(source_part, "dst", scatter_dimension=0, tiled=True)
        from_targets = lax.psum_scatter(target_part, "src", scatter_dimension=0, tiled=True)
        state_out.append(own_grad[:, :width_x] + from_sources + from_targets)
        forcing_out.append(own_grad[:, width_x + width_m :])
        edge_out.append(grad_edge_in[:, 2 * width_x :])
    grad_first, grad_second, grad_node = lax.psum(
        (grad_first, grad_second, grad_node), ("src", "dst")
    )
    return (
        jnp.stack(state_out),
        jnp.stack(forcing_out),
        jnp.stack(edge_out)[:, None, None],
        grad_first,
        grad_second,
        grad_node,
    )


def solution(mesh):
    in_specs = (
        P(None, ("groups", "src", "dst"), None),
        P(None, ("groups", "src", "dst"), None),
        P(None, ("groups", "src"), "dst", None, None),
        P(("groups", "src"), "dst", None),
        P(("groups", "src"), "dst", None),
        P(("groups", "src"), "dst"),
        P(None, ("groups", "src", "dst"), None),
        P(),
        P(),
        P(),
    )
    out_specs = (
        P(None, ("groups", "src", "dst"), None),
        P(None, ("groups", "src", "dst"), None),
        P(None, ("groups", "src"), "dst", None, None),
        P("groups", None),
        P("groups", None),
        P("groups", None),
    )
    square = mesh.shape["src"] == WAYS and mesh.shape["dst"] == WAYS
    body = local if square else local_any
    return jax.shard_map(body, mesh=mesh, in_specs=in_specs, out_specs=out_specs, check_vma=False)
```

```python
import functools

import jax
import jax.numpy as jnp
from jax import lax
from jax.experimental import pallas as pl
from jax.experimental.pallas import tpu as pltpu
from jax.sharding import PartitionSpec as P

T_STEPS = 2
WAYS = 4
ORDER = (3, 1, 2)
BF = jnp.bfloat16
F32 = jnp.float32


def sigmoid(value):
    return 0.5 * jnp.tanh(0.5 * value) + 0.5


def slope_of(value):
    sigma = sigmoid(value)
    return sigma * (1.0 + value * (1.0 - sigma))


def mm(a, b):
    return jnp.dot(a, b, preferred_element_type=F32)


def mm_nt(a, b):
    return lax.dot_general(a, b, (((1,), (1,)), ((), ())), preferred_element_type=F32)


def mm_tn(a, b):
    return lax.dot_general(a, b, (((0,), (0,)), ((), ())), preferred_element_type=F32)


def one_hot_t(index, nodes, live=None):
    hit = lax.broadcasted_iota(jnp.int32, (nodes, index.shape[1]), 0) == index
    if live is not None:
        hit = jnp.logical_and(hit, live)
    return jnp.where(hit, 1.0, 0.0).astype(BF)


def stacked(refs, moment, width):
    return jnp.concatenate([ref[moment, :, :width] for ref in refs], axis=0)


def turned(value, k):
    rows = value.shape[0] // WAYS
    return jnp.concatenate([value[(j ^ k) * rows : ((j ^ k) + 1) * rows] for j in range(WAYS)], axis=0)


def join_kernel(state, forcing, cotangent, joined, sems):
    width = state.shape[2]
    copies = [
        pltpu.make_async_copy(state, joined.at[:, :, :width], sems.at[0]),
        pltpu.make_async_copy(forcing, joined.at[:, :, width : 2 * width], sems.at[1]),
        pltpu.make_async_copy(cotangent, joined.at[:, :, 2 * width :], sems.at[2]),
    ]
    for copy in copies:
        copy.start()
    for copy in copies:
        copy.wait()


def stage_kernel(count, src_hbm, dst_hbm, attr_hbm, w1_hbm, w2_hbm, wn_hbm, *refs):
    attr, w1, w2, wn, src_t, dst_t, base, src_held, dst_held, sems = refs
    width = attr.shape[2]
    nodes, slots = src_t.shape
    rows = nodes // WAYS
    copies = [
        pltpu.make_async_copy(source, target, sems.at[i])
        for i, (source, target) in enumerate(
            [
                (src_hbm, src_held),
                (dst_hbm, dst_held),
                (attr_hbm, attr),
                (w1_hbm, w1),
                (w2_hbm, w2),
                (wn_hbm, wn),
            ]
        )
    ]
    for copy in copies:
        copy.start()
    copies[0].wait()
    copies[1].wait()
    live = lax.broadcasted_iota(jnp.int32, (1, slots), 1) < count[0, 0]
    src_t[...] = one_hot_t(src_held[...] ^ (lax.axis_index("dst") * rows), nodes)
    dst_t[...] = one_hot_t(dst_held[...] ^ (lax.axis_index("src") * rows), nodes, live)
    copies[2].wait()
    copies[3].wait()
    for moment in range(T_STEPS):
        base[moment] = mm(attr[moment], w1[2 * width :])
    for copy in copies[4:]:
        copy.wait()


def forward_kernel(moment, *refs):
    n = WAYS
    sources, targets, refs = refs[:n], refs[n : 2 * n], refs[2 * n :]
    base, src_t, dst_t, w1, w2, message, own, slope, sums = refs
    width = sources[1].shape[2]
    ends = jnp.concatenate(
        [
            mm_tn(src_t[...], stacked(sources, moment, width)).astype(BF),
            mm_tn(dst_t[...], stacked(targets, moment, width)).astype(BF),
        ],
        axis=1,
    )
    pre = base[moment] + mm(ends, w1[: 2 * width])
    sigma = sigmoid(pre)
    hidden = (pre * sigma).astype(BF)
    slope[...] = sigma * (1.0 + pre * (1.0 - sigma))
    total = mm(dst_t[...], hidden)
    high = total.astype(BF)
    low = (total - high.astype(F32)).astype(BF)
    sums[...] = high
    product = mm(high, w2[...]) + mm(low, w2[...])
    own[...] = product
    message[...] = product.astype(BF)


def first_sum_kernel(own, arrived, total, sent):
    value = own[...] + turned(arrived[...].astype(F32), 1)
    total[...] = value
    sent[...] = value.astype(BF)


def backward(moment, put_edges, sources, targets, total, arrived, attr, src_t, dst_t, slope, sums, w1, w2, wn):
    rows, width = sources[1].shape[1:]
    width_m = w2.shape[1]
    joined = stacked(targets, moment, targets[0].shape[2])
    state, forcing, cotangent = joined[:, :width], joined[:, width : 2 * width], joined[:, 2 * width :]
    agg = total[...] + turned(arrived[...].astype(F32), 2)
    node_in = jnp.concatenate([state, agg.astype(BF), forcing], axis=1)
    grad_pre = (cotangent.astype(F32) * slope_of(mm(node_in, wn[...]))).astype(BF)
    grad_in = mm_nt(grad_pre, wn[...])
    grad_agg = grad_in[:, width : width + width_m].astype(BF)
    grad_message = mm_tn(dst_t[...], grad_agg).astype(BF)
    grad_pre_edge = (mm_nt(grad_message, w2[...]) * slope[...]).astype(BF)
    put_edges(mm_nt(grad_pre_edge, w1[2 * width :]), grad_in[:rows, width + width_m :])
    from_src = mm(src_t[...], grad_pre_edge).astype(BF)
    from_dst = mm(dst_t[...], grad_pre_edge).astype(BF)
    to_src = mm_nt(from_src, w1[:width])
    to_dst = mm_nt(from_dst, w1[width : 2 * width])
    first = [
        mm_tn(stacked(sources, moment, width), from_src),
        mm_tn(state, from_dst),
        mm_tn(attr[moment], grad_pre_edge),
    ]
    second = mm_tn(sums[...], grad_agg)
    node_grad = mm_tn(node_in, grad_pre)
    state_own = grad_in[:rows, :width] + to_dst[:rows]
    return state_own, to_src, to_dst, first, second, node_grad


def split_refs(refs):
    n = WAYS
    return refs[:n], refs[n : 2 * n], refs[2 * n : 2 * n + 10], refs[2 * n + 10 :]


def backward_first_kernel(*refs):
    sources, targets, args, refs = split_refs(refs)
    state, forcing, edges, to_src, to_dst, first_out, second_out, node_out = refs

    def put_edges(edge_values, forcing_values):
        edges[...] = edge_values
        forcing[...] = forcing_values

    state[...], to_src[...], to_dst[...], first, second, node_grad = backward(0, put_edges, sources, targets, *args)
    width = first[0].shape[0]
    for i, value in enumerate(first):
        first_out[i * width : (i + 1) * width] = value
    second_out[...] = second
    node_out[...] = node_grad


def backward_last_kernel(*refs):
    n = WAYS
    sources, targets, args, refs = split_refs(refs)
    state_0, to_src_0, to_dst_0, first_0, second_0, node_0 = refs[:6]
    state_own, forcing, edges, first_held, second_held, node_grad_held, src_kept = refs[6:13]
    core_a, core_b, target_kept, target_sent = refs[13:]

    def put_edges(edge_values, forcing_values):
        edges[...] = edge_values
        forcing[...] = forcing_values

    state_1, to_src_1, to_dst_1, first, second, node_grad = backward(1, put_edges, sources, targets, *args)
    state_own[0], state_own[1] = state_0[...], state_1
    width = first[0].shape[0]
    for i, value in enumerate(first):
        first_held[i * width : (i + 1) * width] = first_0[i * width : (i + 1) * width] + value
    second_held[...] = second_0[...] + second
    node_grad_held[...] = node_0[...] + node_grad
    part, block = first_held.shape[0] // n, second_held.shape[0] // n
    size, wide = block // 2, second_held.shape[1]
    for i, k in enumerate((1, 3)):
        other = lax.axis_index("dst") ^ k
        core_a[i * part : (i + 1) * part] = first_held[pl.ds(pl.multiple_of(other * part, part), part)].astype(BF)
        start = i * (core_b.shape[0] // 2)
        for held in (second_held, node_grad_held):
            for j in range(2):
                spot = pl.ds(pl.multiple_of(other * block + j * size, size), size)
                core_b[start : start + size, j * wide : (j + 1) * wide] = held[spot].astype(BF)
            start += size
        put_nodes(core_b, start, k, (to_src_0[...], to_src_1))
    for i, k in enumerate((0, 2)):
        put_nodes(src_kept, i * target_kept.shape[0], k, (to_src_0[...], to_src_1))
    put_nodes(target_kept, 0, 2, (to_dst_0[...], to_dst_1))
    for i, k in enumerate((1, 3)):
        put_nodes(target_sent, i * target_kept.shape[0], k, (to_dst_0[...], to_dst_1))


def out_kernel(forcing_0, edges_0, forcing_1, edges_1, forcing, edges, token, sems):
    pairs = [(edges_0, edges.at[0]), (edges_1, edges.at[1]), (forcing_0, forcing.at[0]), (forcing_1, forcing.at[1])]
    copies = [pltpu.make_async_copy(*ends, sems.at[i]) for i, ends in enumerate(pairs)]
    for copy in copies:
        copy.start()
    token[...] = jnp.zeros_like(token)
    for copy in copies:
        copy.wait()


def put_nodes(into, start, k, values):
    width = values[0].shape[1]
    rows = values[0].shape[0] // WAYS
    half = rows // 2
    for moment, value in enumerate(values):
        for j in range(2):
            lanes = slice((moment * 2 + j) * width, (moment * 2 + j + 1) * width)
            spot = slice(k * rows + j * half, k * rows + (j + 1) * half)
            into[start : start + half, lanes] = value[spot].astype(into.dtype)


def add_nodes(state, base, value):
    width, half = state.shape[2], value.shape[0]
    for moment in range(T_STEPS):
        for j in range(2):
            lanes = slice((moment * 2 + j) * width, (moment * 2 + j + 1) * width)
            spot = slice(j * half, (j + 1) * half)
            state[moment, spot] = base[moment, spot] + value[:, lanes]


def first_near_kernel(whole, arrived, own, across):
    part = own.shape[0]
    for i, (k, into) in enumerate(((0, own), (2, across))):
        spot = pl.ds(pl.multiple_of((lax.axis_index("dst") ^ k) * part, part), part)
        into[...] = (whole[spot] + arrived[i * part : (i + 1) * part].astype(F32)).astype(into.dtype)


def second_near_kernel(second, node_grad, src_kept, arrived, _, own, across):
    wide = second.shape[1]
    block = second.shape[0] // WAYS
    size, half = block // 2, src_kept.shape[0] // 2
    for i, (k, into) in enumerate(((0, own), (2, across))):
        other = lax.axis_index("dst") ^ k
        start = 0
        for whole in (second, node_grad):
            for j in range(2):
                lanes = slice(j * wide, (j + 1) * wide)
                spot = pl.ds(pl.multiple_of(other * block + j * size, size), size)
                value = arrived[i * into.shape[0] + start : i * into.shape[0] + start + size, lanes]
                into[start : start + size, lanes] = (whole[spot] + value.astype(F32)).astype(into.dtype)
            start += size
        value = arrived[i * into.shape[0] + start : (i + 1) * into.shape[0]]
        into[start:] = (src_kept[i * half : (i + 1) * half] + value.astype(F32)).astype(into.dtype)


def add_kernel(mine, arrived, own, sent):
    total = mine[...] + arrived[...].astype(F32)
    own[...] = total
    sent[...] = total.astype(BF)


def second_middle_kernel(mine, arrived, target_sent, own, sent, node_share, nodes):
    total = mine[...] + arrived[...].astype(F32)
    size = own.shape[0]
    own[...] = total[:size]
    sent[:size] = total[:size].astype(BF)
    sent[size:] = target_sent[...]
    node_share[...] = total[size : 2 * size].astype(BF)
    nodes[...] = total[2 * size :]


def second_sum_over_src_kernel(mine, arrived, target_kept, own, sent):
    size, half = own.shape[0], target_kept.shape[0]
    total = mine[...] + arrived[:size].astype(F32)
    own[...] = total
    sent[:size] = total.astype(BF)
    sent[size:] = (target_kept[...] + arrived[size + half :].astype(F32)).astype(BF)


def first_gather_kernel(mine, arrived, share):
    share[...] = (mine[...] + arrived[...].astype(F32)).astype(BF)


def second_gather_kernel(mine, arrived, node_across, share, node_sent):
    share[...] = (mine[...] + arrived[: mine.shape[0]].astype(F32)).astype(BF)
    node_sent[...] = node_across[...]


def put_shares(places, shares, outs, scratch):
    *held, sems = scratch
    copies = []

    def put(source, target):
        copies.append(pltpu.make_async_copy(source, target, sems.at[len(copies)]))
        copies[-1].start()

    for i, k in enumerate(places):
        other = lax.axis_index("dst") ^ k
        for out, into, share in zip(outs, held, shares[i], strict=True):
            rows, wide = into.shape[1:]
            size = share.shape[0]
            for h in range(rows // size):
                into[i, h * size : (h + 1) * size] = share[:, h * wide : (h + 1) * wide].astype(F32)
            put(into.at[i], out.at[pl.ds(pl.multiple_of(other * rows, rows), rows)])
    return copies


def first_shares_kernel(*refs):
    copies = put_shares((0, 1), (refs[:3], refs[3:6]), refs[6:9], refs[9:])
    for copy in copies:
        copy.wait()


def last_shares_kernel(state_own, nodes, arrived_1, arrived_2, *refs):
    shares, outs, scratch = refs[:6], refs[9:13], refs[13:]
    *held, state_held, state_sem = scratch
    copies = put_shares((2, 3), (shares[:3], shares[3:]), outs[1:], held)
    half = nodes.shape[0]
    part = arrived_2.shape[0] - half
    add_nodes(
        state_held,
        state_own,
        nodes[...] + arrived_1[part : part + half].astype(F32) + arrived_2[part:].astype(F32),
    )
    copies.append(pltpu.make_async_copy(state_held, outs[0], state_sem))
    copies[-1].start()
    for copy in copies:
        copy.wait()


def call(kernel, outs, scratch, args, spaces=None, out_spaces=None, aliases=None):
    return pl.pallas_call(
        kernel,
        out_shape=[jax.ShapeDtypeStruct(shape, dtype) for shape, dtype in outs],
        in_specs=[pl.BlockSpec(memory_space=space) for space in spaces or [pltpu.VMEM] * len(args)],
        out_specs=[pl.BlockSpec(memory_space=space) for space in out_spaces or [pltpu.VMEM] * len(outs)],
        scratch_shapes=[
            pltpu.VMEM(*entry) if isinstance(entry, tuple) else entry for entry in scratch
        ],
        input_output_aliases=aliases or {},
        compiler_params=pltpu.CompilerParams(vmem_limit_bytes=32 << 20),
    )(*args)


def in_hbm(value):
    return pltpu.with_memory_space_constraint(value, pltpu.HBM)


def swap(value, axis, k):
    return lax.ppermute(value, axis, [(i, i ^ k) for i in range(WAYS)])


def local(
    node_state,
    forcing,
    edge_attr,
    src_index,
    dst_index,
    edge_count,
    cotangent,
    edge_w1,
    edge_w2,
    node_w1,
):
    rows, width = node_state.shape[1:]
    hid, width_m = edge_w2.shape
    width_out = node_w1.shape[1]
    slots = edge_attr.shape[3]
    nodes = rows * WAYS
    steps = T_STEPS
    attr = edge_attr[:, 0, 0]
    joined = call(
        join_kernel,
        [((steps, rows, 2 * width + width_out), BF)],
        [pltpu.SemaphoreType.DMA((3,))],
        [in_hbm(value) for value in (node_state, forcing, cotangent)],
        [pltpu.HBM] * 3,
    )[0]
    targets = {k: swap(joined, "src", k) for k in ORDER}
    targets = [joined] + [targets[k] for k in range(1, WAYS)]
    sources = [joined] + [swap(node_state, "dst", k) for k in range(1, WAYS)]
    given = (src_index[0], dst_index[0], attr, edge_w1, edge_w2, node_w1)
    attr, w1, w2, wn, src_t, dst_t, base = call(
        stage_kernel,
        [(value.shape, value.dtype) for value in given[2:]]
        + [((nodes, slots), BF), ((nodes, slots), BF), ((steps, slots, hid), F32)],
        [((1, slots), jnp.int32), ((1, slots), jnp.int32), pltpu.SemaphoreType.DMA((len(given),))],
        [edge_count, *(in_hbm(value) for value in given)],
        [pltpu.SMEM] + [pltpu.HBM] * len(given),
    )
    forward, sums = [], []
    for moment in range(steps):
        forward.append(
            call(
                functools.partial(forward_kernel, moment),
                [((nodes, width_m), BF), ((nodes, width_m), F32), ((slots, hid), F32), ((nodes, hid), BF)],
                [],
                [*sources, *targets, base, src_t, dst_t, w1, w2],
            )
        )
    for message, own, _, _ in forward:
        total, sent = call(
            first_sum_kernel,
            [((nodes, width_m), F32), ((nodes, width_m), BF)],
            [],
            [own, swap(message, "src", 1)],
        )
        sums.append([total, swap(sent, "src", 2)])
    args = [
        [*sources, *targets, *sums[moment], attr, src_t, dst_t, *forward[moment][2:], w1, w2, wn]
        for moment in range(steps)
    ]
    state_0, forcing_0, edges_0, *earlier = call(
        backward_first_kernel,
        [
            ((rows, width), F32),
            ((rows, width), F32),
            ((slots, width), F32),
            ((nodes, width), F32),
            ((nodes, width), F32),
            (edge_w1.shape, F32),
            (edge_w2.shape, F32),
            (node_w1.shape, F32),
        ],
        [],
        args[0],
    )
    part, block, half = edge_w1.shape[0] // WAYS, hid // WAYS, rows // 2
    size = block // 2
    wide = 2 * size + half
    state_own, forcing_1, edges_1, first, second, node_grad, src_kept, core_a, core_b, target_kept, target_sent = call(
        backward_last_kernel,
        [
            ((steps, rows, width), F32),
            ((rows, width), F32),
            ((slots, width), F32),
            (edge_w1.shape, F32),
            (edge_w2.shape, F32),
            (node_w1.shape, F32),
            ((2 * half, hid), F32),
            ((2 * part, hid), BF),
            ((2 * wide, hid), BF),
            ((half, hid), F32),
            ((2 * half, hid), BF),
        ],
        [],
        [*args[1], state_0, *earlier],
    )
    grad_forcing, edges, token = call(
        out_kernel,
        [((steps, rows, width), F32), ((steps, slots, width), F32), ((8, 128), F32)],
        [pltpu.SemaphoreType.DMA((4,))],
        [forcing_0, edges_0, forcing_1, edges_1],
        out_spaces=[pltpu.HBM] * 2 + [pltpu.VMEM],
    )

    def both(count, sent):
        return [((count, hid), F32), ((sent, hid), BF)]

    mine_a, across_a = call(first_near_kernel, both(part, part), [], [first, swap(core_a, "dst", 1)])
    mine_b, across_b = call(
        second_near_kernel, both(wide, wide), [], [second, node_grad, src_kept, swap(core_b, "dst", 1), token]
    )
    own_a, sent_a = call(add_kernel, both(part, part), [], [mine_a, swap(across_a, "dst", 2)])
    own_b, sent_b, node_share, nodes_sum = call(
        second_middle_kernel,
        both(size, size + 2 * half) + [((size, hid), BF), ((half, hid), F32)],
        [],
        [mine_b, swap(across_b, "dst", 2), target_sent],
    )
    node_across = swap(node_share, "dst", 2)
    own_a, sent_a = call(add_kernel, both(part, part), [], [own_a, swap(sent_a, "src", 1)])
    arrived_1 = swap(sent_b, "src", 1)
    own_b, sent_b = call(
        second_sum_over_src_kernel, both(size, size + half), [], [own_b, arrived_1, target_kept]
    )
    share_a = call(first_gather_kernel, [((part, hid), BF)], [], [own_a, swap(sent_a, "src", 2)])[0]
    arrived_2 = swap(sent_b, "src", 2)
    share_b, node_across = call(
        second_gather_kernel, [((size, hid), BF)] * 2, [], [own_b, arrived_2, node_across]
    )
    state = ((steps, rows, width), F32)
    own = [share_a, share_b, node_share]
    across = [swap(share_a, "dst", 2), swap(share_b, "dst", 2), node_across]
    outs = [(edge_w1.shape, F32), (edge_w2.shape, F32), (node_w1.shape, F32)]
    held = [((2, value.shape[0] // WAYS, value.shape[1]), F32) for value in (edge_w1, edge_w2, node_w1)]
    held.append(pltpu.SemaphoreType.DMA((6,)))
    grads = call(
        first_shares_kernel,
        outs,
        held,
        own + [swap(share, "dst", 1) for share in own],
        out_spaces=[pltpu.HBM] * 3,
    )
    grad_state, grad_first, grad_second, grad_node = call(
        last_shares_kernel,
        [state] + outs,
        held + [state, pltpu.SemaphoreType.DMA],
        [state_own, nodes_sum, arrived_1, arrived_2] + across + [swap(share, "dst", 1) for share in across] + list(grads),
        [pltpu.VMEM] * 10 + [pltpu.HBM] * 3,
        [pltpu.HBM] * 4,
        {10: 1, 11: 2, 12: 3},
    )
    return grad_state, grad_forcing, edges[:, None, None], grad_first, grad_second, grad_node


def silu_slope(value):
    sigma = jax.nn.sigmoid(value)
    return sigma * (1.0 + value * (1.0 - sigma))


def local_any(
    node_state,
    forcing,
    edge_attr,
    src_index,
    dst_index,
    edge_count,
    cotangent,
    edge_w1,
    edge_w2,
    node_w1,
):
    node_rows = node_state.shape[1]
    width_x = node_state.shape[2]
    width_m = edge_w2.shape[1]
    src_rows = node_rows * lax.axis_size("dst")
    dst_rows = node_rows * lax.axis_size("src")
    sources = lax.all_gather(node_state, "dst", axis=1, tiled=True)
    targets, forcing_block, cotangent_block = (
        lax.all_gather(node_state, "src", axis=1, tiled=True),
        lax.all_gather(forcing, "src", axis=1, tiled=True),
        lax.all_gather(cotangent, "src", axis=1, tiled=True),
    )
    src_local = src_index[0, 0]
    dst_local = dst_index[0, 0]
    alive = lax.iota(jnp.int32, src_local.shape[0]) < edge_count[0, 0]
    alive_float = alive.astype(jnp.float32)[:, None]
    alive_half = alive.astype(jnp.bfloat16)[:, None]
    own_start = lax.axis_index("src") * node_rows
    grad_first = jnp.zeros(edge_w1.shape, jnp.float32)
    grad_second = jnp.zeros(edge_w2.shape, jnp.float32)
    grad_node = jnp.zeros(node_w1.shape, jnp.float32)
    state_out, forcing_out, edge_out = ([], [], [])
    for moment in range(T_STEPS):
        edge_in = jnp.concatenate(
            [sources[moment][src_local], targets[moment][dst_local], edge_attr[moment, 0, 0]],
            axis=1,
        )
        pre_edge = jnp.dot(edge_in, edge_w1, preferred_element_type=jnp.float32)
        hidden = jax.nn.silu(pre_edge).astype(jnp.bfloat16)
        message = jnp.dot(hidden, edge_w2, preferred_element_type=jnp.float32) * alive_float
        partial_value = jax.ops.segment_sum(message, dst_local, num_segments=dst_rows)
        agg_block = lax.psum(partial_value, "src")
        node_in = jnp.concatenate(
            [targets[moment], agg_block.astype(jnp.bfloat16), forcing_block[moment]], axis=1
        )
        pre_node = jnp.dot(node_in, node_w1, preferred_element_type=jnp.float32)
        grad_pre_node = (cotangent_block[moment].astype(jnp.float32) * silu_slope(pre_node)).astype(
            jnp.bfloat16
        )
        grad_node_in = jnp.dot(grad_pre_node, node_w1.T, preferred_element_type=jnp.float32)
        own_in = lax.dynamic_slice_in_dim(node_in, own_start, node_rows, 0)
        own_pre = lax.dynamic_slice_in_dim(grad_pre_node, own_start, node_rows, 0)
        grad_node = grad_node + jnp.dot(own_in.T, own_pre, preferred_element_type=jnp.float32)
        own_grad = lax.dynamic_slice_in_dim(grad_node_in, own_start, node_rows, 0)
        grad_agg = grad_node_in[:, width_x : width_x + width_m].astype(jnp.bfloat16)
        grad_message = grad_agg[dst_local] * alive_half
        grad_second = grad_second + jnp.dot(
            hidden.T, grad_message, preferred_element_type=jnp.float32
        )
        grad_hidden = jnp.dot(grad_message, edge_w2.T, preferred_element_type=jnp.float32)
        grad_pre_edge = (grad_hidden * silu_slope(pre_edge)).astype(jnp.bfloat16)
        grad_first = grad_first + jnp.dot(
            edge_in.T, grad_pre_edge, preferred_element_type=jnp.float32
        )
        grad_edge_in = jnp.dot(grad_pre_edge, edge_w1.T, preferred_element_type=jnp.float32)
        source_part = jax.ops.segment_sum(
            grad_edge_in[:, :width_x], src_local, num_segments=src_rows
        )
        target_part = jax.ops.segment_sum(
            grad_edge_in[:, width_x : 2 * width_x], dst_local, num_segments=dst_rows
        )
        from_sources = lax.psum_scatter(source_part, "dst", scatter_dimension=0, tiled=True)
        from_targets = lax.psum_scatter(target_part, "src", scatter_dimension=0, tiled=True)
        state_out.append(own_grad[:, :width_x] + from_sources + from_targets)
        forcing_out.append(own_grad[:, width_x + width_m :])
        edge_out.append(grad_edge_in[:, 2 * width_x :])
    grad_first, grad_second, grad_node = lax.psum(
        (grad_first, grad_second, grad_node), ("src", "dst")
    )
    return (
        jnp.stack(state_out),
        jnp.stack(forcing_out),
        jnp.stack(edge_out)[:, None, None],
        grad_first,
        grad_second,
        grad_node,
    )


def solution(mesh):
    in_specs = (
        P(None, ("groups", "src", "dst"), None),
        P(None, ("groups", "src", "dst"), None),
        P(None, ("groups", "src"), "dst", None, None),
        P(("groups", "src"), "dst", None),
        P(("groups", "src"), "dst", None),
        P(("groups", "src"), "dst"),
        P(None, ("groups", "src", "dst"), None),
        P(),
        P(),
        P(),
    )
    out_specs = (
        P(None, ("groups", "src", "dst"), None),
        P(None, ("groups", "src", "dst"), None),
        P(None, ("groups", "src"), "dst", None, None),
        P("groups", None),
        P("groups", None),
        P("groups", None),
    )
    square = mesh.shape["src"] == WAYS and mesh.shape["dst"] == WAYS
    body = local if square else local_any
    return jax.shard_map(body, mesh=mesh, in_specs=in_specs, out_specs=out_specs, check_vma=False)
```

```python
import functools

import jax
import jax.numpy as jnp
from jax import lax
from jax.experimental import pallas as pl
from jax.experimental.pallas import tpu as pltpu
from jax.sharding import PartitionSpec as P

T_STEPS = 2
WAYS = 4
ORDER = (3, 1, 2)
BF = jnp.bfloat16
F32 = jnp.float32


def sigmoid(value):
    return 0.5 * jnp.tanh(0.5 * value) + 0.5


def slope_of(value):
    sigma = sigmoid(value)
    return sigma * (1.0 + value * (1.0 - sigma))


def mm(a, b):
    return jnp.dot(a, b, preferred_element_type=F32)


def mm_nt(a, b):
    return lax.dot_general(a, b, (((1,), (1,)), ((), ())), preferred_element_type=F32)


def mm_tn(a, b):
    return lax.dot_general(a, b, (((0,), (0,)), ((), ())), preferred_element_type=F32)


def one_hot_t(index, nodes, live=None):
    hit = lax.broadcasted_iota(jnp.int32, (nodes, index.shape[1]), 0) == index
    if live is not None:
        hit = jnp.logical_and(hit, live)
    return jnp.where(hit, 1.0, 0.0).astype(BF)


def stacked(refs, moment, width):
    return jnp.concatenate([ref[moment, :, :width] for ref in refs], axis=0)


def turned(value, k):
    rows = value.shape[0] // WAYS
    return jnp.concatenate([value[(j ^ k) * rows : ((j ^ k) + 1) * rows] for j in range(WAYS)], axis=0)


def join_kernel(state, forcing, cotangent, joined, sems):
    width = state.shape[2]
    copies = [
        pltpu.make_async_copy(state, joined.at[:, :, :width], sems.at[0]),
        pltpu.make_async_copy(forcing, joined.at[:, :, width : 2 * width], sems.at[1]),
        pltpu.make_async_copy(cotangent, joined.at[:, :, 2 * width :], sems.at[2]),
    ]
    for copy in copies:
        copy.start()
    for copy in copies:
        copy.wait()


def stage_kernel(count, src_hbm, dst_hbm, attr_hbm, w1_hbm, w2_hbm, wn_hbm, *refs):
    attr, w1, w2, wn, src_t, dst_t, base, src_held, dst_held, sems = refs
    width = attr.shape[2]
    nodes, slots = src_t.shape
    rows = nodes // WAYS
    copies = [
        pltpu.make_async_copy(source, target, sems.at[i])
        for i, (source, target) in enumerate(
            [
                (src_hbm, src_held),
                (dst_hbm, dst_held),
                (attr_hbm, attr),
                (w1_hbm, w1),
                (w2_hbm, w2),
                (wn_hbm, wn),
            ]
        )
    ]
    for copy in copies:
        copy.start()
    copies[0].wait()
    copies[1].wait()
    live = lax.broadcasted_iota(jnp.int32, (1, slots), 1) < count[0, 0]
    src_t[...] = one_hot_t(src_held[...] ^ (lax.axis_index("dst") * rows), nodes)
    dst_t[...] = one_hot_t(dst_held[...] ^ (lax.axis_index("src") * rows), nodes, live)
    copies[2].wait()
    copies[3].wait()
    for moment in range(T_STEPS):
        base[moment] = mm(attr[moment], w1[2 * width :])
    for copy in copies[4:]:
        copy.wait()


def forward_kernel(moment, *refs):
    n = WAYS
    sources, targets, refs = refs[:n], refs[n : 2 * n], refs[2 * n :]
    base, src_t, dst_t, w1, w2, message, own, slope, sums = refs
    width = sources[1].shape[2]
    ends = jnp.concatenate(
        [
            mm_tn(src_t[...], stacked(sources, moment, width)).astype(BF),
            mm_tn(dst_t[...], stacked(targets, moment, width)).astype(BF),
        ],
        axis=1,
    )
    pre = base[moment] + mm(ends, w1[: 2 * width])
    sigma = sigmoid(pre)
    hidden = (pre * sigma).astype(BF)
    slope[...] = sigma * (1.0 + pre * (1.0 - sigma))
    total = mm(dst_t[...], hidden)
    high = total.astype(BF)
    low = (total - high.astype(F32)).astype(BF)
    sums[...] = high
    product = mm(high, w2[...]) + mm(low, w2[...])
    own[...] = product
    message[...] = product.astype(BF)


def first_sum_kernel(own, arrived, total, sent):
    value = own[...] + turned(arrived[...].astype(F32), 1)
    total[...] = value
    sent[...] = value.astype(BF)


def backward(moment, put_edges, sources, targets, total, arrived, attr, src_t, dst_t, slope, sums, w1, w2, wn):
    rows, width = sources[1].shape[1:]
    width_m = w2.shape[1]
    joined = stacked(targets, moment, targets[0].shape[2])
    state, forcing, cotangent = joined[:, :width], joined[:, width : 2 * width], joined[:, 2 * width :]
    agg = total[...] + turned(arrived[...].astype(F32), 2)
    node_in = jnp.concatenate([state, agg.astype(BF), forcing], axis=1)
    grad_pre = (cotangent.astype(F32) * slope_of(mm(node_in, wn[...]))).astype(BF)
    grad_in = mm_nt(grad_pre, wn[...])
    grad_agg = grad_in[:, width : width + width_m].astype(BF)
    grad_message = mm_tn(dst_t[...], grad_agg).astype(BF)
    grad_pre_edge = (mm_nt(grad_message, w2[...]) * slope[...]).astype(BF)
    put_edges(mm_nt(grad_pre_edge, w1[2 * width :]), grad_in[:rows, width + width_m :])
    from_src = mm(src_t[...], grad_pre_edge).astype(BF)
    from_dst = mm(dst_t[...], grad_pre_edge).astype(BF)
    to_src = mm_nt(from_src, w1[:width])
    to_dst = mm_nt(from_dst, w1[width : 2 * width])
    first = [
        mm_tn(stacked(sources, moment, width), from_src),
        mm_tn(state, from_dst),
        mm_tn(attr[moment], grad_pre_edge),
    ]
    second = mm_tn(sums[...], grad_agg)
    node_grad = mm_tn(node_in, grad_pre)
    state_own = grad_in[:rows, :width] + to_dst[:rows]
    return state_own, to_src, to_dst, first, second, node_grad


def split_refs(refs):
    n = WAYS
    return refs[:n], refs[n : 2 * n], refs[2 * n : 2 * n + 10], refs[2 * n + 10 :]


def backward_first_kernel(*refs):
    sources, targets, args, refs = split_refs(refs)
    state, forcing, edges, to_src, to_dst, first_out, second_out, node_out = refs

    def put_edges(edge_values, forcing_values):
        edges[...] = edge_values
        forcing[...] = forcing_values

    state[...], to_src[...], to_dst[...], first, second, node_grad = backward(0, put_edges, sources, targets, *args)
    width = first[0].shape[0]
    for i, value in enumerate(first):
        first_out[i * width : (i + 1) * width] = value
    second_out[...] = second
    node_out[...] = node_grad


def backward_last_kernel(*refs):
    n = WAYS
    sources, targets, args, refs = split_refs(refs)
    state_0, to_src_0, to_dst_0, first_0, second_0, node_0 = refs[:6]
    state_own, forcing, edges, first_held, second_held, node_grad_held, src_kept = refs[6:13]
    core_a, core_b, target_kept, target_sent = refs[13:]

    def put_edges(edge_values, forcing_values):
        edges[...] = edge_values
        forcing[...] = forcing_values

    state_1, to_src_1, to_dst_1, first, second, node_grad = backward(1, put_edges, sources, targets, *args)
    state_own[0], state_own[1] = state_0[...], state_1
    width = first[0].shape[0]
    for i, value in enumerate(first):
        first_held[i * width : (i + 1) * width] = first_0[i * width : (i + 1) * width] + value
    second_held[...] = second_0[...] + second
    node_grad_held[...] = node_0[...] + node_grad
    part, block = first_held.shape[0] // n, second_held.shape[0] // n
    size, wide = block // 2, second_held.shape[1]
    for i, k in enumerate((1, 3)):
        other = lax.axis_index("dst") ^ k
        core_a[i * part : (i + 1) * part] = first_held[pl.ds(pl.multiple_of(other * part, part), part)].astype(BF)
        start = i * (core_b.shape[0] // 2)
        for held in (second_held, node_grad_held):
            for j in range(2):
                spot = pl.ds(pl.multiple_of(other * block + j * size, size), size)
                core_b[start : start + size, j * wide : (j + 1) * wide] = held[spot].astype(BF)
            start += size
        put_nodes(core_b, start, k, (to_src_0[...], to_src_1))
    for i, k in enumerate((0, 2)):
        put_nodes(src_kept, i * target_kept.shape[0], k, (to_src_0[...], to_src_1))
    put_nodes(target_kept, 0, 2, (to_dst_0[...], to_dst_1))
    for i, k in enumerate((1, 3)):
        put_nodes(target_sent, i * target_kept.shape[0], k, (to_dst_0[...], to_dst_1))


def out_kernel(forcing_0, edges_0, forcing_1, edges_1, forcing, edges, token, sems):
    pairs = [(edges_0, edges.at[0]), (edges_1, edges.at[1]), (forcing_0, forcing.at[0]), (forcing_1, forcing.at[1])]
    copies = [pltpu.make_async_copy(*ends, sems.at[i]) for i, ends in enumerate(pairs)]
    for copy in copies:
        copy.start()
    token[...] = jnp.zeros_like(token)
    for copy in copies:
        copy.wait()


def put_nodes(into, start, k, values):
    width = values[0].shape[1]
    rows = values[0].shape[0] // WAYS
    half = rows // 2
    for moment, value in enumerate(values):
        for j in range(2):
            lanes = slice((moment * 2 + j) * width, (moment * 2 + j + 1) * width)
            spot = slice(k * rows + j * half, k * rows + (j + 1) * half)
            into[start : start + half, lanes] = value[spot].astype(into.dtype)


def add_nodes(state, base, value):
    width, half = state.shape[2], value.shape[0]
    for moment in range(T_STEPS):
        for j in range(2):
            lanes = slice((moment * 2 + j) * width, (moment * 2 + j + 1) * width)
            spot = slice(j * half, (j + 1) * half)
            state[moment, spot] = base[moment, spot] + value[:, lanes]


def first_near_kernel(whole, arrived, own, across):
    part = own.shape[0]
    for i, (k, into) in enumerate(((0, own), (2, across))):
        spot = pl.ds(pl.multiple_of((lax.axis_index("dst") ^ k) * part, part), part)
        into[...] = (whole[spot] + arrived[i * part : (i + 1) * part].astype(F32)).astype(into.dtype)


def second_near_kernel(second, node_grad, src_kept, arrived, _, own, across):
    wide = second.shape[1]
    block = second.shape[0] // WAYS
    size, half = block // 2, src_kept.shape[0] // 2
    for i, (k, into) in enumerate(((0, own), (2, across))):
        other = lax.axis_index("dst") ^ k
        start = 0
        for whole in (second, node_grad):
            for j in range(2):
                lanes = slice(j * wide, (j + 1) * wide)
                spot = pl.ds(pl.multiple_of(other * block + j * size, size), size)
                value = arrived[i * into.shape[0] + start : i * into.shape[0] + start + size, lanes]
                into[start : start + size, lanes] = (whole[spot] + value.astype(F32)).astype(into.dtype)
            start += size
        value = arrived[i * into.shape[0] + start : (i + 1) * into.shape[0]]
        into[start:] = (src_kept[i * half : (i + 1) * half] + value.astype(F32)).astype(into.dtype)


def add_kernel(mine, arrived, own, sent):
    total = mine[...] + arrived[...].astype(F32)
    own[...] = total
    sent[...] = total.astype(BF)


def second_middle_kernel(mine, arrived, target_sent, own, sent, node_share, nodes):
    total = mine[...] + arrived[...].astype(F32)
    size = own.shape[0]
    own[...] = total[:size]
    sent[:size] = total[:size].astype(BF)
    sent[size:] = target_sent[...]
    node_share[...] = total[size : 2 * size].astype(BF)
    nodes[...] = total[2 * size :]


def second_sum_over_src_kernel(mine, arrived, target_kept, own, sent):
    size, half = own.shape[0], target_kept.shape[0]
    total = mine[...] + arrived[:size].astype(F32)
    own[...] = total
    sent[:size] = total.astype(BF)
    sent[size:] = (target_kept[...] + arrived[size + half :].astype(F32)).astype(BF)


def first_gather_kernel(mine, arrived, share):
    share[...] = (mine[...] + arrived[...].astype(F32)).astype(BF)


def second_gather_kernel(mine, arrived, node_across, share, node_sent):
    share[...] = (mine[...] + arrived[: mine.shape[0]].astype(F32)).astype(BF)
    node_sent[...] = node_across[...]


def put_shares(places, shares, outs, scratch):
    *held, sems = scratch
    copies = []

    def put(source, target):
        copies.append(pltpu.make_async_copy(source, target, sems.at[len(copies)]))
        copies[-1].start()

    for i, k in enumerate(places):
        other = lax.axis_index("dst") ^ k
        for out, into, share in zip(outs, held, shares[i], strict=True):
            rows, wide = into.shape[1:]
            size = share.shape[0]
            for h in range(rows // size):
                into[i, h * size : (h + 1) * size] = share[:, h * wide : (h + 1) * wide].astype(F32)
            put(into.at[i], out.at[pl.ds(pl.multiple_of(other * rows, rows), rows)])
    return copies


def first_shares_kernel(*refs):
    copies = put_shares((0, 1, 2), (refs[:3], refs[3:6], refs[6:9]), refs[9:12], refs[12:])
    for copy in copies:
        copy.wait()


def last_shares_kernel(state_own, nodes, arrived_1, arrived_2, *refs):
    shares, outs, scratch = refs[:3], refs[6:10], refs[10:]
    *held, state_held, state_sem = scratch
    copies = put_shares((3,), (shares,), outs[1:], held)
    half = nodes.shape[0]
    part = arrived_2.shape[0] - half
    add_nodes(
        state_held,
        state_own,
        nodes[...] + arrived_1[part : part + half].astype(F32) + arrived_2[part:].astype(F32),
    )
    copies.append(pltpu.make_async_copy(state_held, outs[0], state_sem))
    copies[-1].start()
    for copy in copies:
        copy.wait()


def call(kernel, outs, scratch, args, spaces=None, out_spaces=None, aliases=None):
    return pl.pallas_call(
        kernel,
        out_shape=[jax.ShapeDtypeStruct(shape, dtype) for shape, dtype in outs],
        in_specs=[pl.BlockSpec(memory_space=space) for space in spaces or [pltpu.VMEM] * len(args)],
        out_specs=[pl.BlockSpec(memory_space=space) for space in out_spaces or [pltpu.VMEM] * len(outs)],
        scratch_shapes=[
            pltpu.VMEM(*entry) if isinstance(entry, tuple) else entry for entry in scratch
        ],
        input_output_aliases=aliases or {},
        compiler_params=pltpu.CompilerParams(vmem_limit_bytes=32 << 20),
    )(*args)


def in_hbm(value):
    return pltpu.with_memory_space_constraint(value, pltpu.HBM)


def swap(value, axis, k):
    return lax.ppermute(value, axis, [(i, i ^ k) for i in range(WAYS)])


def local(
    node_state,
    forcing,
    edge_attr,
    src_index,
    dst_index,
    edge_count,
    cotangent,
    edge_w1,
    edge_w2,
    node_w1,
):
    rows, width = node_state.shape[1:]
    hid, width_m = edge_w2.shape
    width_out = node_w1.shape[1]
    slots = edge_attr.shape[3]
    nodes = rows * WAYS
    steps = T_STEPS
    attr = edge_attr[:, 0, 0]
    joined = call(
        join_kernel,
        [((steps, rows, 2 * width + width_out), BF)],
        [pltpu.SemaphoreType.DMA((3,))],
        [in_hbm(value) for value in (node_state, forcing, cotangent)],
        [pltpu.HBM] * 3,
    )[0]
    targets = {k: swap(joined, "src", k) for k in ORDER}
    targets = [joined] + [targets[k] for k in range(1, WAYS)]
    sources = [joined] + [swap(node_state, "dst", k) for k in range(1, WAYS)]
    given = (src_index[0], dst_index[0], attr, edge_w1, edge_w2, node_w1)
    attr, w1, w2, wn, src_t, dst_t, base = call(
        stage_kernel,
        [(value.shape, value.dtype) for value in given[2:]]
        + [((nodes, slots), BF), ((nodes, slots), BF), ((steps, slots, hid), F32)],
        [((1, slots), jnp.int32), ((1, slots), jnp.int32), pltpu.SemaphoreType.DMA((len(given),))],
        [edge_count, *(in_hbm(value) for value in given)],
        [pltpu.SMEM] + [pltpu.HBM] * len(given),
    )
    forward, sums = [], []
    for moment in range(steps):
        forward.append(
            call(
                functools.partial(forward_kernel, moment),
                [((nodes, width_m), BF), ((nodes, width_m), F32), ((slots, hid), F32), ((nodes, hid), BF)],
                [],
                [*sources, *targets, base, src_t, dst_t, w1, w2],
            )
        )
    for message, own, _, _ in forward:
        total, sent = call(
            first_sum_kernel,
            [((nodes, width_m), F32), ((nodes, width_m), BF)],
            [],
            [own, swap(message, "src", 1)],
        )
        sums.append([total, swap(sent, "src", 2)])
    args = [
        [*sources, *targets, *sums[moment], attr, src_t, dst_t, *forward[moment][2:], w1, w2, wn]
        for moment in range(steps)
    ]
    state_0, forcing_0, edges_0, *earlier = call(
        backward_first_kernel,
        [
            ((rows, width), F32),
            ((rows, width), F32),
            ((slots, width), F32),
            ((nodes, width), F32),
            ((nodes, width), F32),
            (edge_w1.shape, F32),
            (edge_w2.shape, F32),
            (node_w1.shape, F32),
        ],
        [],
        args[0],
    )
    part, block, half = edge_w1.shape[0] // WAYS, hid // WAYS, rows // 2
    size = block // 2
    wide = 2 * size + half
    state_own, forcing_1, edges_1, first, second, node_grad, src_kept, core_a, core_b, target_kept, target_sent = call(
        backward_last_kernel,
        [
            ((steps, rows, width), F32),
            ((rows, width), F32),
            ((slots, width), F32),
            (edge_w1.shape, F32),
            (edge_w2.shape, F32),
            (node_w1.shape, F32),
            ((2 * half, hid), F32),
            ((2 * part, hid), BF),
            ((2 * wide, hid), BF),
            ((half, hid), F32),
            ((2 * half, hid), BF),
        ],
        [],
        [*args[1], state_0, *earlier],
    )
    grad_forcing, edges, token = call(
        out_kernel,
        [((steps, rows, width), F32), ((steps, slots, width), F32), ((8, 128), F32)],
        [pltpu.SemaphoreType.DMA((4,))],
        [forcing_0, edges_0, forcing_1, edges_1],
        out_spaces=[pltpu.HBM] * 2 + [pltpu.VMEM],
    )

    def both(count, sent):
        return [((count, hid), F32), ((sent, hid), BF)]

    mine_a, across_a = call(first_near_kernel, both(part, part), [], [first, swap(core_a, "dst", 1)])
    mine_b, across_b = call(
        second_near_kernel, both(wide, wide), [], [second, node_grad, src_kept, swap(core_b, "dst", 1), token]
    )
    own_a, sent_a = call(add_kernel, both(part, part), [], [mine_a, swap(across_a, "dst", 2)])
    own_b, sent_b, node_share, nodes_sum = call(
        second_middle_kernel,
        both(size, size + 2 * half) + [((size, hid), BF), ((half, hid), F32)],
        [],
        [mine_b, swap(across_b, "dst", 2), target_sent],
    )
    node_across = swap(node_share, "dst", 2)
    own_a, sent_a = call(add_kernel, both(part, part), [], [own_a, swap(sent_a, "src", 1)])
    arrived_1 = swap(sent_b, "src", 1)
    own_b, sent_b = call(
        second_sum_over_src_kernel, both(size, size + half), [], [own_b, arrived_1, target_kept]
    )
    share_a = call(first_gather_kernel, [((part, hid), BF)], [], [own_a, swap(sent_a, "src", 2)])[0]
    arrived_2 = swap(sent_b, "src", 2)
    share_b, node_across = call(
        second_gather_kernel, [((size, hid), BF)] * 2, [], [own_b, arrived_2, node_across]
    )
    state = ((steps, rows, width), F32)
    own = [share_a, share_b, node_share]
    across = [swap(share_a, "dst", 2), swap(share_b, "dst", 2), node_across]
    outs = [(edge_w1.shape, F32), (edge_w2.shape, F32), (node_w1.shape, F32)]

    def held(count):
        shapes = [((count, value.shape[0] // WAYS, value.shape[1]), F32) for value in (edge_w1, edge_w2, node_w1)]
        return shapes + [pltpu.SemaphoreType.DMA((3 * count,))]

    grads = call(
        first_shares_kernel,
        outs,
        held(WAYS - 1),
        own + [swap(share, "dst", 1) for share in own] + across,
        out_spaces=[pltpu.HBM] * 3,
    )
    grad_state, grad_first, grad_second, grad_node = call(
        last_shares_kernel,
        [state] + outs,
        held(1) + [state, pltpu.SemaphoreType.DMA],
        [state_own, nodes_sum, arrived_1, arrived_2] + [swap(share, "dst", 1) for share in across] + list(grads),
        [pltpu.VMEM] * 7 + [pltpu.HBM] * 3,
        [pltpu.HBM] * 4,
        {7: 1, 8: 2, 9: 3},
    )
    return grad_state, grad_forcing, edges[:, None, None], grad_first, grad_second, grad_node


def silu_slope(value):
    sigma = jax.nn.sigmoid(value)
    return sigma * (1.0 + value * (1.0 - sigma))


def local_any(
    node_state,
    forcing,
    edge_attr,
    src_index,
    dst_index,
    edge_count,
    cotangent,
    edge_w1,
    edge_w2,
    node_w1,
):
    node_rows = node_state.shape[1]
    width_x = node_state.shape[2]
    width_m = edge_w2.shape[1]
    src_rows = node_rows * lax.axis_size("dst")
    dst_rows = node_rows * lax.axis_size("src")
    sources = lax.all_gather(node_state, "dst", axis=1, tiled=True)
    targets, forcing_block, cotangent_block = (
        lax.all_gather(node_state, "src", axis=1, tiled=True),
        lax.all_gather(forcing, "src", axis=1, tiled=True),
        lax.all_gather(cotangent, "src", axis=1, tiled=True),
    )
    src_local = src_index[0, 0]
    dst_local = dst_index[0, 0]
    alive = lax.iota(jnp.int32, src_local.shape[0]) < edge_count[0, 0]
    alive_float = alive.astype(jnp.float32)[:, None]
    alive_half = alive.astype(jnp.bfloat16)[:, None]
    own_start = lax.axis_index("src") * node_rows
    grad_first = jnp.zeros(edge_w1.shape, jnp.float32)
    grad_second = jnp.zeros(edge_w2.shape, jnp.float32)
    grad_node = jnp.zeros(node_w1.shape, jnp.float32)
    state_out, forcing_out, edge_out = ([], [], [])
    for moment in range(T_STEPS):
        edge_in = jnp.concatenate(
            [sources[moment][src_local], targets[moment][dst_local], edge_attr[moment, 0, 0]],
            axis=1,
        )
        pre_edge = jnp.dot(edge_in, edge_w1, preferred_element_type=jnp.float32)
        hidden = jax.nn.silu(pre_edge).astype(jnp.bfloat16)
        message = jnp.dot(hidden, edge_w2, preferred_element_type=jnp.float32) * alive_float
        partial_value = jax.ops.segment_sum(message, dst_local, num_segments=dst_rows)
        agg_block = lax.psum(partial_value, "src")
        node_in = jnp.concatenate(
            [targets[moment], agg_block.astype(jnp.bfloat16), forcing_block[moment]], axis=1
        )
        pre_node = jnp.dot(node_in, node_w1, preferred_element_type=jnp.float32)
        grad_pre_node = (cotangent_block[moment].astype(jnp.float32) * silu_slope(pre_node)).astype(
            jnp.bfloat16
        )
        grad_node_in = jnp.dot(grad_pre_node, node_w1.T, preferred_element_type=jnp.float32)
        own_in = lax.dynamic_slice_in_dim(node_in, own_start, node_rows, 0)
        own_pre = lax.dynamic_slice_in_dim(grad_pre_node, own_start, node_rows, 0)
        grad_node = grad_node + jnp.dot(own_in.T, own_pre, preferred_element_type=jnp.float32)
        own_grad = lax.dynamic_slice_in_dim(grad_node_in, own_start, node_rows, 0)
        grad_agg = grad_node_in[:, width_x : width_x + width_m].astype(jnp.bfloat16)
        grad_message = grad_agg[dst_local] * alive_half
        grad_second = grad_second + jnp.dot(
            hidden.T, grad_message, preferred_element_type=jnp.float32
        )
        grad_hidden = jnp.dot(grad_message, edge_w2.T, preferred_element_type=jnp.float32)
        grad_pre_edge = (grad_hidden * silu_slope(pre_edge)).astype(jnp.bfloat16)
        grad_first = grad_first + jnp.dot(
            edge_in.T, grad_pre_edge, preferred_element_type=jnp.float32
        )
        grad_edge_in = jnp.dot(grad_pre_edge, edge_w1.T, preferred_element_type=jnp.float32)
        source_part = jax.ops.segment_sum(
            grad_edge_in[:, :width_x], src_local, num_segments=src_rows
        )
        target_part = jax.ops.segment_sum(
            grad_edge_in[:, width_x : 2 * width_x], dst_local, num_segments=dst_rows
        )
        from_sources = lax.psum_scatter(source_part, "dst", scatter_dimension=0, tiled=True)
        from_targets = lax.psum_scatter(target_part, "src", scatter_dimension=0, tiled=True)
        state_out.append(own_grad[:, :width_x] + from_sources + from_targets)
        forcing_out.append(own_grad[:, width_x + width_m :])
        edge_out.append(grad_edge_in[:, 2 * width_x :])
    grad_first, grad_second, grad_node = lax.psum(
        (grad_first, grad_second, grad_node), ("src", "dst")
    )
    return (
        jnp.stack(state_out),
        jnp.stack(forcing_out),
        jnp.stack(edge_out)[:, None, None],
        grad_first,
        grad_second,
        grad_node,
    )


def solution(mesh):
    in_specs = (
        P(None, ("groups", "src", "dst"), None),
        P(None, ("groups", "src", "dst"), None),
        P(None, ("groups", "src"), "dst", None, None),
        P(("groups", "src"), "dst", None),
        P(("groups", "src"), "dst", None),
        P(("groups", "src"), "dst"),
        P(None, ("groups", "src", "dst"), None),
        P(),
        P(),
        P(),
    )
    out_specs = (
        P(None, ("groups", "src", "dst"), None),
        P(None, ("groups", "src", "dst"), None),
        P(None, ("groups", "src"), "dst", None, None),
        P("groups", None),
        P("groups", None),
        P("groups", None),
    )
    square = mesh.shape["src"] == WAYS and mesh.shape["dst"] == WAYS
    body = local if square else local_any
    return jax.shard_map(body, mesh=mesh, in_specs=in_specs, out_specs=out_specs, check_vma=False)
```

```python
import functools

import jax
import jax.numpy as jnp
from jax import lax
from jax.experimental import pallas as pl
from jax.experimental.pallas import tpu as pltpu
from jax.sharding import PartitionSpec as P

T_STEPS = 2
WAYS = 4
ORDER = (3, 1, 2)
BF = jnp.bfloat16
F32 = jnp.float32


def sigmoid(value):
    return 0.5 * jnp.tanh(0.5 * value) + 0.5


def slope_of(value):
    sigma = sigmoid(value)
    return sigma * (1.0 + value * (1.0 - sigma))


def mm(a, b):
    return jnp.dot(a, b, preferred_element_type=F32)


def mm_nt(a, b):
    return lax.dot_general(a, b, (((1,), (1,)), ((), ())), preferred_element_type=F32)


def mm_tn(a, b):
    return lax.dot_general(a, b, (((0,), (0,)), ((), ())), preferred_element_type=F32)


def one_hot_t(index, nodes, live=None):
    hit = lax.broadcasted_iota(jnp.int32, (nodes, index.shape[1]), 0) == index
    if live is not None:
        hit = jnp.logical_and(hit, live)
    return jnp.where(hit, 1.0, 0.0).astype(BF)


def stacked(refs, moment, width):
    return jnp.concatenate([ref[moment, :, :width] for ref in refs], axis=0)


def turned(value, k):
    rows = value.shape[0] // WAYS
    return jnp.concatenate([value[(j ^ k) * rows : ((j ^ k) + 1) * rows] for j in range(WAYS)], axis=0)


def join_kernel(state, forcing, cotangent, joined, sems):
    width = state.shape[2]
    copies = [
        pltpu.make_async_copy(state, joined.at[:, :, :width], sems.at[0]),
        pltpu.make_async_copy(forcing, joined.at[:, :, width : 2 * width], sems.at[1]),
        pltpu.make_async_copy(cotangent, joined.at[:, :, 2 * width :], sems.at[2]),
    ]
    for copy in copies:
        copy.start()
    for copy in copies:
        copy.wait()


def stage_kernel(count, src_hbm, dst_hbm, attr_hbm, w1_hbm, w2_hbm, wn_hbm, *refs):
    attr, w1, w2, wn, src_t, dst_t, base, src_held, dst_held, sems = refs
    width = attr.shape[2]
    nodes, slots = src_t.shape
    rows = nodes // WAYS
    copies = [
        pltpu.make_async_copy(source, target, sems.at[i])
        for i, (source, target) in enumerate(
            [
                (src_hbm, src_held),
                (dst_hbm, dst_held),
                (attr_hbm, attr),
                (w1_hbm, w1),
                (w2_hbm, w2),
                (wn_hbm, wn),
            ]
        )
    ]
    for copy in copies:
        copy.start()
    copies[0].wait()
    copies[1].wait()
    live = lax.broadcasted_iota(jnp.int32, (1, slots), 1) < count[0, 0]
    src_t[...] = one_hot_t(src_held[...] ^ (lax.axis_index("dst") * rows), nodes)
    dst_t[...] = one_hot_t(dst_held[...] ^ (lax.axis_index("src") * rows), nodes, live)
    copies[2].wait()
    copies[3].wait()
    for moment in range(T_STEPS):
        base[moment] = mm(attr[moment], w1[2 * width :])
    for copy in copies[4:]:
        copy.wait()


def forward_kernel(moment, *refs):
    n = WAYS
    sources, targets, refs = refs[:n], refs[n : 2 * n], refs[2 * n :]
    base, src_t, dst_t, w1, w2, message, own, slope, sums = refs
    width = sources[1].shape[2]
    ends = jnp.concatenate(
        [
            mm_tn(src_t[...], stacked(sources, moment, width)).astype(BF),
            mm_tn(dst_t[...], stacked(targets, moment, width)).astype(BF),
        ],
        axis=1,
    )
    pre = base[moment] + mm(ends, w1[: 2 * width])
    sigma = sigmoid(pre)
    hidden = (pre * sigma).astype(BF)
    slope[...] = sigma * (1.0 + pre * (1.0 - sigma))
    total = mm(dst_t[...], hidden)
    high = total.astype(BF)
    low = (total - high.astype(F32)).astype(BF)
    sums[...] = high
    product = mm(high, w2[...]) + mm(low, w2[...])
    own[...] = product
    message[...] = product.astype(BF)


def first_sum_kernel(own, arrived, total, sent):
    value = own[...] + turned(arrived[...].astype(F32), 1)
    total[...] = value
    sent[...] = value.astype(BF)


def backward(moment, put_edges, sources, targets, total, arrived, attr, src_t, dst_t, slope, sums, w1, w2, wn):
    rows, width = sources[1].shape[1:]
    width_m = w2.shape[1]
    joined = stacked(targets, moment, targets[0].shape[2])
    state, forcing, cotangent = joined[:, :width], joined[:, width : 2 * width], joined[:, 2 * width :]
    agg = total[...] + turned(arrived[...].astype(F32), 2)
    node_in = jnp.concatenate([state, agg.astype(BF), forcing], axis=1)
    grad_pre = (cotangent.astype(F32) * slope_of(mm(node_in, wn[...]))).astype(BF)
    grad_in = mm_nt(grad_pre, wn[...])
    grad_agg = grad_in[:, width : width + width_m].astype(BF)
    grad_message = mm_tn(dst_t[...], grad_agg).astype(BF)
    grad_pre_edge = (mm_nt(grad_message, w2[...]) * slope[...]).astype(BF)
    put_edges(mm_nt(grad_pre_edge, w1[2 * width :]), grad_in[:rows, width + width_m :])
    from_src = mm(src_t[...], grad_pre_edge).astype(BF)
    from_dst = mm(dst_t[...], grad_pre_edge).astype(BF)
    to_src = mm_nt(from_src, w1[:width])
    to_dst = mm_nt(from_dst, w1[width : 2 * width])
    attr_grad = mm_tn(attr[moment], grad_pre_edge)
    state_own = grad_in[:rows, :width] + to_dst[:rows]
    return state_own, to_src, to_dst, attr_grad, from_src, from_dst, grad_agg, node_in, grad_pre


def split_refs(refs):
    n = WAYS
    return refs[:n], refs[n : 2 * n], refs[2 * n : 2 * n + 10], refs[2 * n + 10 :]


def backward_first_kernel(*refs):
    sources, targets, args, refs = split_refs(refs)
    state, forcing, edges, *outs = refs

    def put_edges(edge_values, forcing_values):
        edges[...] = edge_values
        forcing[...] = forcing_values

    state[...], *values = backward(0, put_edges, sources, targets, *args)
    for ref, value in zip(outs, values, strict=True):
        ref[...] = value


def backward_last_kernel(*refs):
    n = WAYS
    sources, targets, args, refs = split_refs(refs)
    state_0, to_src_0, to_dst_0, attr_0, *earlier, sums_0 = refs[:10]
    state_own, forcing, edges, first_held, second_held, node_grad_held, src_kept = refs[10:17]
    core_a, core_b, target_kept, target_sent = refs[17:]

    def put_edges(edge_values, forcing_values):
        edges[...] = edge_values
        forcing[...] = forcing_values

    state_1, to_src_1, to_dst_1, attr_1, *later = backward(1, put_edges, sources, targets, *args)
    state_own[0], state_own[1] = state_0[...], state_1
    from_src, from_dst, grad_agg, node_in, grad_pre = (
        jnp.concatenate([ref[...], value], axis=0) for ref, value in zip(earlier, later, strict=True)
    )
    width = attr_1.shape[0]
    states = jnp.concatenate([stacked(sources, moment, width) for moment in range(T_STEPS)], axis=0)
    first_held[:width] = mm_tn(states, from_src)
    first_held[width : 2 * width] = mm_tn(node_in[:, :width], from_dst)
    first_held[2 * width :] = attr_0[...] + attr_1
    sums = args[6]
    second_held[...] = mm_tn(jnp.concatenate([sums_0[...], sums[...]], axis=0), grad_agg)
    node_grad_held[...] = mm_tn(node_in, grad_pre)
    part, block = first_held.shape[0] // n, second_held.shape[0] // n
    size, wide = block // 2, second_held.shape[1]
    for i, k in enumerate((1, 3)):
        other = lax.axis_index("dst") ^ k
        core_a[i * part : (i + 1) * part] = first_held[pl.ds(pl.multiple_of(other * part, part), part)].astype(BF)
        start = i * (core_b.shape[0] // 2)
        for held in (second_held, node_grad_held):
            for j in range(2):
                spot = pl.ds(pl.multiple_of(other * block + j * size, size), size)
                core_b[start : start + size, j * wide : (j + 1) * wide] = held[spot].astype(BF)
            start += size
        put_nodes(core_b, start, k, (to_src_0[...], to_src_1))
    for i, k in enumerate((0, 2)):
        put_nodes(src_kept, i * target_kept.shape[0], k, (to_src_0[...], to_src_1))
    put_nodes(target_kept, 0, 2, (to_dst_0[...], to_dst_1))
    for i, k in enumerate((1, 3)):
        put_nodes(target_sent, i * target_kept.shape[0], k, (to_dst_0[...], to_dst_1))


def out_kernel(forcing_0, edges_0, forcing_1, edges_1, forcing, edges, token, sems):
    pairs = [(edges_0, edges.at[0]), (edges_1, edges.at[1]), (forcing_0, forcing.at[0]), (forcing_1, forcing.at[1])]
    copies = [pltpu.make_async_copy(*ends, sems.at[i]) for i, ends in enumerate(pairs)]
    for copy in copies:
        copy.start()
    token[...] = jnp.zeros_like(token)
    for copy in copies:
        copy.wait()


def put_nodes(into, start, k, values):
    width = values[0].shape[1]
    rows = values[0].shape[0] // WAYS
    half = rows // 2
    for moment, value in enumerate(values):
        for j in range(2):
            lanes = slice((moment * 2 + j) * width, (moment * 2 + j + 1) * width)
            spot = slice(k * rows + j * half, k * rows + (j + 1) * half)
            into[start : start + half, lanes] = value[spot].astype(into.dtype)


def add_nodes(state, base, value):
    width, half = state.shape[2], value.shape[0]
    for moment in range(T_STEPS):
        for j in range(2):
            lanes = slice((moment * 2 + j) * width, (moment * 2 + j + 1) * width)
            spot = slice(j * half, (j + 1) * half)
            state[moment, spot] = base[moment, spot] + value[:, lanes]


def first_near_kernel(whole, arrived, own, across):
    part = own.shape[0]
    for i, (k, into) in enumerate(((0, own), (2, across))):
        spot = pl.ds(pl.multiple_of((lax.axis_index("dst") ^ k) * part, part), part)
        into[...] = (whole[spot] + arrived[i * part : (i + 1) * part].astype(F32)).astype(into.dtype)


def second_near_kernel(second, node_grad, src_kept, arrived, _, own, across):
    wide = second.shape[1]
    block = second.shape[0] // WAYS
    size, half = block // 2, src_kept.shape[0] // 2
    for i, (k, into) in enumerate(((0, own), (2, across))):
        other = lax.axis_index("dst") ^ k
        start = 0
        for whole in (second, node_grad):
            for j in range(2):
                lanes = slice(j * wide, (j + 1) * wide)
                spot = pl.ds(pl.multiple_of(other * block + j * size, size), size)
                value = arrived[i * into.shape[0] + start : i * into.shape[0] + start + size, lanes]
                into[start : start + size, lanes] = (whole[spot] + value.astype(F32)).astype(into.dtype)
            start += size
        value = arrived[i * into.shape[0] + start : (i + 1) * into.shape[0]]
        into[start:] = (src_kept[i * half : (i + 1) * half] + value.astype(F32)).astype(into.dtype)


def add_kernel(mine, arrived, own, sent):
    total = mine[...] + arrived[...].astype(F32)
    own[...] = total
    sent[...] = total.astype(BF)


def second_middle_kernel(mine, arrived, target_sent, own, sent, node_share, nodes):
    total = mine[...] + arrived[...].astype(F32)
    size = own.shape[0]
    own[...] = total[:size]
    sent[:size] = total[:size].astype(BF)
    sent[size:] = target_sent[...]
    node_share[...] = total[size : 2 * size].astype(BF)
    nodes[...] = total[2 * size :]


def second_sum_over_src_kernel(mine, arrived, target_kept, own, sent):
    size, half = own.shape[0], target_kept.shape[0]
    total = mine[...] + arrived[:size].astype(F32)
    own[...] = total
    sent[:size] = total.astype(BF)
    sent[size:] = (target_kept[...] + arrived[size + half :].astype(F32)).astype(BF)


def first_gather_kernel(mine, arrived, share):
    share[...] = (mine[...] + arrived[...].astype(F32)).astype(BF)


def second_gather_kernel(mine, arrived, node_across, share, node_sent):
    share[...] = (mine[...] + arrived[: mine.shape[0]].astype(F32)).astype(BF)
    node_sent[...] = node_across[...]


def put_shares(places, shares, outs, scratch):
    *held, sems = scratch
    copies = []

    def put(source, target):
        copies.append(pltpu.make_async_copy(source, target, sems.at[len(copies)]))
        copies[-1].start()

    for i, k in enumerate(places):
        other = lax.axis_index("dst") ^ k
        for out, into, share in zip(outs, held, shares[i], strict=True):
            rows, wide = into.shape[1:]
            size = share.shape[0]
            for h in range(rows // size):
                into[i, h * size : (h + 1) * size] = share[:, h * wide : (h + 1) * wide].astype(F32)
            put(into.at[i], out.at[pl.ds(pl.multiple_of(other * rows, rows), rows)])
    return copies


def first_shares_kernel(*refs):
    copies = put_shares((0, 1, 2), (refs[:3], refs[3:6], refs[6:9]), refs[9:12], refs[12:])
    for copy in copies:
        copy.wait()


def last_shares_kernel(state_own, nodes, arrived_1, arrived_2, *refs):
    shares, outs, scratch = refs[:3], refs[6:10], refs[10:]
    *held, state_held, state_sem = scratch
    copies = put_shares((3,), (shares,), outs[1:], held)
    half = nodes.shape[0]
    part = arrived_2.shape[0] - half
    add_nodes(
        state_held,
        state_own,
        nodes[...] + arrived_1[part : part + half].astype(F32) + arrived_2[part:].astype(F32),
    )
    copies.append(pltpu.make_async_copy(state_held, outs[0], state_sem))
    copies[-1].start()
    for copy in copies:
        copy.wait()


def call(kernel, outs, scratch, args, spaces=None, out_spaces=None, aliases=None):
    return pl.pallas_call(
        kernel,
        out_shape=[jax.ShapeDtypeStruct(shape, dtype) for shape, dtype in outs],
        in_specs=[pl.BlockSpec(memory_space=space) for space in spaces or [pltpu.VMEM] * len(args)],
        out_specs=[pl.BlockSpec(memory_space=space) for space in out_spaces or [pltpu.VMEM] * len(outs)],
        scratch_shapes=[
            pltpu.VMEM(*entry) if isinstance(entry, tuple) else entry for entry in scratch
        ],
        input_output_aliases=aliases or {},
        compiler_params=pltpu.CompilerParams(vmem_limit_bytes=32 << 20),
    )(*args)


def in_hbm(value):
    return pltpu.with_memory_space_constraint(value, pltpu.HBM)


def swap(value, axis, k):
    return lax.ppermute(value, axis, [(i, i ^ k) for i in range(WAYS)])


def local(
    node_state,
    forcing,
    edge_attr,
    src_index,
    dst_index,
    edge_count,
    cotangent,
    edge_w1,
    edge_w2,
    node_w1,
):
    rows, width = node_state.shape[1:]
    hid, width_m = edge_w2.shape
    width_out = node_w1.shape[1]
    slots = edge_attr.shape[3]
    nodes = rows * WAYS
    steps = T_STEPS
    attr = edge_attr[:, 0, 0]
    joined = call(
        join_kernel,
        [((steps, rows, 2 * width + width_out), BF)],
        [pltpu.SemaphoreType.DMA((3,))],
        [in_hbm(value) for value in (node_state, forcing, cotangent)],
        [pltpu.HBM] * 3,
    )[0]
    targets = {k: swap(joined, "src", k) for k in ORDER}
    targets = [joined] + [targets[k] for k in range(1, WAYS)]
    sources = [joined] + [swap(node_state, "dst", k) for k in range(1, WAYS)]
    given = (src_index[0], dst_index[0], attr, edge_w1, edge_w2, node_w1)
    attr, w1, w2, wn, src_t, dst_t, base = call(
        stage_kernel,
        [(value.shape, value.dtype) for value in given[2:]]
        + [((nodes, slots), BF), ((nodes, slots), BF), ((steps, slots, hid), F32)],
        [((1, slots), jnp.int32), ((1, slots), jnp.int32), pltpu.SemaphoreType.DMA((len(given),))],
        [edge_count, *(in_hbm(value) for value in given)],
        [pltpu.SMEM] + [pltpu.HBM] * len(given),
    )
    forward, sums = [], []
    for moment in range(steps):
        forward.append(
            call(
                functools.partial(forward_kernel, moment),
                [((nodes, width_m), BF), ((nodes, width_m), F32), ((slots, hid), F32), ((nodes, hid), BF)],
                [],
                [*sources, *targets, base, src_t, dst_t, w1, w2],
            )
        )
    for message, own, _, _ in forward:
        total, sent = call(
            first_sum_kernel,
            [((nodes, width_m), F32), ((nodes, width_m), BF)],
            [],
            [own, swap(message, "src", 1)],
        )
        sums.append([total, swap(sent, "src", 2)])
    args = [
        [*sources, *targets, *sums[moment], attr, src_t, dst_t, *forward[moment][2:], w1, w2, wn]
        for moment in range(steps)
    ]
    state_0, forcing_0, edges_0, *earlier = call(
        backward_first_kernel,
        [
            ((rows, width), F32),
            ((rows, width), F32),
            ((slots, width), F32),
            ((nodes, width), F32),
            ((nodes, width), F32),
            ((width, hid), F32),
            ((nodes, hid), BF),
            ((nodes, hid), BF),
            ((nodes, width_m), BF),
            ((nodes, node_w1.shape[0]), BF),
            ((nodes, width_out), BF),
        ],
        [],
        args[0],
    )
    part, block, half = edge_w1.shape[0] // WAYS, hid // WAYS, rows // 2
    size = block // 2
    wide = 2 * size + half
    state_own, forcing_1, edges_1, first, second, node_grad, src_kept, core_a, core_b, target_kept, target_sent = call(
        backward_last_kernel,
        [
            ((steps, rows, width), F32),
            ((rows, width), F32),
            ((slots, width), F32),
            (edge_w1.shape, F32),
            (edge_w2.shape, F32),
            (node_w1.shape, F32),
            ((2 * half, hid), F32),
            ((2 * part, hid), BF),
            ((2 * wide, hid), BF),
            ((half, hid), F32),
            ((2 * half, hid), BF),
        ],
        [],
        [*args[1], state_0, *earlier, forward[0][3]],
    )
    grad_forcing, edges, token = call(
        out_kernel,
        [((steps, rows, width), F32), ((steps, slots, width), F32), ((8, 128), F32)],
        [pltpu.SemaphoreType.DMA((4,))],
        [forcing_0, edges_0, forcing_1, edges_1],
        out_spaces=[pltpu.HBM] * 2 + [pltpu.VMEM],
    )

    def both(count, sent):
        return [((count, hid), F32), ((sent, hid), BF)]

    mine_a, across_a = call(first_near_kernel, both(part, part), [], [first, swap(core_a, "dst", 1)])
    mine_b, across_b = call(
        second_near_kernel, both(wide, wide), [], [second, node_grad, src_kept, swap(core_b, "dst", 1), token]
    )
    own_a, sent_a = call(add_kernel, both(part, part), [], [mine_a, swap(across_a, "dst", 2)])
    own_b, sent_b, node_share, nodes_sum = call(
        second_middle_kernel,
        both(size, size + 2 * half) + [((size, hid), BF), ((half, hid), F32)],
        [],
        [mine_b, swap(across_b, "dst", 2), target_sent],
    )
    node_across = swap(node_share, "dst", 2)
    own_a, sent_a = call(add_kernel, both(part, part), [], [own_a, swap(sent_a, "src", 1)])
    arrived_1 = swap(sent_b, "src", 1)
    own_b, sent_b = call(
        second_sum_over_src_kernel, both(size, size + half), [], [own_b, arrived_1, target_kept]
    )
    share_a = call(first_gather_kernel, [((part, hid), BF)], [], [own_a, swap(sent_a, "src", 2)])[0]
    arrived_2 = swap(sent_b, "src", 2)
    share_b, node_across = call(
        second_gather_kernel, [((size, hid), BF)] * 2, [], [own_b, arrived_2, node_across]
    )
    state = ((steps, rows, width), F32)
    own = [share_a, share_b, node_share]
    across = [swap(share_a, "dst", 2), swap(share_b, "dst", 2), node_across]
    outs = [(edge_w1.shape, F32), (edge_w2.shape, F32), (node_w1.shape, F32)]

    def held(count):
        shapes = [((count, value.shape[0] // WAYS, value.shape[1]), F32) for value in (edge_w1, edge_w2, node_w1)]
        return shapes + [pltpu.SemaphoreType.DMA((3 * count,))]

    grads = call(
        first_shares_kernel,
        outs,
        held(WAYS - 1),
        own + [swap(share, "dst", 1) for share in own] + across,
        out_spaces=[pltpu.HBM] * 3,
    )
    grad_state, grad_first, grad_second, grad_node = call(
        last_shares_kernel,
        [state] + outs,
        held(1) + [state, pltpu.SemaphoreType.DMA],
        [state_own, nodes_sum, arrived_1, arrived_2] + [swap(share, "dst", 1) for share in across] + list(grads),
        [pltpu.VMEM] * 7 + [pltpu.HBM] * 3,
        [pltpu.HBM] * 4,
        {7: 1, 8: 2, 9: 3},
    )
    return grad_state, grad_forcing, edges[:, None, None], grad_first, grad_second, grad_node


def silu_slope(value):
    sigma = jax.nn.sigmoid(value)
    return sigma * (1.0 + value * (1.0 - sigma))


def local_any(
    node_state,
    forcing,
    edge_attr,
    src_index,
    dst_index,
    edge_count,
    cotangent,
    edge_w1,
    edge_w2,
    node_w1,
):
    node_rows = node_state.shape[1]
    width_x = node_state.shape[2]
    width_m = edge_w2.shape[1]
    src_rows = node_rows * lax.axis_size("dst")
    dst_rows = node_rows * lax.axis_size("src")
    sources = lax.all_gather(node_state, "dst", axis=1, tiled=True)
    targets, forcing_block, cotangent_block = (
        lax.all_gather(node_state, "src", axis=1, tiled=True),
        lax.all_gather(forcing, "src", axis=1, tiled=True),
        lax.all_gather(cotangent, "src", axis=1, tiled=True),
    )
    src_local = src_index[0, 0]
    dst_local = dst_index[0, 0]
    alive = lax.iota(jnp.int32, src_local.shape[0]) < edge_count[0, 0]
    alive_float = alive.astype(jnp.float32)[:, None]
    alive_half = alive.astype(jnp.bfloat16)[:, None]
    own_start = lax.axis_index("src") * node_rows
    grad_first = jnp.zeros(edge_w1.shape, jnp.float32)
    grad_second = jnp.zeros(edge_w2.shape, jnp.float32)
    grad_node = jnp.zeros(node_w1.shape, jnp.float32)
    state_out, forcing_out, edge_out = ([], [], [])
    for moment in range(T_STEPS):
        edge_in = jnp.concatenate(
            [sources[moment][src_local], targets[moment][dst_local], edge_attr[moment, 0, 0]],
            axis=1,
        )
        pre_edge = jnp.dot(edge_in, edge_w1, preferred_element_type=jnp.float32)
        hidden = jax.nn.silu(pre_edge).astype(jnp.bfloat16)
        message = jnp.dot(hidden, edge_w2, preferred_element_type=jnp.float32) * alive_float
        partial_value = jax.ops.segment_sum(message, dst_local, num_segments=dst_rows)
        agg_block = lax.psum(partial_value, "src")
        node_in = jnp.concatenate(
            [targets[moment], agg_block.astype(jnp.bfloat16), forcing_block[moment]], axis=1
        )
        pre_node = jnp.dot(node_in, node_w1, preferred_element_type=jnp.float32)
        grad_pre_node = (cotangent_block[moment].astype(jnp.float32) * silu_slope(pre_node)).astype(
            jnp.bfloat16
        )
        grad_node_in = jnp.dot(grad_pre_node, node_w1.T, preferred_element_type=jnp.float32)
        own_in = lax.dynamic_slice_in_dim(node_in, own_start, node_rows, 0)
        own_pre = lax.dynamic_slice_in_dim(grad_pre_node, own_start, node_rows, 0)
        grad_node = grad_node + jnp.dot(own_in.T, own_pre, preferred_element_type=jnp.float32)
        own_grad = lax.dynamic_slice_in_dim(grad_node_in, own_start, node_rows, 0)
        grad_agg = grad_node_in[:, width_x : width_x + width_m].astype(jnp.bfloat16)
        grad_message = grad_agg[dst_local] * alive_half
        grad_second = grad_second + jnp.dot(
            hidden.T, grad_message, preferred_element_type=jnp.float32
        )
        grad_hidden = jnp.dot(grad_message, edge_w2.T, preferred_element_type=jnp.float32)
        grad_pre_edge = (grad_hidden * silu_slope(pre_edge)).astype(jnp.bfloat16)
        grad_first = grad_first + jnp.dot(
            edge_in.T, grad_pre_edge, preferred_element_type=jnp.float32
        )
        grad_edge_in = jnp.dot(grad_pre_edge, edge_w1.T, preferred_element_type=jnp.float32)
        source_part = jax.ops.segment_sum(
            grad_edge_in[:, :width_x], src_local, num_segments=src_rows
        )
        target_part = jax.ops.segment_sum(
            grad_edge_in[:, width_x : 2 * width_x], dst_local, num_segments=dst_rows
        )
        from_sources = lax.psum_scatter(source_part, "dst", scatter_dimension=0, tiled=True)
        from_targets = lax.psum_scatter(target_part, "src", scatter_dimension=0, tiled=True)
        state_out.append(own_grad[:, :width_x] + from_sources + from_targets)
        forcing_out.append(own_grad[:, width_x + width_m :])
        edge_out.append(grad_edge_in[:, 2 * width_x :])
    grad_first, grad_second, grad_node = lax.psum(
        (grad_first, grad_second, grad_node), ("src", "dst")
    )
    return (
        jnp.stack(state_out),
        jnp.stack(forcing_out),
        jnp.stack(edge_out)[:, None, None],
        grad_first,
        grad_second,
        grad_node,
    )


def solution(mesh):
    in_specs = (
        P(None, ("groups", "src", "dst"), None),
        P(None, ("groups", "src", "dst"), None),
        P(None, ("groups", "src"), "dst", None, None),
        P(("groups", "src"), "dst", None),
        P(("groups", "src"), "dst", None),
        P(("groups", "src"), "dst"),
        P(None, ("groups", "src", "dst"), None),
        P(),
        P(),
        P(),
    )
    out_specs = (
        P(None, ("groups", "src", "dst"), None),
        P(None, ("groups", "src", "dst"), None),
        P(None, ("groups", "src"), "dst", None, None),
        P("groups", None),
        P("groups", None),
        P("groups", None),
    )
    square = mesh.shape["src"] == WAYS and mesh.shape["dst"] == WAYS
    body = local if square else local_any
    return jax.shard_map(body, mesh=mesh, in_specs=in_specs, out_specs=out_specs, check_vma=False)
```

```python
import functools

import jax
import jax.numpy as jnp
from jax import lax
from jax.experimental import pallas as pl
from jax.experimental.pallas import tpu as pltpu
from jax.sharding import PartitionSpec as P

T_STEPS = 2
WAYS = 4
ORDER = (3, 1, 2)
BF = jnp.bfloat16
F32 = jnp.float32


def sigmoid(value):
    return 0.5 * jnp.tanh(0.5 * value) + 0.5


def slope_of(value):
    sigma = sigmoid(value)
    return sigma * (1.0 + value * (1.0 - sigma))


def mm(a, b):
    return jnp.dot(a, b, preferred_element_type=F32)


def mm_nt(a, b):
    return lax.dot_general(a, b, (((1,), (1,)), ((), ())), preferred_element_type=F32)


def mm_tn(a, b):
    return lax.dot_general(a, b, (((0,), (0,)), ((), ())), preferred_element_type=F32)


def one_hot_t(index, nodes, live=None):
    hit = lax.broadcasted_iota(jnp.int32, (nodes, index.shape[1]), 0) == index
    if live is not None:
        hit = jnp.logical_and(hit, live)
    return jnp.where(hit, 1.0, 0.0).astype(BF)


def stacked(refs, moment, width):
    return jnp.concatenate([ref[moment, :, :width] for ref in refs], axis=0)


def turned(value, k):
    rows = value.shape[0] // WAYS
    return jnp.concatenate([value[(j ^ k) * rows : ((j ^ k) + 1) * rows] for j in range(WAYS)], axis=0)


def join_kernel(state, forcing, cotangent, joined, sems):
    width = state.shape[2]
    copies = [
        pltpu.make_async_copy(state, joined.at[:, :, :width], sems.at[0]),
        pltpu.make_async_copy(forcing, joined.at[:, :, width : 2 * width], sems.at[1]),
        pltpu.make_async_copy(cotangent, joined.at[:, :, 2 * width :], sems.at[2]),
    ]
    for copy in copies:
        copy.start()
    for copy in copies:
        copy.wait()


def stage_kernel(count, src_hbm, dst_hbm, attr_hbm, w1_hbm, w2_hbm, wn_hbm, *refs):
    attr, w1, w2, wn, src_t, dst_t, base, src_held, dst_held, sems = refs
    width = attr.shape[2]
    nodes, slots = src_t.shape
    rows = nodes // WAYS
    copies = [
        pltpu.make_async_copy(source, target, sems.at[i])
        for i, (source, target) in enumerate(
            [
                (src_hbm, src_held),
                (dst_hbm, dst_held),
                (attr_hbm, attr),
                (w1_hbm, w1),
                (w2_hbm, w2),
                (wn_hbm, wn),
            ]
        )
    ]
    for copy in copies:
        copy.start()
    copies[0].wait()
    copies[1].wait()
    live = lax.broadcasted_iota(jnp.int32, (1, slots), 1) < count[0, 0]
    src_t[...] = one_hot_t(src_held[...] ^ (lax.axis_index("dst") * rows), nodes)
    dst_t[...] = one_hot_t(dst_held[...] ^ (lax.axis_index("src") * rows), nodes, live)
    copies[2].wait()
    copies[3].wait()
    for moment in range(T_STEPS):
        base[moment] = mm(attr[moment], w1[2 * width :])
    for copy in copies[4:]:
        copy.wait()


def forward_kernel(moment, *refs):
    n = WAYS
    sources, targets, refs = refs[:n], refs[n : 2 * n], refs[2 * n :]
    base, src_t, dst_t, w1, w2, message, own, slope, sums = refs
    width = sources[1].shape[2]
    ends = jnp.concatenate(
        [
            mm_tn(src_t[...], stacked(sources, moment, width)).astype(BF),
            mm_tn(dst_t[...], stacked(targets, moment, width)).astype(BF),
        ],
        axis=1,
    )
    pre = base[moment] + mm(ends, w1[: 2 * width])
    sigma = sigmoid(pre)
    value = pre * sigma
    hidden = value.astype(BF)
    slope[...] = value + sigma * (1.0 - value)
    total = mm(dst_t[...], hidden)
    high = total.astype(BF)
    low = (total - high.astype(F32)).astype(BF)
    sums[...] = high
    product = mm(high, w2[...]) + mm(low, w2[...])
    own[...] = product
    message[...] = product.astype(BF)


def first_sum_kernel(own, arrived, total, sent):
    value = own[...] + turned(arrived[...].astype(F32), 1)
    total[...] = value
    sent[...] = value.astype(BF)


def backward(moment, put_edges, sources, targets, total, arrived, attr, src_t, dst_t, slope, sums, w1, w2, wn):
    rows, width = sources[1].shape[1:]
    width_m = w2.shape[1]
    joined = stacked(targets, moment, targets[0].shape[2])
    state, forcing, cotangent = joined[:, :width], joined[:, width : 2 * width], joined[:, 2 * width :]
    agg = total[...] + turned(arrived[...].astype(F32), 2)
    node_in = jnp.concatenate([state, agg.astype(BF), forcing], axis=1)
    grad_pre = (cotangent.astype(F32) * slope_of(mm(node_in, wn[...]))).astype(BF)
    grad_in = mm_nt(grad_pre, wn[...])
    grad_agg = grad_in[:, width : width + width_m].astype(BF)
    grad_message = mm_tn(dst_t[...], grad_agg).astype(BF)
    grad_pre_edge = (mm_nt(grad_message, w2[...]) * slope[...]).astype(BF)
    put_edges(mm_nt(grad_pre_edge, w1[2 * width :]), grad_in[:rows, width + width_m :])
    from_src = mm(src_t[...], grad_pre_edge).astype(BF)
    from_dst = mm(dst_t[...], grad_pre_edge).astype(BF)
    to_src = mm_nt(from_src, w1[:width])
    to_dst = mm_nt(from_dst, w1[width : 2 * width])
    attr_grad = mm_tn(attr[moment], grad_pre_edge)
    state_own = grad_in[:rows, :width] + to_dst[:rows]
    return state_own, to_src, to_dst, attr_grad, from_src, from_dst, grad_agg, node_in, grad_pre


def split_refs(refs):
    n = WAYS
    return refs[:n], refs[n : 2 * n], refs[2 * n : 2 * n + 10], refs[2 * n + 10 :]


def backward_first_kernel(*refs):
    sources, targets, args, refs = split_refs(refs)
    state, forcing, edges, *outs = refs

    def put_edges(edge_values, forcing_values):
        edges[...] = edge_values
        forcing[...] = forcing_values

    state[...], *values = backward(0, put_edges, sources, targets, *args)
    for ref, value in zip(outs, values, strict=True):
        ref[...] = value


def backward_last_kernel(*refs):
    n = WAYS
    sources, targets, args, refs = split_refs(refs)
    state_0, to_src_0, to_dst_0, attr_0, *earlier, sums_0 = refs[:10]
    state_own, forcing, edges, first_held, second_held, node_grad_held, src_kept = refs[10:17]
    core_a, core_b, target_kept, target_sent = refs[17:]

    def put_edges(edge_values, forcing_values):
        edges[...] = edge_values
        forcing[...] = forcing_values

    state_1, to_src_1, to_dst_1, attr_1, *later = backward(1, put_edges, sources, targets, *args)
    state_own[0], state_own[1] = state_0[...], state_1
    from_src, from_dst, grad_agg, node_in, grad_pre = (
        jnp.concatenate([ref[...], value], axis=0) for ref, value in zip(earlier, later, strict=True)
    )
    width = attr_1.shape[0]
    states = jnp.concatenate([stacked(sources, moment, width) for moment in range(T_STEPS)], axis=0)
    first_held[:width] = mm_tn(states, from_src)
    first_held[width : 2 * width] = mm_tn(node_in[:, :width], from_dst)
    first_held[2 * width :] = attr_0[...] + attr_1
    sums = args[6]
    second_held[...] = mm_tn(jnp.concatenate([sums_0[...], sums[...]], axis=0), grad_agg)
    node_grad_held[...] = mm_tn(node_in, grad_pre)
    part, block = first_held.shape[0] // n, second_held.shape[0] // n
    size, wide = block // 2, second_held.shape[1]
    for i, k in enumerate((1, 3)):
        other = lax.axis_index("dst") ^ k
        core_a[i * part : (i + 1) * part] = first_held[pl.ds(pl.multiple_of(other * part, part), part)].astype(BF)
        start = i * (core_b.shape[0] // 2)
        for held in (second_held, node_grad_held):
            for j in range(2):
                spot = pl.ds(pl.multiple_of(other * block + j * size, size), size)
                core_b[start : start + size, j * wide : (j + 1) * wide] = held[spot].astype(BF)
            start += size
        put_nodes(core_b, start, k, (to_src_0[...], to_src_1))
    for i, k in enumerate((0, 2)):
        put_nodes(src_kept, i * target_kept.shape[0], k, (to_src_0[...], to_src_1))
    put_nodes(target_kept, 0, 2, (to_dst_0[...], to_dst_1))
    for i, k in enumerate((1, 3)):
        put_nodes(target_sent, i * target_kept.shape[0], k, (to_dst_0[...], to_dst_1))


def out_kernel(forcing_0, edges_0, forcing_1, edges_1, forcing, edges, token, sems):
    pairs = [(edges_0, edges.at[0]), (edges_1, edges.at[1]), (forcing_0, forcing.at[0]), (forcing_1, forcing.at[1])]
    copies = [pltpu.make_async_copy(*ends, sems.at[i]) for i, ends in enumerate(pairs)]
    for copy in copies:
        copy.start()
    token[...] = jnp.zeros_like(token)
    for copy in copies:
        copy.wait()


def put_nodes(into, start, k, values):
    width = values[0].shape[1]
    rows = values[0].shape[0] // WAYS
    half = rows // 2
    for moment, value in enumerate(values):
        for j in range(2):
            lanes = slice((moment * 2 + j) * width, (moment * 2 + j + 1) * width)
            spot = slice(k * rows + j * half, k * rows + (j + 1) * half)
            into[start : start + half, lanes] = value[spot].astype(into.dtype)


def add_nodes(state, base, value):
    width, half = state.shape[2], value.shape[0]
    for moment in range(T_STEPS):
        for j in range(2):
            lanes = slice((moment * 2 + j) * width, (moment * 2 + j + 1) * width)
            spot = slice(j * half, (j + 1) * half)
            state[moment, spot] = base[moment, spot] + value[:, lanes]


def first_near_kernel(whole, arrived, own, across):
    part = own.shape[0]
    for i, (k, into) in enumerate(((0, own), (2, across))):
        spot = pl.ds(pl.multiple_of((lax.axis_index("dst") ^ k) * part, part), part)
        into[...] = (whole[spot] + arrived[i * part : (i + 1) * part].astype(F32)).astype(into.dtype)


def second_near_kernel(second, node_grad, src_kept, arrived, _, own, across):
    wide = second.shape[1]
    block = second.shape[0] // WAYS
    size, half = block // 2, src_kept.shape[0] // 2
    for i, (k, into) in enumerate(((0, own), (2, across))):
        other = lax.axis_index("dst") ^ k
        start = 0
        for whole in (second, node_grad):
            for j in range(2):
                lanes = slice(j * wide, (j + 1) * wide)
                spot = pl.ds(pl.multiple_of(other * block + j * size, size), size)
                value = arrived[i * into.shape[0] + start : i * into.shape[0] + start + size, lanes]
                into[start : start + size, lanes] = (whole[spot] + value.astype(F32)).astype(into.dtype)
            start += size
        value = arrived[i * into.shape[0] + start : (i + 1) * into.shape[0]]
        into[start:] = (src_kept[i * half : (i + 1) * half] + value.astype(F32)).astype(into.dtype)


def add_kernel(mine, arrived, own, sent):
    total = mine[...] + arrived[...].astype(F32)
    own[...] = total
    sent[...] = total.astype(BF)


def second_middle_kernel(mine, arrived, target_sent, own, sent, node_share, nodes):
    total = mine[...] + arrived[...].astype(F32)
    size = own.shape[0]
    own[...] = total[:size]
    sent[:size] = total[:size].astype(BF)
    sent[size:] = target_sent[...]
    node_share[...] = total[size : 2 * size].astype(BF)
    nodes[...] = total[2 * size :]


def second_sum_over_src_kernel(mine, arrived, target_kept, own, sent):
    size, half = own.shape[0], target_kept.shape[0]
    total = mine[...] + arrived[:size].astype(F32)
    own[...] = total
    sent[:size] = total.astype(BF)
    sent[size:] = (target_kept[...] + arrived[size + half :].astype(F32)).astype(BF)


def first_gather_kernel(mine, arrived, share):
    share[...] = (mine[...] + arrived[...].astype(F32)).astype(BF)


def second_gather_kernel(mine, arrived, node_across, share, node_sent):
    share[...] = (mine[...] + arrived[: mine.shape[0]].astype(F32)).astype(BF)
    node_sent[...] = node_across[...]


def put_shares(places, shares, outs, scratch):
    *held, sems = scratch
    copies = []

    def put(source, target):
        copies.append(pltpu.make_async_copy(source, target, sems.at[len(copies)]))
        copies[-1].start()

    for i, k in enumerate(places):
        other = lax.axis_index("dst") ^ k
        for out, into, share in zip(outs, held, shares[i], strict=True):
            rows, wide = into.shape[1:]
            size = share.shape[0]
            for h in range(rows // size):
                into[i, h * size : (h + 1) * size] = share[:, h * wide : (h + 1) * wide].astype(F32)
            put(into.at[i], out.at[pl.ds(pl.multiple_of(other * rows, rows), rows)])
    return copies


def first_shares_kernel(*refs):
    copies = put_shares((0, 1, 2), (refs[:3], refs[3:6], refs[6:9]), refs[9:12], refs[12:])
    for copy in copies:
        copy.wait()


def last_shares_kernel(state_own, nodes, arrived_1, arrived_2, *refs):
    shares, outs, scratch = refs[:3], refs[6:10], refs[10:]
    *held, state_held, state_sem = scratch
    copies = put_shares((3,), (shares,), outs[1:], held)
    half = nodes.shape[0]
    part = arrived_2.shape[0] - half
    add_nodes(
        state_held,
        state_own,
        nodes[...] + arrived_1[part : part + half].astype(F32) + arrived_2[part:].astype(F32),
    )
    copies.append(pltpu.make_async_copy(state_held, outs[0], state_sem))
    copies[-1].start()
    for copy in copies:
        copy.wait()


def call(kernel, outs, scratch, args, spaces=None, out_spaces=None, aliases=None):
    return pl.pallas_call(
        kernel,
        out_shape=[jax.ShapeDtypeStruct(shape, dtype) for shape, dtype in outs],
        in_specs=[pl.BlockSpec(memory_space=space) for space in spaces or [pltpu.VMEM] * len(args)],
        out_specs=[pl.BlockSpec(memory_space=space) for space in out_spaces or [pltpu.VMEM] * len(outs)],
        scratch_shapes=[
            pltpu.VMEM(*entry) if isinstance(entry, tuple) else entry for entry in scratch
        ],
        input_output_aliases=aliases or {},
        compiler_params=pltpu.CompilerParams(vmem_limit_bytes=32 << 20),
    )(*args)


def in_hbm(value):
    return pltpu.with_memory_space_constraint(value, pltpu.HBM)


def swap(value, axis, k):
    return lax.ppermute(value, axis, [(i, i ^ k) for i in range(WAYS)])


def local(
    node_state,
    forcing,
    edge_attr,
    src_index,
    dst_index,
    edge_count,
    cotangent,
    edge_w1,
    edge_w2,
    node_w1,
):
    rows, width = node_state.shape[1:]
    hid, width_m = edge_w2.shape
    width_out = node_w1.shape[1]
    slots = edge_attr.shape[3]
    nodes = rows * WAYS
    steps = T_STEPS
    attr = edge_attr[:, 0, 0]
    joined = call(
        join_kernel,
        [((steps, rows, 2 * width + width_out), BF)],
        [pltpu.SemaphoreType.DMA((3,))],
        [in_hbm(value) for value in (node_state, forcing, cotangent)],
        [pltpu.HBM] * 3,
    )[0]
    targets = {k: swap(joined, "src", k) for k in ORDER}
    targets = [joined] + [targets[k] for k in range(1, WAYS)]
    sources = [joined] + [swap(node_state, "dst", k) for k in range(1, WAYS)]
    given = (src_index[0], dst_index[0], attr, edge_w1, edge_w2, node_w1)
    attr, w1, w2, wn, src_t, dst_t, base = call(
        stage_kernel,
        [(value.shape, value.dtype) for value in given[2:]]
        + [((nodes, slots), BF), ((nodes, slots), BF), ((steps, slots, hid), F32)],
        [((1, slots), jnp.int32), ((1, slots), jnp.int32), pltpu.SemaphoreType.DMA((len(given),))],
        [edge_count, *(in_hbm(value) for value in given)],
        [pltpu.SMEM] + [pltpu.HBM] * len(given),
    )
    forward, sums = [], []
    for moment in range(steps):
        forward.append(
            call(
                functools.partial(forward_kernel, moment),
                [((nodes, width_m), BF), ((nodes, width_m), F32), ((slots, hid), F32), ((nodes, hid), BF)],
                [],
                [*sources, *targets, base, src_t, dst_t, w1, w2],
            )
        )
    for message, own, _, _ in forward:
        total, sent = call(
            first_sum_kernel,
            [((nodes, width_m), F32), ((nodes, width_m), BF)],
            [],
            [own, swap(message, "src", 1)],
        )
        sums.append([total, swap(sent, "src", 2)])
    args = [
        [*sources, *targets, *sums[moment], attr, src_t, dst_t, *forward[moment][2:], w1, w2, wn]
        for moment in range(steps)
    ]
    state_0, forcing_0, edges_0, *earlier = call(
        backward_first_kernel,
        [
            ((rows, width), F32),
            ((rows, width), F32),
            ((slots, width), F32),
            ((nodes, width), F32),
            ((nodes, width), F32),
            ((width, hid), F32),
            ((nodes, hid), BF),
            ((nodes, hid), BF),
            ((nodes, width_m), BF),
            ((nodes, node_w1.shape[0]), BF),
            ((nodes, width_out), BF),
        ],
        [],
        args[0],
    )
    part, block, half = edge_w1.shape[0] // WAYS, hid // WAYS, rows // 2
    size = block // 2
    wide = 2 * size + half
    state_own, forcing_1, edges_1, first, second, node_grad, src_kept, core_a, core_b, target_kept, target_sent = call(
        backward_last_kernel,
        [
            ((steps, rows, width), F32),
            ((rows, width), F32),
            ((slots, width), F32),
            (edge_w1.shape, F32),
            (edge_w2.shape, F32),
            (node_w1.shape, F32),
            ((2 * half, hid), F32),
            ((2 * part, hid), BF),
            ((2 * wide, hid), BF),
            ((half, hid), F32),
            ((2 * half, hid), BF),
        ],
        [],
        [*args[1], state_0, *earlier, forward[0][3]],
    )
    grad_forcing, edges, token = call(
        out_kernel,
        [((steps, rows, width), F32), ((steps, slots, width), F32), ((8, 128), F32)],
        [pltpu.SemaphoreType.DMA((4,))],
        [forcing_0, edges_0, forcing_1, edges_1],
        out_spaces=[pltpu.HBM] * 2 + [pltpu.VMEM],
    )

    def both(count, sent):
        return [((count, hid), F32), ((sent, hid), BF)]

    mine_a, across_a = call(first_near_kernel, both(part, part), [], [first, swap(core_a, "dst", 1)])
    mine_b, across_b = call(
        second_near_kernel, both(wide, wide), [], [second, node_grad, src_kept, swap(core_b, "dst", 1), token]
    )
    own_a, sent_a = call(add_kernel, both(part, part), [], [mine_a, swap(across_a, "dst", 2)])
    own_b, sent_b, node_share, nodes_sum = call(
        second_middle_kernel,
        both(size, size + 2 * half) + [((size, hid), BF), ((half, hid), F32)],
        [],
        [mine_b, swap(across_b, "dst", 2), target_sent],
    )
    node_across = swap(node_share, "dst", 2)
    own_a, sent_a = call(add_kernel, both(part, part), [], [own_a, swap(sent_a, "src", 1)])
    arrived_1 = swap(sent_b, "src", 1)
    own_b, sent_b = call(
        second_sum_over_src_kernel, both(size, size + half), [], [own_b, arrived_1, target_kept]
    )
    share_a = call(first_gather_kernel, [((part, hid), BF)], [], [own_a, swap(sent_a, "src", 2)])[0]
    arrived_2 = swap(sent_b, "src", 2)
    share_b, node_across = call(
        second_gather_kernel, [((size, hid), BF)] * 2, [], [own_b, arrived_2, node_across]
    )
    state = ((steps, rows, width), F32)
    own = [share_a, share_b, node_share]
    across = [swap(share_a, "dst", 2), swap(share_b, "dst", 2), node_across]
    outs = [(edge_w1.shape, F32), (edge_w2.shape, F32), (node_w1.shape, F32)]

    def held(count):
        shapes = [((count, value.shape[0] // WAYS, value.shape[1]), F32) for value in (edge_w1, edge_w2, node_w1)]
        return shapes + [pltpu.SemaphoreType.DMA((3 * count,))]

    grads = call(
        first_shares_kernel,
        outs,
        held(WAYS - 1),
        own + [swap(share, "dst", 1) for share in own] + across,
        out_spaces=[pltpu.HBM] * 3,
    )
    grad_state, grad_first, grad_second, grad_node = call(
        last_shares_kernel,
        [state] + outs,
        held(1) + [state, pltpu.SemaphoreType.DMA],
        [state_own, nodes_sum, arrived_1, arrived_2] + [swap(share, "dst", 1) for share in across] + list(grads),
        [pltpu.VMEM] * 7 + [pltpu.HBM] * 3,
        [pltpu.HBM] * 4,
        {7: 1, 8: 2, 9: 3},
    )
    return grad_state, grad_forcing, edges[:, None, None], grad_first, grad_second, grad_node


def silu_slope(value):
    sigma = jax.nn.sigmoid(value)
    return sigma * (1.0 + value * (1.0 - sigma))


def local_any(
    node_state,
    forcing,
    edge_attr,
    src_index,
    dst_index,
    edge_count,
    cotangent,
    edge_w1,
    edge_w2,
    node_w1,
):
    node_rows = node_state.shape[1]
    width_x = node_state.shape[2]
    width_m = edge_w2.shape[1]
    src_rows = node_rows * lax.axis_size("dst")
    dst_rows = node_rows * lax.axis_size("src")
    sources = lax.all_gather(node_state, "dst", axis=1, tiled=True)
    targets, forcing_block, cotangent_block = (
        lax.all_gather(node_state, "src", axis=1, tiled=True),
        lax.all_gather(forcing, "src", axis=1, tiled=True),
        lax.all_gather(cotangent, "src", axis=1, tiled=True),
    )
    src_local = src_index[0, 0]
    dst_local = dst_index[0, 0]
    alive = lax.iota(jnp.int32, src_local.shape[0]) < edge_count[0, 0]
    alive_float = alive.astype(jnp.float32)[:, None]
    alive_half = alive.astype(jnp.bfloat16)[:, None]
    own_start = lax.axis_index("src") * node_rows
    grad_first = jnp.zeros(edge_w1.shape, jnp.float32)
    grad_second = jnp.zeros(edge_w2.shape, jnp.float32)
    grad_node = jnp.zeros(node_w1.shape, jnp.float32)
    state_out, forcing_out, edge_out = ([], [], [])
    for moment in range(T_STEPS):
        edge_in = jnp.concatenate(
            [sources[moment][src_local], targets[moment][dst_local], edge_attr[moment, 0, 0]],
            axis=1,
        )
        pre_edge = jnp.dot(edge_in, edge_w1, preferred_element_type=jnp.float32)
        hidden = jax.nn.silu(pre_edge).astype(jnp.bfloat16)
        message = jnp.dot(hidden, edge_w2, preferred_element_type=jnp.float32) * alive_float
        partial_value = jax.ops.segment_sum(message, dst_local, num_segments=dst_rows)
        agg_block = lax.psum(partial_value, "src")
        node_in = jnp.concatenate(
            [targets[moment], agg_block.astype(jnp.bfloat16), forcing_block[moment]], axis=1
        )
        pre_node = jnp.dot(node_in, node_w1, preferred_element_type=jnp.float32)
        grad_pre_node = (cotangent_block[moment].astype(jnp.float32) * silu_slope(pre_node)).astype(
            jnp.bfloat16
        )
        grad_node_in = jnp.dot(grad_pre_node, node_w1.T, preferred_element_type=jnp.float32)
        own_in = lax.dynamic_slice_in_dim(node_in, own_start, node_rows, 0)
        own_pre = lax.dynamic_slice_in_dim(grad_pre_node, own_start, node_rows, 0)
        grad_node = grad_node + jnp.dot(own_in.T, own_pre, preferred_element_type=jnp.float32)
        own_grad = lax.dynamic_slice_in_dim(grad_node_in, own_start, node_rows, 0)
        grad_agg = grad_node_in[:, width_x : width_x + width_m].astype(jnp.bfloat16)
        grad_message = grad_agg[dst_local] * alive_half
        grad_second = grad_second + jnp.dot(
            hidden.T, grad_message, preferred_element_type=jnp.float32
        )
        grad_hidden = jnp.dot(grad_message, edge_w2.T, preferred_element_type=jnp.float32)
        grad_pre_edge = (grad_hidden * silu_slope(pre_edge)).astype(jnp.bfloat16)
        grad_first = grad_first + jnp.dot(
            edge_in.T, grad_pre_edge, preferred_element_type=jnp.float32
        )
        grad_edge_in = jnp.dot(grad_pre_edge, edge_w1.T, preferred_element_type=jnp.float32)
        source_part = jax.ops.segment_sum(
            grad_edge_in[:, :width_x], src_local, num_segments=src_rows
        )
        target_part = jax.ops.segment_sum(
            grad_edge_in[:, width_x : 2 * width_x], dst_local, num_segments=dst_rows
        )
        from_sources = lax.psum_scatter(source_part, "dst", scatter_dimension=0, tiled=True)
        from_targets = lax.psum_scatter(target_part, "src", scatter_dimension=0, tiled=True)
        state_out.append(own_grad[:, :width_x] + from_sources + from_targets)
        forcing_out.append(own_grad[:, width_x + width_m :])
        edge_out.append(grad_edge_in[:, 2 * width_x :])
    grad_first, grad_second, grad_node = lax.psum(
        (grad_first, grad_second, grad_node), ("src", "dst")
    )
    return (
        jnp.stack(state_out),
        jnp.stack(forcing_out),
        jnp.stack(edge_out)[:, None, None],
        grad_first,
        grad_second,
        grad_node,
    )


def solution(mesh):
    in_specs = (
        P(None, ("groups", "src", "dst"), None),
        P(None, ("groups", "src", "dst"), None),
        P(None, ("groups", "src"), "dst", None, None),
        P(("groups", "src"), "dst", None),
        P(("groups", "src"), "dst", None),
        P(("groups", "src"), "dst"),
        P(None, ("groups", "src", "dst"), None),
        P(),
        P(),
        P(),
    )
    out_specs = (
        P(None, ("groups", "src", "dst"), None),
        P(None, ("groups", "src", "dst"), None),
        P(None, ("groups", "src"), "dst", None, None),
        P("groups", None),
        P("groups", None),
        P("groups", None),
    )
    square = mesh.shape["src"] == WAYS and mesh.shape["dst"] == WAYS
    body = local if square else local_any
    return jax.shard_map(body, mesh=mesh, in_specs=in_specs, out_specs=out_specs, check_vma=False)
```
